256 devices in a mesh: dp: 8 (over x, core), seq: 32 (over y, z).
Axes of the slice: x: 4, y: 4, z: 8, core: 2. Of those that a mesh axis runs over, the one named last changes fastest.
Arguments:
- node_feats: bfloat16 [8, 8192, 1024], P('dp', 'seq'), may hold values from -11 to 11
- w_qkv: bfloat16 [1024, 3072], replicated, may hold values from -1 to 1
- w_out: bfloat16 [1024, 1024], replicated, may hold values from -6 to 6
- cotangent: bfloat16 [8, 8192, 1024], P('dp', 'seq'), may hold values from -0.1796875 to 0.1796875
- block_neighbors: int32 [8, 64, 8], P('dp'), may hold values from 0 to 63, as said below
- block_counts: int32 [8, 64], P('dp'), may hold values from 1 to 8, as said below
- global_blocks: int32 [8, 4], P('dp'), may hold values from 1 to 62, as said below
Outputs:
- attn_update: bfloat16 [8, 8192, 1024], P('dp', 'seq')
- grad_nodes: bfloat16 [8, 8192, 1024], P('dp', 'seq')
- grad_weights: float32 [1024, 3072], P(('dp', 'seq'))
The draws below stay inside these ranges and needn't reach their ends.
Inputs may be any that keep to these rules, and one draw needn't show every extreme that they name: `block_neighbors`: each row holds 8 distinct block ids, none of them one of the graph's global blocks; the first block_counts of them are the row's neighbour blocks and the rest are to be ignored. A block row that is not global lists itself among its neighbour blocks. `block_counts`: in every subgraph some block row has exactly 8. `global_blocks`: the 4 ids of a subgraph are distinct, and include blocks 1 and 62.
All inputs are finite; a program needn't handle non-finite values.
Results may differ from the reference program's by a relative error of at most 0.017.
The reference program's roundings to bfloat16 on the way count: a program that leaves them out, or rounds other values in their place, can miss the bound.
Values may be sent and summed in bfloat16 or wider, within the bound.
No kernel may reach another device: no remote copies, remote signals or barrier semaphores. Data moves between devices by JAX's collectives and lax.ppermute only.
A program may use at most 128 MiB of HBM per device.

```python
import math
from functools import partial
import jax
import jax.numpy as jnp
import numpy as np
from jax import lax

D = 1024
H = 16
HD = 64
BLOCK = 128
MAXNB = 8
NGLOB = 4
NODE_DEV = 256
GRAPHS = 8
NODES = 8192
NBLK = 64
N_SEQ = 32


def graph_tables(key):

    def one_graph_tables(graph_key):
        perm_key, count_key, full_key, score_key, far_key = jax.random.split(graph_key, 5)
        middle_ids = (jax.random.permutation(perm_key, NBLK - 4)[:NGLOB - 2] + 2).astype(jnp.int32)
        global_ids = jnp.concatenate([jnp.array([1, NBLK - 2], dtype=jnp.int32), middle_ids]).astype(jnp.int32)
        block_index = jnp.arange(NBLK, dtype=jnp.int32)
        counts = jax.random.randint(count_key, (NBLK,), 1, MAXNB + 1, dtype=jnp.int32)
        full_row = jax.random.randint(full_key, (), 0, NBLK, dtype=jnp.int32)
        counts = jnp.where(block_index == full_row, MAXNB, counts)
        far_rows = (jax.random.randint(far_key, (NBLK,), 0, 3, dtype=jnp.int32) == 0) | (block_index == full_row)
        distance = jnp.abs(block_index[:, None] - block_index[None, :])
        penalty = jnp.where(far_rows[:, None], 0, 8 * distance)
        scores = jax.random.randint(score_key, (NBLK, NBLK), 0, 4 * NBLK, dtype=jnp.int32) - penalty
        scores = jnp.where(distance == 0, 1 << 20, scores)
        is_global = jnp.any(block_index[:, None] == global_ids[None, :], axis=1)
        scores = jnp.where(is_global[None, :], -(1 << 20), scores)
        scores = scores * NBLK + block_index[None, :]
        neighbors = lax.top_k(scores, MAXNB)[1].astype(jnp.int32)
        return (neighbors, counts.astype(jnp.int32), global_ids)
    graph_keys = jax.random.split(jax.random.fold_in(key, 29), GRAPHS)
    return jax.vmap(one_graph_tables)(graph_keys)


def draw_block_neighbors(key, part):
    return graph_tables(key)[0]


def draw_block_counts(key, part):
    return graph_tables(key)[1]


def draw_global_blocks(key, part):
    return graph_tables(key)[2]


def draw_node_feats(key, part):
    base_key = jax.random.fold_in(key, 0)
    features = jnp.clip(jax.random.normal(base_key, (GRAPHS, NODES, D), jnp.float32), -6.0, 6.0)
    return features.astype(jnp.bfloat16)


def draw_w_qkv(key, part):
    query_key, key_key, value_key = jax.random.split(key, 3)
    shape = (D, D)
    factor = 1.0 / math.sqrt(D)
    w_query = jnp.clip(jax.random.normal(query_key, shape, jnp.float32), -6.0, 6.0) * factor
    w_key = jnp.clip(jax.random.normal(key_key, shape, jnp.float32), -6.0, 6.0) * factor
    w_value = jnp.clip(jax.random.normal(value_key, shape, jnp.float32), -6.0, 6.0) * factor
    return jnp.concatenate([w_query, w_key, w_value], axis=1).astype(jnp.bfloat16)


def shard_levels(stream_key, extent, shards, low, high):
    level = 1.0
    for position, blocks in shards:
        heights = jax.random.uniform(jax.random.fold_in(jax.random.fold_in(stream_key, 6), position), (blocks,), jnp.float32, low / len(shards), high / len(shards))
        level = level * jnp.repeat(jnp.exp(heights), extent[position] // blocks).reshape((-1,) + (1,) * (len(extent) - 1 - position))
    return level


def scatter_about(own_key, dims, spread, reach, cuts=(), held_as=jnp.bfloat16):
    values = jax.random.normal(own_key, dims, jnp.float32) * spread
    if len(cuts) > 0:
        values = shard_levels(own_key, dims, cuts, -0.22, 0.18) * values
    return jnp.clip(values, min=-reach, max=reach).astype(held_as)


def setup_inputs(seed: int = 0) -> dict:
    key_of = jax.random.split(jax.random.key(seed), 8)
    return {
        "node_feats": draw_node_feats(jax.random.fold_in(key_of[7], 71), 0),
        "w_qkv": draw_w_qkv(jax.random.fold_in(key_of[7], 71), 0),
        "w_out": scatter_about(key_of[2], (D, D), 1.0, 6.0),
        "cotangent": scatter_about(key_of[3], (GRAPHS, NODES, D), 0.03, 0.1796875, ((0, 8), (1, 32))),
        "block_neighbors": draw_block_neighbors(jax.random.fold_in(key_of[7], 71), 0),
        "block_counts": draw_block_counts(jax.random.fold_in(key_of[7], 71), 0),
        "global_blocks": draw_global_blocks(jax.random.fold_in(key_of[7], 71), 0),
    }


def block_probs(queries, key_vecs, key_valid):
    scores = jnp.einsum("qhd,khd->hqk", queries.astype(jnp.float32), key_vecs.astype(jnp.float32)) * (HD ** -0.5)
    scores = jnp.where(key_valid[None, None, :], scores, -jnp.inf)
    scores = scores - jnp.max(scores, axis=-1, keepdims=True)
    weights = jnp.exp(scores)
    return weights / jnp.sum(weights, axis=-1, keepdims=True)


def to_low(values):
    return lax.optimization_barrier(values.astype(jnp.bfloat16)).astype(jnp.float32)


def one_graph(inputs, w_qkv, w_out):
    features, cotangent, neighbors, counts, global_ids = inputs
    slot_count = MAXNB + NGLOB
    projected = jnp.dot(features, w_qkv, preferred_element_type=jnp.float32).astype(jnp.bfloat16)
    query_blocks = projected[:, :D].reshape(NBLK, BLOCK, H, HD)
    key_blocks = projected[:, D:2 * D].reshape(NBLK, BLOCK, H, HD)
    value_blocks = projected[:, 2 * D:].reshape(NBLK, BLOCK, H, HD)
    id_table = jnp.concatenate([neighbors, jnp.broadcast_to(global_ids[None, :], (NBLK, NGLOB))], axis=1)
    slot_index = jnp.arange(slot_count, dtype=jnp.int32)
    valid_table = (slot_index[None, :] < counts[:, None]) | (slot_index[None, :] >= MAXNB)
    valid_table = jnp.repeat(valid_table, BLOCK, axis=1)

    def fetch(block_row):
        key_rows = id_table[block_row]
        key_vecs = key_blocks[key_rows].reshape(slot_count * BLOCK, H, HD)
        value_vecs = value_blocks[key_rows].reshape(slot_count * BLOCK, H, HD)
        return key_vecs, value_vecs, key_rows

    def forward_block(block_row):
        key_vecs, value_vecs, key_rows = fetch(block_row)
        probs = block_probs(query_blocks[block_row], key_vecs, valid_table[block_row])
        result = jnp.einsum("hqk,khd->qhd", to_low(probs), value_vecs.astype(jnp.float32))
        return result.astype(jnp.bfloat16)

    attended = lax.map(forward_block, jnp.arange(NBLK, dtype=jnp.int32)).reshape(NODES, D)
    attn_update = jnp.dot(attended, w_out, preferred_element_type=jnp.float32).astype(jnp.bfloat16)
    grad_attended = jnp.dot(cotangent, w_out.T, preferred_element_type=jnp.float32).astype(jnp.bfloat16)
    grad_blocks = grad_attended.reshape(NBLK, BLOCK, H, HD)

    def backward_block(running, block_row):
        key_vecs, value_vecs, key_rows = fetch(block_row)
        queries = query_blocks[block_row].astype(jnp.float32)
        grad_rows = grad_blocks[block_row].astype(jnp.float32)
        probs = block_probs(query_blocks[block_row], key_vecs, valid_table[block_row])
        grad_probs = jnp.einsum("qhd,khd->hqk", grad_rows, value_vecs.astype(jnp.float32))
        row_delta = jnp.sum(probs * grad_probs, axis=-1, keepdims=True)
        dscore = to_low(probs * (grad_probs - row_delta) * (HD ** -0.5))
        grad_q = jnp.einsum("hqk,khd->qhd", dscore, key_vecs.astype(jnp.float32)).astype(jnp.bfloat16)
        grad_k = jnp.einsum("hqk,qhd->khd", dscore, queries)
        grad_v = jnp.einsum("hqk,qhd->khd", to_low(probs), grad_rows)
        grad_kv = jnp.stack([grad_k, grad_v], axis=1).reshape(slot_count, BLOCK, 2, H, HD)
        return running.at[key_rows].add(grad_kv), grad_q

    qsplit = max(1, N_SEQ // H)
    per_device = NODE_DEV // BLOCK
    per_group = per_device // qsplit
    block_index = np.arange(NBLK)
    grad_kv_sum = jnp.zeros((NBLK, BLOCK, 2, H, HD), jnp.float32)
    grad_q_all = jnp.zeros((NBLK, BLOCK, H, HD), jnp.bfloat16)
    for group_id in range(qsplit):
        group_rows = jnp.asarray(block_index[(block_index % per_device) // per_group == group_id], dtype=jnp.int32)
        running, grad_q = lax.scan(backward_block, jnp.zeros((NBLK, BLOCK, 2, H, HD), jnp.float32), group_rows)
        grad_kv_sum = grad_kv_sum + to_low(running)
        grad_q_all = grad_q_all.at[group_rows].set(grad_q)
    grad_kv = grad_kv_sum.astype(jnp.bfloat16).reshape(NODES, 2 * D)
    grad_qkv = jnp.concatenate([grad_q_all.reshape(NODES, D), grad_kv], axis=1)
    grad_nodes = jnp.dot(grad_qkv, w_qkv.T, preferred_element_type=jnp.float32).astype(jnp.bfloat16)
    grad_proj = jnp.dot(features.T, grad_qkv, preferred_element_type=jnp.float32)
    return attn_update, grad_nodes, grad_proj


def reference(node_feats, w_qkv, w_out, cotangent, block_neighbors, block_counts, global_blocks):
    outputs = lax.map(partial(one_graph, w_qkv=w_qkv, w_out=w_out), (node_feats, cotangent, block_neighbors, block_counts, global_blocks))
    return outputs[0], outputs[1], jnp.sum(outputs[2], axis=0)
```

```python
import functools
import math

import jax
import jax.numpy as jnp
import numpy as np
from jax import lax
from jax.experimental import pallas as pl
from jax.experimental.pallas import tpu as pltpu
from jax.sharding import Mesh
from jax.sharding import PartitionSpec as P

H = 16
HD = 64
BLOCK = 128
MAXNB = 8
NGLOB = 4
SLOTS = MAXNB + NGLOB
YS = 4
ZS = 8
NODE_DEV = 256
ROW = NODE_DEV * ZS
QBLK = ROW // BLOCK
NODES = ROW * YS
HALF = ROW // 2
SCALE = HD**-0.5
LOG2E = math.log2(math.e)
MASKED = -3.0e38
VMEM = pltpu.CompilerParams(vmem_limit_bytes=48 * 1024 * 1024)

bf16 = jnp.bfloat16
f32 = jnp.float32


def low_half(shape):
    return lax.broadcasted_iota(jnp.int32, shape, 1) < HD


def pair_up(first, second):
    low = low_half(first.shape)
    return (
        jnp.where(low, first, pltpu.roll(second, HD, 1)),
        jnp.where(low, pltpu.roll(first, HD, 1), second),
    )


def nt(a, b):
    return lax.dot_general(a, b, (((1,), (1,)), ((), ())), preferred_element_type=f32)


def nn(a, b):
    return lax.dot_general(a, b, (((1,), (0,)), ((), ())), preferred_element_type=f32)


def kv_kernel(f_ref, wk_ref, wv_ref, a_ref, b_ref):
    both = nn(f_ref[...], jnp.concatenate([wk_ref[...], wv_ref[...]], axis=1))
    a, b = pair_up(both[:, :128], both[:, 128:])
    a_ref[0] = a.astype(bf16)
    b_ref[0] = b.astype(bf16)


def qg_kernel(f_ref, c_ref, wq_ref, wo_ref, a_ref, b_ref):
    a, b = pair_up(nn(f_ref[...], wq_ref[...]), nt(c_ref[...], wo_ref[...]))
    a_ref[0] = a.astype(bf16)
    b_ref[0] = b.astype(bf16)


def whole(shape):
    return pl.BlockSpec(shape, lambda i: (0,) * len(shape))


def project_kv(feats, w_qkv):
    d = feats.shape[1]
    out = jax.ShapeDtypeStruct((ZS, NODE_DEV, 128), bf16)
    tile = pl.BlockSpec((1, NODE_DEV, 128), lambda i: (i, 0, 0))
    return pl.pallas_call(
        kv_kernel,
        grid=(ZS,),
        in_specs=[
            whole((NODE_DEV, d)),
            pl.BlockSpec((d, 128), lambda i: (0, ZS + i)),
            pl.BlockSpec((d, 128), lambda i: (0, 2 * ZS + i)),
        ],
        out_specs=[tile, tile],
        out_shape=[out, out],
        compiler_params=VMEM,
        name="project_kv",
    )(feats, w_qkv, w_qkv)


def project_qg(feats, cot, w_qkv, w_out):
    d = feats.shape[1]
    out = jax.ShapeDtypeStruct((ZS, NODE_DEV, 128), bf16)
    tile = pl.BlockSpec((1, NODE_DEV, 128), lambda i: (i, 0, 0))
    return pl.pallas_call(
        qg_kernel,
        grid=(ZS,),
        in_specs=[
            whole((NODE_DEV, d)),
            whole((NODE_DEV, d)),
            pl.BlockSpec((d, 128), lambda i: (0, i)),
            pl.BlockSpec((128, d), lambda i: (i, 0)),
        ],
        out_specs=[tile, tile],
        out_shape=[out, out],
        compiler_params=VMEM,
        name="project_qg",
    )(feats, cot, w_qkv, w_out)


def attend_kernel(
    tab_ref, cnt_ref, y_ref, own_ref, left_ref, right_ref, opp_lo_ref, opp_hi_ref, qg_ref,
    od_ref, sum_own_ref, sum_right_ref, sum_left_ref, sum_opp_ref,
    kv_s, acc, sc, xs,
):
    y = y_ref[0]
    at = lambda step: lax.rem(y + step, YS) * ROW

    kv_s[pl.ds(pl.multiple_of(at(0), ROW), ROW), :] = own_ref[...]
    kv_s[pl.ds(pl.multiple_of(at(YS - 1), ROW), ROW), :] = left_ref[...]
    kv_s[pl.ds(pl.multiple_of(at(1), ROW), ROW), :] = right_ref[...]
    kv_s[pl.ds(pl.multiple_of(at(2), ROW), HALF), :] = opp_lo_ref[...]
    kv_s[pl.ds(pl.multiple_of(at(2) + HALF, HALF), HALF), :] = opp_hi_ref[...]

    @pl.loop(0, NODES // 512)
    def _(t):
        acc[:, pl.ds(pl.multiple_of(t * 512, 512), 512)] = jnp.zeros((128, 512), f32)

    def keys(ids, t):
        rows = [kv_s[pl.ds(pl.multiple_of(ids[2 * t + u] * BLOCK, BLOCK), BLOCK), :] for u in (0, 1)]
        return jnp.concatenate(rows, axis=0)

    def row_block(i, pairs):
        width = pairs * 256
        ids = [tab_ref[i * SLOTS + t] for t in range(2 * pairs)]
        odd = lax.rem(cnt_ref[i], 2) == 1
        rows = pl.ds(pl.multiple_of(i * BLOCK, BLOCK), BLOCK)
        qg = qg_ref[rows, :].astype(f32)
        low = low_half(qg.shape)
        zero = jnp.zeros_like(qg)
        wide32 = jnp.concatenate([jnp.where(low, qg, zero), jnp.where(low, zero, qg)], axis=0)
        wide = wide32.astype(bf16)
        for t in range(pairs):
            sc[:, t * 256 : (t + 1) * 256] = nt(wide, keys(ids, t))
        step = 16
        for r in range(BLOCK // step):
            s = sc[r * step : (r + 1) * step, :width]
            dp = sc[BLOCK + r * step : BLOCK + (r + 1) * step, :width]
            last = jnp.where(odd, MASKED, s[:, width - BLOCK :])
            s = jnp.concatenate([s[:, : width - BLOCK], last], axis=1)
            e = jnp.exp2((s - jnp.max(s, axis=1, keepdims=True)) * (SCALE * LOG2E))
            p = e * (1.0 / jnp.sum(e, axis=1, keepdims=True))
            delta = jnp.sum(p * dp, axis=1, keepdims=True)
            ds = p * (dp - delta) * SCALE
            xs[r * step : (r + 1) * step, :width] = ds.astype(bf16)
            xs[BLOCK + r * step : BLOCK + (r + 1) * step, :width] = p.astype(bf16)
        every = jnp.concatenate([keys(ids, t) for t in range(pairs)], axis=0)
        mixed = nn(xs[:, :width], every)
        od_ref[rows, :] = jnp.where(low, mixed[:BLOCK], mixed[BLOCK:]).astype(bf16)
        wide_t = wide32.T.astype(bf16)
        for t in range(pairs):
            part = nn(wide_t, xs[:, t * 256 : (t + 1) * 256])
            for u in (0, 1):
                at_key = pl.ds(pl.multiple_of(ids[2 * t + u] * BLOCK, BLOCK), BLOCK)
                acc[:, at_key] += part[:, u * BLOCK : (u + 1) * BLOCK]

    @pl.loop(0, QBLK)
    def _(i):
        pairs = NGLOB // 2 + (cnt_ref[i] + 1) // 2
        for v in range(NGLOB // 2 + 1, SLOTS // 2 + 1):
            pl.when(pairs == v)(functools.partial(row_block, i, v))

    for step, out in ((0, sum_own_ref), (1, sum_right_ref), (YS - 1, sum_left_ref), (2, sum_opp_ref)):
        start = at(step)

        @pl.loop(0, ROW // 256)
        def _(t):
            cols = pl.ds(pl.multiple_of(start + t * 256, 256), 256)
            out[pl.ds(pl.multiple_of(t * 256, 256), 256), :] = acc[:, cols].T.astype(bf16)


def attend(table, counts, y, kv_parts, qg):
    vmem = pl.BlockSpec(memory_space=pltpu.VMEM)
    smem = pl.BlockSpec(memory_space=pltpu.SMEM)
    row = jax.ShapeDtypeStruct((ROW, 128), bf16)
    return pl.pallas_call(
        attend_kernel,
        in_specs=[smem] * 3 + [vmem] * 6,
        out_specs=[vmem] * 5,
        out_shape=[row] * 5,
        scratch_shapes=[
            pltpu.VMEM((NODES, 128), bf16),
            pltpu.VMEM((128, NODES), f32),
            pltpu.VMEM((256, SLOTS * BLOCK), f32),
            pltpu.VMEM((256, SLOTS * BLOCK), bf16),
        ],
        compiler_params=VMEM,
        cost_estimate=pl.CostEstimate(
            flops=6 * QBLK * BLOCK * 1152 * 128 * 2, bytes_accessed=6 << 20, transcendentals=0
        ),
        name="attend",
    )(table, counts, y, *kv_parts, qg)


def out_kernel(a_ref, b_ref, wo_ref, o_ref, total):
    step = pl.program_id(0)

    @pl.when(step == 0)
    def _():
        total[...] = jnp.zeros_like(total)

    cols = [pair_up(a_ref[u].astype(f32), b_ref[u].astype(f32))[1] for u in (0, 1)]
    total[...] += nn(jnp.concatenate(cols, axis=1).astype(bf16), wo_ref[...])

    @pl.when(step == pl.num_programs(0) - 1)
    def _():
        o_ref[...] = total[...].astype(bf16)


def project_out(od_a, od_b, w_out):
    d = w_out.shape[1]
    tile = pl.BlockSpec((2, NODE_DEV, 128), lambda i: (i, 0, 0))
    return pl.pallas_call(
        out_kernel,
        grid=(ZS // 2,),
        in_specs=[tile, tile, pl.BlockSpec((256, d), lambda i: (i, 0))],
        out_specs=whole((NODE_DEV, d)),
        out_shape=jax.ShapeDtypeStruct((NODE_DEV, d), bf16),
        scratch_shapes=[pltpu.VMEM((NODE_DEV, d), f32)],
        compiler_params=VMEM,
        name="project_out",
    )(od_a, od_b, w_out)


def nodes_kernel(oa_ref, ob_ref, ka_ref, kb_ref, wq_ref, wk_ref, wv_ref, o_ref, total):
    step = pl.program_id(0)

    @pl.when(step == 0)
    def _():
        total[...] = jnp.zeros_like(total)

    dq, dk, dv = [], [], []
    for u in (0, 1):
        dq.append(pair_up(oa_ref[u].astype(f32), ob_ref[u].astype(f32))[0])
        k, v = pair_up(ka_ref[u].astype(f32), kb_ref[u].astype(f32))
        dk.append(k)
        dv.append(v)
    add = nt(jnp.concatenate(dq, axis=1).astype(bf16), wq_ref[...])
    add += nt(jnp.concatenate(dk, axis=1).astype(bf16), wk_ref[...])
    add += nt(jnp.concatenate(dv, axis=1).astype(bf16), wv_ref[...])
    total[...] += add

    @pl.when(step == pl.num_programs(0) - 1)
    def _():
        o_ref[...] = total[...].astype(bf16)


def node_grads(od_a, od_b, kv_a, kv_b, w_qkv):
    d = w_qkv.shape[0]
    tile = pl.BlockSpec((2, NODE_DEV, 128), lambda i: (i, 0, 0))
    steps = ZS // 2
    return pl.pallas_call(
        nodes_kernel,
        grid=(steps,),
        in_specs=[tile] * 4
        + [pl.BlockSpec((d, 256), functools.partial(lambda i, third: (0, third * steps + i), third=k)) for k in range(3)],
        out_specs=whole((NODE_DEV, d)),
        out_shape=jax.ShapeDtypeStruct((NODE_DEV, d), bf16),
        scratch_shapes=[pltpu.VMEM((NODE_DEV, d), f32)],
        compiler_params=VMEM,
        name="node_grads",
    )(od_a, od_b, kv_a, kv_b, w_qkv, w_qkv, w_qkv)


def swap(values, axis):
    return lax.all_to_all(values, axis, split_axis=0, concat_axis=0, tiled=True)


RIGHT = [(i, (i + 1) % YS) for i in range(YS)]
LEFT = [(i, (i - 1) % YS) for i in range(YS)]


def gather_row(own):
    left = lax.ppermute(own, "y", RIGHT)
    right = lax.ppermute(own, "y", LEFT)
    opp_lo = lax.ppermute(left[:HALF], "y", RIGHT)
    opp_hi = lax.ppermute(right[HALF:], "y", LEFT)
    return own, left, right, opp_lo, opp_hi


def sum_row(own, to_right, to_left, opp):
    lo = lax.ppermute(opp[:HALF], "y", RIGHT)
    hi = lax.ppermute(opp[HALF:], "y", LEFT)
    add = lambda *v: sum(x.astype(f32) for x in v)
    to_right = jnp.concatenate([add(to_right[:HALF], lo).astype(bf16), to_right[HALF:]], axis=0)
    to_left = jnp.concatenate([to_left[:HALF], add(to_left[HALF:], hi).astype(bf16)], axis=0)
    return add(own, lax.ppermute(to_right, "y", RIGHT), lax.ppermute(to_left, "y", LEFT)).astype(bf16)


def on_device(node_feats, w_qkv, w_out, cotangent, block_neighbors, block_counts, global_blocks):
    feats = node_feats[0]
    cot = cotangent[0]
    y = lax.axis_index("y")
    neighbors = lax.dynamic_slice_in_dim(block_neighbors[0], y * QBLK, QBLK, 0)
    counts = lax.dynamic_slice_in_dim(block_counts[0], y * QBLK, QBLK, 0)
    table = jnp.concatenate([jnp.broadcast_to(global_blocks[0][None], (QBLK, NGLOB)), neighbors], axis=1).reshape(-1)
    y_arr = y.reshape(1).astype(jnp.int32)

    kv = project_kv(feats, w_qkv)
    qg = project_qg(feats, cot, w_qkv, w_out)
    feats_row = lax.all_gather(feats, "z", axis=0, tiled=True)
    od, kv_sum = [], []
    for p in (0, 1):
        kv_row = swap(kv[p], "z").reshape(ROW, 128)
        qg_row = swap(qg[p], "z").reshape(ROW, 128)
        outs = attend(table, counts, y_arr, gather_row(kv_row), qg_row)
        od.append(outs[0])
        kv_sum.append(sum_row(*outs[1:]))
    od_nodes = [swap(v.reshape(ZS, NODE_DEV, 128), "z") for v in od]
    kv_nodes = [swap(v.reshape(ZS, NODE_DEV, 128), "z") for v in kv_sum]
    attn_update = project_out(od_nodes[0], od_nodes[1], w_out)
    grad_nodes = node_grads(od_nodes[0], od_nodes[1], kv_nodes[0], kv_nodes[1], w_qkv)

    grads = jnp.concatenate([od[0][:, :HD], od[1][:, :HD], kv_sum[0], kv_sum[1]], axis=1)
    share = lax.dot_general(feats_row, grads, (((0,), (0,)), ((), ())), preferred_element_type=f32)
    rows = share.shape[0] // 32
    share = swap(share.astype(bf16).reshape(32, rows, 6 * HD), ("x", "c", "y"))
    share = jnp.sum(share.astype(f32), axis=0)
    share = swap(share.reshape(ZS, rows // ZS, 6, HD), "z")
    pick = lambda a, b: jnp.stack([share[:, :, a], share[:, :, b]], axis=2)
    grad_weights = jnp.stack([pick(0, 1), pick(2, 4), pick(3, 5)], axis=0)
    grad_weights = grad_weights.transpose(2, 0, 1, 3, 4).reshape(rows // ZS, 3 * H * HD)
    return attn_update[None], grad_nodes[None], grad_weights


def solution(mesh):
    fine = Mesh(np.asarray(mesh.devices).reshape(4, 2, YS, ZS), ("x", "c", "y", "z"))
    dp, seq = ("x", "c"), ("y", "z")
    in_specs = (P(dp, seq, None), P(), P(), P(dp, seq, None), P(dp, None, None), P(dp, None), P(dp, None))
    out_specs = (P(dp, seq, None), P(dp, seq, None), P(dp + seq, None))
    return jax.shard_map(on_device, mesh=fine, in_specs=in_specs, out_specs=out_specs, check_vma=False)
```

```python
import functools
import math

import jax
import jax.numpy as jnp
import numpy as np
from jax import lax
from jax.experimental import pallas as pl
from jax.experimental.pallas import tpu as pltpu
from jax.sharding import Mesh
from jax.sharding import PartitionSpec as P

H = 16
HD = 64
BLOCK = 128
MAXNB = 8
NGLOB = 4
SLOTS = MAXNB + NGLOB
YS = 4
ZS = 8
NODE_DEV = 256
ROW = NODE_DEV * ZS
QBLK = ROW // BLOCK
NODES = ROW * YS
HALF = ROW // 2
SCALE = HD**-0.5
LOG2E = math.log2(math.e)
MASKED = -3.0e38
VMEM = pltpu.CompilerParams(vmem_limit_bytes=60 * 1024 * 1024)

bf16 = jnp.bfloat16
f32 = jnp.float32


def low_half(shape):
    return lax.broadcasted_iota(jnp.int32, shape, 1) < HD


def pair_up(first, second):
    low = low_half(first.shape)
    return (
        jnp.where(low, first, pltpu.roll(second, HD, 1)),
        jnp.where(low, pltpu.roll(first, HD, 1), second),
    )


def nt(a, b):
    return lax.dot_general(a, b, (((1,), (1,)), ((), ())), preferred_element_type=f32)


def nn(a, b):
    return lax.dot_general(a, b, (((1,), (0,)), ((), ())), preferred_element_type=f32)


def put_pairs(first, second, a_ref, b_ref):
    for u in (0, 1):
        cols = slice(u * 128, (u + 1) * 128)
        a, b = pair_up(first[:, cols], second[:, cols])
        a_ref[u] = a.astype(bf16)
        b_ref[u] = b.astype(bf16)


def kv_kernel(f_ref, wk_ref, wv_ref, a_ref, b_ref):
    put_pairs(nn(f_ref[...], wk_ref[...]), nn(f_ref[...], wv_ref[...]), a_ref, b_ref)


def qg_kernel(f_ref, c_ref, wq_ref, wo_ref, a_ref, b_ref):
    put_pairs(nn(f_ref[...], wq_ref[...]), nt(c_ref[...], wo_ref[...]), a_ref, b_ref)


def whole(shape):
    return pl.BlockSpec(shape, lambda i: (0,) * len(shape))


def project_kv(feats, w_qkv):
    d = feats.shape[1]
    out = jax.ShapeDtypeStruct((ZS, NODE_DEV, 128), bf16)
    tile = pl.BlockSpec((2, NODE_DEV, 128), lambda i: (i, 0, 0))
    return pl.pallas_call(
        kv_kernel,
        grid=(ZS // 2,),
        in_specs=[
            whole((NODE_DEV, d)),
            pl.BlockSpec((d, 256), lambda i: (0, ZS // 2 + i)),
            pl.BlockSpec((d, 256), lambda i: (0, ZS + i)),
        ],
        out_specs=[tile, tile],
        out_shape=[out, out],
        compiler_params=VMEM,
        name="project_kv",
    )(feats, w_qkv, w_qkv)


def project_qg(feats, cot, w_qkv, w_out):
    d = feats.shape[1]
    out = jax.ShapeDtypeStruct((ZS, NODE_DEV, 128), bf16)
    tile = pl.BlockSpec((2, NODE_DEV, 128), lambda i: (i, 0, 0))
    return pl.pallas_call(
        qg_kernel,
        grid=(ZS // 2,),
        in_specs=[
            whole((NODE_DEV, d)),
            whole((NODE_DEV, d)),
            pl.BlockSpec((d, 256), lambda i: (0, i)),
            pl.BlockSpec((256, d), lambda i: (i, 0)),
        ],
        out_specs=[tile, tile],
        out_shape=[out, out],
        compiler_params=VMEM,
        name="project_qg",
    )(feats, cot, w_qkv, w_out)


def attend_kernel(
    tab_ref, cnt_ref, y_ref, own_ref, left_ref, right_ref, opp_lo_ref, opp_hi_ref, qg_ref, after_ref,
    od_ref, sum_own_ref, sum_right_ref, sum_left_ref, sum_opp_ref,
    kv_s, acc, sc, xs,
):
    y = y_ref[0]
    at = lambda step: lax.rem(y + step, YS) * ROW

    kv_s[pl.ds(pl.multiple_of(at(0), ROW), ROW), :] = own_ref[...]
    kv_s[pl.ds(pl.multiple_of(at(YS - 1), ROW), ROW), :] = left_ref[...]
    kv_s[pl.ds(pl.multiple_of(at(1), ROW), ROW), :] = right_ref[...]
    kv_s[pl.ds(pl.multiple_of(at(2), ROW), HALF), :] = opp_lo_ref[...]
    kv_s[pl.ds(pl.multiple_of(at(2) + HALF, HALF), HALF), :] = opp_hi_ref[...]

    @pl.loop(0, NODES // 512)
    def _(t):
        acc[:, pl.ds(pl.multiple_of(t * 512, 512), 512)] = jnp.zeros((128, 512), f32)

    def keys(ids, t):
        rows = [kv_s[pl.ds(pl.multiple_of(ids[2 * t + u] * BLOCK, BLOCK), BLOCK), :] for u in (0, 1)]
        return jnp.concatenate(rows, axis=0)

    def row_block(i, pairs):
        width = pairs * 256
        ids = [tab_ref[i * SLOTS + t] for t in range(2 * pairs)]
        odd = lax.rem(cnt_ref[i], 2) == 1
        rows = pl.ds(pl.multiple_of(i * BLOCK, BLOCK), BLOCK)
        qg = qg_ref[rows, :].astype(f32)
        low = low_half(qg.shape)
        zero = jnp.zeros_like(qg)
        wide32 = jnp.concatenate([jnp.where(low, qg, zero), jnp.where(low, zero, qg)], axis=0)
        wide = wide32.astype(bf16)
        for t in range(pairs):
            sc[:, t * 256 : (t + 1) * 256] = nt(wide, keys(ids, t))
        step = 16
        for r in range(BLOCK // step):
            s = sc[r * step : (r + 1) * step, :width]
            dp = sc[BLOCK + r * step : BLOCK + (r + 1) * step, :width]
            last = jnp.where(odd, MASKED, s[:, width - BLOCK :])
            s = jnp.concatenate([s[:, : width - BLOCK], last], axis=1)
            e = jnp.exp2((s - jnp.max(s, axis=1, keepdims=True)) * (SCALE * LOG2E))
            p = e * (1.0 / jnp.sum(e, axis=1, keepdims=True))
            delta = jnp.sum(p * dp, axis=1, keepdims=True)
            ds = p * (dp - delta) * SCALE
            xs[r * step : (r + 1) * step, :width] = ds.astype(bf16)
            xs[BLOCK + r * step : BLOCK + (r + 1) * step, :width] = p.astype(bf16)
        every = jnp.concatenate([keys(ids, t) for t in range(pairs)], axis=0)
        mixed = nn(xs[:, :width], every)
        od_ref[rows, :] = jnp.where(low, mixed[:BLOCK], mixed[BLOCK:]).astype(bf16)
        wide_t = wide32.T.astype(bf16)
        for t in range(pairs):
            part = nn(wide_t, xs[:, t * 256 : (t + 1) * 256])
            for u in (0, 1):
                at_key = pl.ds(pl.multiple_of(ids[2 * t + u] * BLOCK, BLOCK), BLOCK)
                acc[:, at_key] += part[:, u * BLOCK : (u + 1) * BLOCK]

    @pl.loop(0, QBLK)
    def _(i):
        pairs = NGLOB // 2 + (cnt_ref[i] + 1) // 2
        for v in range(NGLOB // 2 + 1, SLOTS // 2 + 1):
            pl.when(pairs == v)(functools.partial(row_block, i, v))

    for step, out in ((0, sum_own_ref), (1, sum_right_ref), (YS - 1, sum_left_ref), (2, sum_opp_ref)):
        start = at(step)

        @pl.loop(0, ROW // 256)
        def _(t):
            cols = pl.ds(pl.multiple_of(start + t * 256, 256), 256)
            out[pl.ds(pl.multiple_of(t * 256, 256), 256), :] = acc[:, cols].T.astype(bf16)


def attend(table, counts, y, kv_parts, qg, after):
    vmem = pl.BlockSpec(memory_space=pltpu.VMEM)
    smem = pl.BlockSpec(memory_space=pltpu.SMEM)
    row = jax.ShapeDtypeStruct((ROW, 128), bf16)
    return pl.pallas_call(
        attend_kernel,
        in_specs=[smem] * 3 + [vmem] * 6 + [pl.BlockSpec(memory_space=pl.ANY)],
        out_specs=[vmem] * 5,
        out_shape=[row] * 5,
        scratch_shapes=[
            pltpu.VMEM((NODES, 128), bf16),
            pltpu.VMEM((128, NODES), f32),
            pltpu.VMEM((256, SLOTS * BLOCK), f32),
            pltpu.VMEM((256, SLOTS * BLOCK), bf16),
        ],
        compiler_params=VMEM,
        cost_estimate=pl.CostEstimate(
            flops=26 * 10**9, bytes_accessed=6 << 20, transcendentals=0
        ),
        name="attend",
    )(table, counts, y, *kv_parts, qg, after)


def out_kernel(a_ref, b_ref, wo_ref, o_ref, total):
    step = pl.program_id(0)

    @pl.when(step == 0)
    def _():
        total[...] = jnp.zeros_like(total)

    cols = [pair_up(a_ref[u].astype(f32), b_ref[u].astype(f32))[1] for u in (0, 1)]
    total[...] += nn(jnp.concatenate(cols, axis=1).astype(bf16), wo_ref[...])

    @pl.when(step == pl.num_programs(0) - 1)
    def _():
        o_ref[...] = total[...].astype(bf16)


SECOND = pl.BlockSpec((2, NODE_DEV, 128), lambda i: (i, 1, 0))


def project_out(od_a, joint, w_out):
    d = w_out.shape[1]
    tile = pl.BlockSpec((2, NODE_DEV, 128), lambda i: (i, 0, 0))
    return pl.pallas_call(
        out_kernel,
        grid=(ZS // 2,),
        in_specs=[tile, SECOND, pl.BlockSpec((256, d), lambda i: (i, 0))],
        out_specs=whole((NODE_DEV, d)),
        out_shape=jax.ShapeDtypeStruct((NODE_DEV, d), bf16),
        scratch_shapes=[pltpu.VMEM((NODE_DEV, d), f32)],
        compiler_params=VMEM,
        name="project_out",
    )(od_a, joint, w_out)


def nodes_kernel(oa_ref, ob_ref, ka_ref, kb_ref, wq_ref, wk_ref, wv_ref, o_ref, total):
    step = pl.program_id(0)

    @pl.when(step == 0)
    def _():
        total[...] = jnp.zeros_like(total)

    dq, dk, dv = [], [], []
    for u in (0, 1):
        dq.append(pair_up(oa_ref[u].astype(f32), ob_ref[u].astype(f32))[0])
        k, v = pair_up(ka_ref[u].astype(f32), kb_ref[u].astype(f32))
        dk.append(k)
        dv.append(v)
    add = nt(jnp.concatenate(dq, axis=1).astype(bf16), wq_ref[...])
    add += nt(jnp.concatenate(dk, axis=1).astype(bf16), wk_ref[...])
    add += nt(jnp.concatenate(dv, axis=1).astype(bf16), wv_ref[...])
    total[...] += add

    @pl.when(step == pl.num_programs(0) - 1)
    def _():
        o_ref[...] = total[...].astype(bf16)


def node_grads(od_a, joint, kv_b, w_qkv):
    d = w_qkv.shape[0]
    tile = pl.BlockSpec((2, NODE_DEV, 128), lambda i: (i, 0, 0))
    steps = ZS // 2
    return pl.pallas_call(
        nodes_kernel,
        grid=(steps,),
        in_specs=[tile, SECOND, tile, tile]
        + [pl.BlockSpec((d, 256), functools.partial(lambda i, third: (0, third * steps + i), third=k)) for k in range(3)],
        out_specs=whole((NODE_DEV, d)),
        out_shape=jax.ShapeDtypeStruct((NODE_DEV, d), bf16),
        scratch_shapes=[pltpu.VMEM((NODE_DEV, d), f32)],
        compiler_params=VMEM,
        name="node_grads",
    )(od_a, joint, joint, kv_b, w_qkv, w_qkv, w_qkv)


def swap(values, axis):
    return lax.all_to_all(values, axis, split_axis=0, concat_axis=0, tiled=True)


RIGHT = [(i, (i + 1) % YS) for i in range(YS)]
LEFT = [(i, (i - 1) % YS) for i in range(YS)]
OPPOSITE = [(i, (i + 2) % YS) for i in range(YS)]


def gather_row(own):
    left = lax.ppermute(own, "y", RIGHT)
    right = lax.ppermute(own, "y", LEFT)
    opp_lo = lax.ppermute(left[:HALF], "y", RIGHT)
    opp_hi = lax.ppermute(right[HALF:], "y", LEFT)
    return own, left, right, opp_lo, opp_hi


def sum_kernel(count, *refs):
    parts = (r[...].astype(f32) for r in refs[:count])
    refs[-1][...] = sum(parts).astype(bf16)


def sum_parts(parts, after):
    rows, cols = parts[0].shape
    tile = pl.BlockSpec((rows // 2, cols), lambda i: (i, 0))
    return pl.pallas_call(
        functools.partial(sum_kernel, len(parts)),
        grid=(2,),
        in_specs=[tile] * len(parts) + [pl.BlockSpec(memory_space=pl.ANY)] * len(after),
        out_specs=tile,
        out_shape=jax.ShapeDtypeStruct((rows, cols), bf16),
        compiler_params=VMEM,
        name="sum_parts",
    )(*parts, *after)


def sum_join_kernel(a_ref, b_ref, c_ref, d_ref, od_ref, o_ref):
    total = sum(r[...].astype(f32) for r in (a_ref, b_ref, c_ref, d_ref)).astype(bf16)
    pieces = o_ref.shape[0]
    for u in range(pieces):
        rows = slice(u * NODE_DEV, (u + 1) * NODE_DEV)
        o_ref[u, :NODE_DEV, :] = total[rows]
        o_ref[u, NODE_DEV:, :] = od_ref[rows, :]


def sum_join(parts, od):
    tile = pl.BlockSpec((HALF, 128), lambda i: (i, 0))
    return pl.pallas_call(
        sum_join_kernel,
        grid=(2,),
        in_specs=[tile] * 5,
        out_specs=pl.BlockSpec((ZS // 2, 2 * NODE_DEV, 128), lambda i: (i, 0, 0)),
        out_shape=jax.ShapeDtypeStruct((ZS, 2 * NODE_DEV, 128), bf16),
        compiler_params=VMEM,
        name="sum_join",
    )(*parts, od)


def send_row(own, to_right, to_left, opp):
    return [
        own,
        lax.ppermute(to_right, "y", RIGHT),
        lax.ppermute(to_left, "y", LEFT),
        lax.ppermute(opp, "y", OPPOSITE),
    ]


def hold_kernel(x_ref, after_ref, o_ref):
    o_ref[...] = x_ref[...]


def hold(values, after):
    vmem = pl.BlockSpec(memory_space=pltpu.VMEM)
    return pl.pallas_call(
        hold_kernel,
        in_specs=[vmem, pl.BlockSpec(memory_space=pl.ANY)],
        out_specs=vmem,
        out_shape=jax.ShapeDtypeStruct(values.shape, values.dtype),
        compiler_params=VMEM,
        name="hold",
    )(values, after)


def gate_kernel(*refs):
    pass


def gate(values, after):
    anywhere = pl.BlockSpec(memory_space=pl.ANY)
    return pl.pallas_call(
        gate_kernel,
        in_specs=[anywhere] * (len(values) + len(after)),
        out_specs=[anywhere] * len(values),
        out_shape=[jax.ShapeDtypeStruct(v.shape, v.dtype) for v in values],
        input_output_aliases={i: i for i in range(len(values))},
        compiler_params=VMEM,
        name="gate",
    )(*values, *after)


def weight_kernel(oa_ref, ob_ref, ka_ref, kb_ref, f_ref, o_ref, grads):
    @pl.when(pl.program_id(0) == 0)
    def _():
        @pl.loop(0, ZS)
        def _(t):
            rows = pl.ds(pl.multiple_of(t * NODE_DEV, NODE_DEV), NODE_DEV)
            dq = pair_up(oa_ref[rows, :].astype(f32), ob_ref[rows, :].astype(f32))[0]
            dk, dv = pair_up(ka_ref[t, :NODE_DEV, :].astype(f32), kb_ref[rows, :].astype(f32))
            for k, part in enumerate((dq, dk, dv)):
                grads[k * 128 : (k + 1) * 128, rows] = part.T.astype(bf16)

    o_ref[...] = nn(grads[...], f_ref[...]).T.astype(bf16)


def weight_share(od_a, od_b, joint, kv_b, feats_row):
    d = feats_row.shape[1]
    part = whole((ROW, 128))
    return pl.pallas_call(
        weight_kernel,
        grid=(d // 256,),
        in_specs=[part, part, whole(joint.shape), part, pl.BlockSpec((ROW, 256), lambda i: (0, i))],
        out_specs=pl.BlockSpec((256, 384), lambda i: (i, 0)),
        out_shape=jax.ShapeDtypeStruct((d, 384), bf16),
        scratch_shapes=[pltpu.VMEM((384, ROW), bf16)],
        compiler_params=VMEM,
        name="weight_share",
    )(od_a, od_b, joint, kv_b, feats_row)


def on_device(node_feats, w_qkv, w_out, cotangent, block_neighbors, block_counts, global_blocks):
    feats = node_feats[0]
    cot = cotangent[0]
    y = lax.axis_index("y")
    neighbors = lax.dynamic_slice_in_dim(block_neighbors[0], y * QBLK, QBLK, 0)
    counts = lax.dynamic_slice_in_dim(block_counts[0], y * QBLK, QBLK, 0)
    table = jnp.concatenate([jnp.broadcast_to(global_blocks[0][None], (QBLK, NGLOB)), neighbors], axis=1).reshape(-1)
    y_arr = y.reshape(1).astype(jnp.int32)

    kv = project_kv(feats, w_qkv)
    qg = project_qg(feats, cot, w_qkv, w_out)
    kv_row = [gather_row(swap(v, "z").reshape(ROW, 128)) for v in kv]
    qg_row = [swap(v, "z").reshape(ROW, 128) for v in qg]
    feats_late = hold(feats, qg_row[0])
    feats_row = lax.all_gather(feats_late, "z", axis=0, tiled=True)
    od_a, *kv_a = attend(table, counts, y_arr, kv_row[0], qg_row[0], feats_late)
    to_nodes = lambda v: swap(v.reshape(ZS, NODE_DEV, 128), "z")
    (od_a_late,) = gate([od_a], [qg_row[1]])
    od_nodes_a = to_nodes(od_a_late)
    parts_a = send_row(*kv_a)
    late = attend(table, counts, y_arr, kv_row[1], qg_row[1], od_a_late)
    od_b, *kv_b = gate(late, parts_a[1:] + [od_nodes_a])
    parts_b = send_row(*kv_b)
    joint = sum_join(parts_a, od_b)
    joint_nodes = swap(joint, "z")
    sum_b = sum_parts(parts_b, (joint_nodes,))
    kv_nodes_b = to_nodes(sum_b)
    attn_update = project_out(od_nodes_a, joint_nodes, w_out)
    grad_nodes = node_grads(od_nodes_a, joint_nodes, kv_nodes_b, w_qkv)

    share = weight_share(od_a_late, od_b, joint, sum_b, feats_row)
    d = share.shape[0]
    share = share.reshape(4, 2, d // 8, 384)
    c = lax.axis_index("c")
    mine, theirs = (lax.dynamic_index_in_dim(share, k, 1, keepdims=False) for k in (c, 1 - c))
    theirs = lax.ppermute(theirs, "c", [(0, 1), (1, 0)])
    share = sum_parts([v.reshape(d // 2, 384) for v in (mine, theirs)], (kv_nodes_b,))
    share = share.reshape(16, d // 32, 384)
    share = jnp.sum(swap(share, ("x", "y")).astype(f32), axis=0)
    share = swap(share.reshape(ZS, d // 256, 384), "z")
    share = share.reshape(ZS, d // 256, 3, 128).transpose(1, 2, 0, 3)
    grad_weights = share.reshape(d // 256, 3 * H * HD)
    return attn_update[None], grad_nodes[None], grad_weights


def solution(mesh):
    fine = Mesh(np.asarray(mesh.devices).reshape(4, 2, YS, ZS), ("x", "c", "y", "z"))
    dp, seq = ("x", "c"), ("y", "z")
    in_specs = (P(dp, seq, None), P(), P(), P(dp, seq, None), P(dp, None, None), P(dp, None), P(dp, None))
    out_specs = (P(dp, seq, None), P(dp, seq, None), P(dp + seq, None))
    return jax.shard_map(on_device, mesh=fine, in_specs=in_specs, out_specs=out_specs, check_vma=False)
```

```python
import functools
import math

import jax
import jax.numpy as jnp
import numpy as np
from jax import lax
from jax.experimental import pallas as pl
from jax.experimental.pallas import tpu as pltpu
from jax.sharding import Mesh
from jax.sharding import PartitionSpec as P

H = 16
HD = 64
BLOCK = 128
MAXNB = 8
NGLOB = 4
SLOTS = MAXNB + NGLOB
YS = 4
ZS = 8
NODE_DEV = 256
ROW = NODE_DEV * ZS
QBLK = ROW // BLOCK
NODES = ROW * YS
HALF = ROW // 2
SCALE = HD**-0.5
LOG2E = math.log2(math.e)
MASKED = -3.0e38
VMEM = pltpu.CompilerParams(vmem_limit_bytes=60 * 1024 * 1024)

bf16 = jnp.bfloat16
f32 = jnp.float32


def low_half(shape):
    return lax.broadcasted_iota(jnp.int32, shape, 1) < HD


def pair_up(first, second):
    low = low_half(first.shape)
    return (
        jnp.where(low, first, pltpu.roll(second, HD, 1)),
        jnp.where(low, pltpu.roll(first, HD, 1), second),
    )


def nt(a, b):
    return lax.dot_general(a, b, (((1,), (1,)), ((), ())), preferred_element_type=f32)


def nn(a, b):
    return lax.dot_general(a, b, (((1,), (0,)), ((), ())), preferred_element_type=f32)


def put_pairs(first, second, a_ref, b_ref):
    for u in (0, 1):
        cols = slice(u * 128, (u + 1) * 128)
        a, b = pair_up(first[:, cols], second[:, cols])
        a_ref[u] = a.astype(bf16)
        b_ref[u] = b.astype(bf16)


def kv_kernel(f_ref, wk_ref, wv_ref, o_ref):
    a_ref, b_ref = o_ref.at[:, :NODE_DEV], o_ref.at[:, NODE_DEV:]
    put_pairs(nn(f_ref[...], wk_ref[...]), nn(f_ref[...], wv_ref[...]), a_ref, b_ref)


def split_kernel(x_ref, a_ref, b_ref):
    for u in range(x_ref.shape[0]):
        rows = slice(u * NODE_DEV, (u + 1) * NODE_DEV)
        a_ref[rows, :] = x_ref[u, :NODE_DEV, :]
        b_ref[rows, :] = x_ref[u, NODE_DEV:, :]


def split_heads(both):
    tile = pl.BlockSpec((HALF, 128), lambda i: (i, 0))
    return pl.pallas_call(
        split_kernel,
        grid=(2,),
        in_specs=[pl.BlockSpec((ZS // 2, 2 * NODE_DEV, 128), lambda i: (i, 0, 0))],
        out_specs=[tile, tile],
        out_shape=[jax.ShapeDtypeStruct((ROW, 128), bf16)] * 2,
        compiler_params=VMEM,
        name="split_heads",
    )(both)


def qg_kernel(f_ref, c_ref, wq_ref, wo_ref, a_ref, b_ref):
    put_pairs(nn(f_ref[...], wq_ref[...]), nt(c_ref[...], wo_ref[...]), a_ref, b_ref)


def whole(shape):
    return pl.BlockSpec(shape, lambda i: (0,) * len(shape))


def project_kv(feats, w_qkv):
    d = feats.shape[1]
    return pl.pallas_call(
        kv_kernel,
        grid=(ZS // 2,),
        in_specs=[
            whole((NODE_DEV, d)),
            pl.BlockSpec((d, 256), lambda i: (0, ZS // 2 + i)),
            pl.BlockSpec((d, 256), lambda i: (0, ZS + i)),
        ],
        out_specs=pl.BlockSpec((2, 2 * NODE_DEV, 128), lambda i: (i, 0, 0)),
        out_shape=jax.ShapeDtypeStruct((ZS, 2 * NODE_DEV, 128), bf16),
        compiler_params=VMEM,
        name="project_kv",
    )(feats, w_qkv, w_qkv)


def project_qg(feats, cot, w_qkv, w_out):
    d = feats.shape[1]
    out = jax.ShapeDtypeStruct((ZS, NODE_DEV, 128), bf16)
    tile = pl.BlockSpec((2, NODE_DEV, 128), lambda i: (i, 0, 0))
    return pl.pallas_call(
        qg_kernel,
        grid=(ZS // 2,),
        in_specs=[
            whole((NODE_DEV, d)),
            whole((NODE_DEV, d)),
            pl.BlockSpec((d, 256), lambda i: (0, i)),
            pl.BlockSpec((256, d), lambda i: (i, 0)),
        ],
        out_specs=[tile, tile],
        out_shape=[out, out],
        compiler_params=VMEM,
        name="project_qg",
    )(feats, cot, w_qkv, w_out)


def attend_kernel(
    tab_ref, cnt_ref, y_ref, own_ref, left_ref, right_ref, opp_ref, qg_ref, after_ref,
    od_ref, sum_own_ref, sum_right_ref, sum_left_ref, sum_opp_ref,
    kv_s, acc, sc, xs,
):
    y = y_ref[0]
    at = lambda step: lax.rem(y + step, YS) * ROW

    kv_s[pl.ds(pl.multiple_of(at(0), ROW), ROW), :] = own_ref[...]
    kv_s[pl.ds(pl.multiple_of(at(YS - 1), ROW), ROW), :] = left_ref[...]
    kv_s[pl.ds(pl.multiple_of(at(1), ROW), ROW), :] = right_ref[...]
    kv_s[pl.ds(pl.multiple_of(at(2), ROW), ROW), :] = opp_ref[...]

    @pl.loop(0, NODES // 512)
    def _(t):
        acc[:, pl.ds(pl.multiple_of(t * 512, 512), 512)] = jnp.zeros((128, 512), f32)

    def keys(ids, t):
        rows = [kv_s[pl.ds(pl.multiple_of(ids[2 * t + u] * BLOCK, BLOCK), BLOCK), :] for u in (0, 1)]
        return jnp.concatenate(rows, axis=0)

    def row_block(i, pairs):
        width = pairs * 256
        ids = [tab_ref[i * SLOTS + t] for t in range(2 * pairs)]
        odd = lax.rem(cnt_ref[i], 2) == 1
        rows = pl.ds(pl.multiple_of(i * BLOCK, BLOCK), BLOCK)
        qg = qg_ref[rows, :].astype(f32)
        low = low_half(qg.shape)
        zero = jnp.zeros_like(qg)
        wide32 = jnp.concatenate([jnp.where(low, qg, zero), jnp.where(low, zero, qg)], axis=0)
        wide = wide32.astype(bf16)
        for t in range(pairs):
            sc[:, t * 256 : (t + 1) * 256] = nt(wide, keys(ids, t))
        step = 16
        for r in range(BLOCK // step):
            s = sc[r * step : (r + 1) * step, :width]
            dp = sc[BLOCK + r * step : BLOCK + (r + 1) * step, :width]
            last = jnp.where(odd, MASKED, s[:, width - BLOCK :])
            s = jnp.concatenate([s[:, : width - BLOCK], last], axis=1)
            e = jnp.exp2((s - jnp.max(s, axis=1, keepdims=True)) * (SCALE * LOG2E))
            p = e * (1.0 / jnp.sum(e, axis=1, keepdims=True))
            delta = jnp.sum(p * dp, axis=1, keepdims=True)
            ds = p * (dp - delta) * SCALE
            xs[r * step : (r + 1) * step, :width] = ds.astype(bf16)
            xs[BLOCK + r * step : BLOCK + (r + 1) * step, :width] = p.astype(bf16)
        every = jnp.concatenate([keys(ids, t) for t in range(pairs)], axis=0)
        mixed = nn(xs[:, :width], every)
        od_ref[rows, :] = jnp.where(low, mixed[:BLOCK], mixed[BLOCK:]).astype(bf16)
        wide_t = wide32.T.astype(bf16)
        for t in range(pairs):
            part = nn(wide_t, xs[:, t * 256 : (t + 1) * 256])
            for u in (0, 1):
                at_key = pl.ds(pl.multiple_of(ids[2 * t + u] * BLOCK, BLOCK), BLOCK)
                acc[:, at_key] += part[:, u * BLOCK : (u + 1) * BLOCK]

    @pl.loop(0, QBLK)
    def _(i):
        pairs = NGLOB // 2 + (cnt_ref[i] + 1) // 2
        for v in range(NGLOB // 2 + 1, SLOTS // 2 + 1):
            pl.when(pairs == v)(functools.partial(row_block, i, v))

    for step, out in ((0, sum_own_ref), (1, sum_right_ref), (YS - 1, sum_left_ref), (2, sum_opp_ref)):
        start = at(step)

        @pl.loop(0, ROW // 256)
        def _(t):
            cols = pl.ds(pl.multiple_of(start + t * 256, 256), 256)
            out[pl.ds(pl.multiple_of(t * 256, 256), 256), :] = acc[:, cols].T.astype(bf16)


def attend(table, counts, y, kv_parts, qg, after):
    vmem = pl.BlockSpec(memory_space=pltpu.VMEM)
    smem = pl.BlockSpec(memory_space=pltpu.SMEM)
    row = jax.ShapeDtypeStruct((ROW, 128), bf16)
    return pl.pallas_call(
        attend_kernel,
        in_specs=[smem] * 3 + [vmem] * 5 + [pl.BlockSpec(memory_space=pl.ANY)],
        out_specs=[vmem] * 5,
        out_shape=[row] * 5,
        scratch_shapes=[
            pltpu.VMEM((NODES, 128), bf16),
            pltpu.VMEM((128, NODES), f32),
            pltpu.VMEM((256, SLOTS * BLOCK), f32),
            pltpu.VMEM((256, SLOTS * BLOCK), bf16),
        ],
        compiler_params=VMEM,
        cost_estimate=pl.CostEstimate(
            flops=26 * 10**9, bytes_accessed=6 << 20, transcendentals=0
        ),
        name="attend",
    )(table, counts, y, *kv_parts, qg, after)


def out_kernel(a_ref, b_ref, wo_ref, o_ref, total):
    step = pl.program_id(0)

    @pl.when(step == 0)
    def _():
        total[...] = jnp.zeros_like(total)

    cols = [pair_up(a_ref[u].astype(f32), b_ref[u].astype(f32))[1] for u in (0, 1)]
    total[...] += nn(jnp.concatenate(cols, axis=1).astype(bf16), wo_ref[...])

    @pl.when(step == pl.num_programs(0) - 1)
    def _():
        o_ref[...] = total[...].astype(bf16)


SECOND = pl.BlockSpec((2, NODE_DEV, 128), lambda i: (i, 1, 0))


def project_out(od_a, joint, w_out):
    d = w_out.shape[1]
    tile = pl.BlockSpec((2, NODE_DEV, 128), lambda i: (i, 0, 0))
    return pl.pallas_call(
        out_kernel,
        grid=(ZS // 2,),
        in_specs=[tile, SECOND, pl.BlockSpec((256, d), lambda i: (i, 0))],
        out_specs=whole((NODE_DEV, d)),
        out_shape=jax.ShapeDtypeStruct((NODE_DEV, d), bf16),
        scratch_shapes=[pltpu.VMEM((NODE_DEV, d), f32)],
        compiler_params=VMEM,
        name="project_out",
    )(od_a, joint, w_out)


def nodes_kernel(oa_ref, ob_ref, ka_ref, kb_ref, wq_ref, wk_ref, wv_ref, o_ref, total):
    step = pl.program_id(0)

    @pl.when(step == 0)
    def _():
        total[...] = jnp.zeros_like(total)

    dq, dk, dv = [], [], []
    for u in (0, 1):
        dq.append(pair_up(oa_ref[u].astype(f32), ob_ref[u].astype(f32))[0])
        k, v = pair_up(ka_ref[u].astype(f32), kb_ref[u].astype(f32))
        dk.append(k)
        dv.append(v)
    add = nt(jnp.concatenate(dq, axis=1).astype(bf16), wq_ref[...])
    add += nt(jnp.concatenate(dk, axis=1).astype(bf16), wk_ref[...])
    add += nt(jnp.concatenate(dv, axis=1).astype(bf16), wv_ref[...])
    total[...] += add

    @pl.when(step == pl.num_programs(0) - 1)
    def _():
        o_ref[...] = total[...].astype(bf16)


def node_grads(od_a, joint, kv_b, w_qkv):
    d = w_qkv.shape[0]
    tile = pl.BlockSpec((2, NODE_DEV, 128), lambda i: (i, 0, 0))
    steps = ZS // 2
    return pl.pallas_call(
        nodes_kernel,
        grid=(steps,),
        in_specs=[tile, SECOND, tile, tile]
        + [pl.BlockSpec((d, 256), functools.partial(lambda i, third: (0, third * steps + i), third=k)) for k in range(3)],
        out_specs=whole((NODE_DEV, d)),
        out_shape=jax.ShapeDtypeStruct((NODE_DEV, d), bf16),
        scratch_shapes=[pltpu.VMEM((NODE_DEV, d), f32)],
        compiler_params=VMEM,
        name="node_grads",
    )(od_a, joint, joint, kv_b, w_qkv, w_qkv, w_qkv)


def spread_kernel(x_ref, o_ref):
    for z in range(ZS):
        for third in range(3):
            cols = third * H * HD + z * 128
            o_ref[:, cols : cols + 128] = x_ref[z, :, third * 128 : (third + 1) * 128]


def spread(share):
    vmem = pl.BlockSpec(memory_space=pltpu.VMEM)
    return pl.pallas_call(
        spread_kernel,
        in_specs=[vmem],
        out_specs=vmem,
        out_shape=jax.ShapeDtypeStruct((share.shape[1], 3 * H * HD), f32),
        compiler_params=VMEM,
        name="spread",
    )(share)


def swap(values, axis):
    return lax.all_to_all(values, axis, split_axis=0, concat_axis=0, tiled=True)


RIGHT = [(i, (i + 1) % YS) for i in range(YS)]
LEFT = [(i, (i - 1) % YS) for i in range(YS)]
OPPOSITE = [(i, (i + 2) % YS) for i in range(YS)]


def gather_row(own):
    return own, lax.ppermute(own, "y", RIGHT), lax.ppermute(own, "y", LEFT), lax.ppermute(own, "y", OPPOSITE)


def sum_kernel(count, *refs):
    parts = (r[...].astype(f32) for r in refs[:count])
    refs[-1][...] = sum(parts).astype(bf16)


def sum_parts(parts, after):
    rows, cols = parts[0].shape
    tile = pl.BlockSpec((rows // 2, cols), lambda i: (i, 0))
    return pl.pallas_call(
        functools.partial(sum_kernel, len(parts)),
        grid=(2,),
        in_specs=[tile] * len(parts) + [pl.BlockSpec(memory_space=pl.ANY)] * len(after),
        out_specs=tile,
        out_shape=jax.ShapeDtypeStruct((rows, cols), bf16),
        compiler_params=VMEM,
        name="sum_parts",
    )(*parts, *after)


def sum_join_kernel(a_ref, b_ref, c_ref, d_ref, od_ref, o_ref):
    total = sum(r[...].astype(f32) for r in (a_ref, b_ref, c_ref, d_ref)).astype(bf16)
    pieces = o_ref.shape[0]
    for u in range(pieces):
        rows = slice(u * NODE_DEV, (u + 1) * NODE_DEV)
        o_ref[u, :NODE_DEV, :] = total[rows]
        o_ref[u, NODE_DEV:, :] = od_ref[rows, :]


def sum_join(parts, od):
    tile = pl.BlockSpec((HALF, 128), lambda i: (i, 0))
    return pl.pallas_call(
        sum_join_kernel,
        grid=(2,),
        in_specs=[tile] * 5,
        out_specs=pl.BlockSpec((ZS // 2, 2 * NODE_DEV, 128), lambda i: (i, 0, 0)),
        out_shape=jax.ShapeDtypeStruct((ZS, 2 * NODE_DEV, 128), bf16),
        compiler_params=VMEM,
        name="sum_join",
    )(*parts, od)


def send_row(own, to_right, to_left, opp):
    return [
        own,
        lax.ppermute(to_right, "y", RIGHT),
        lax.ppermute(to_left, "y", LEFT),
        lax.ppermute(opp, "y", OPPOSITE),
    ]


def hold_kernel(x_ref, after_ref, o_ref):
    o_ref[...] = x_ref[...]


def hold(values, after):
    vmem = pl.BlockSpec(memory_space=pltpu.VMEM)
    return pl.pallas_call(
        hold_kernel,
        in_specs=[vmem, pl.BlockSpec(memory_space=pl.ANY)],
        out_specs=vmem,
        out_shape=jax.ShapeDtypeStruct(values.shape, values.dtype),
        compiler_params=VMEM,
        name="hold",
    )(values, after)


def gate_kernel(*refs):
    pass


def gate(values, after):
    anywhere = pl.BlockSpec(memory_space=pl.ANY)
    return pl.pallas_call(
        gate_kernel,
        in_specs=[anywhere] * (len(values) + len(after)),
        out_specs=[anywhere] * len(values),
        out_shape=[jax.ShapeDtypeStruct(v.shape, v.dtype) for v in values],
        input_output_aliases={i: i for i in range(len(values))},
        compiler_params=VMEM,
        name="gate",
    )(*values, *after)


def weight_kernel(oa_ref, ob_ref, ka_ref, kb_ref, f_ref, o_ref, grads):
    @pl.when(pl.program_id(0) == 0)
    def _():
        @pl.loop(0, ZS)
        def _(t):
            rows = pl.ds(pl.multiple_of(t * NODE_DEV, NODE_DEV), NODE_DEV)
            dq = pair_up(oa_ref[rows, :].astype(f32), ob_ref[rows, :].astype(f32))[0]
            dk, dv = pair_up(ka_ref[t, :NODE_DEV, :].astype(f32), kb_ref[rows, :].astype(f32))
            for k, part in enumerate((dq, dk, dv)):
                grads[k * 128 : (k + 1) * 128, rows] = part.T.astype(bf16)

    o_ref[...] = nn(grads[...], f_ref[...]).T.astype(bf16)


def weight_share(od_a, od_b, joint, kv_b, feats_row):
    d = feats_row.shape[1]
    part = whole((ROW, 128))
    return pl.pallas_call(
        weight_kernel,
        grid=(d // 256,),
        in_specs=[part, part, whole(joint.shape), part, pl.BlockSpec((ROW, 256), lambda i: (0, i))],
        out_specs=pl.BlockSpec((256, 384), lambda i: (i, 0)),
        out_shape=jax.ShapeDtypeStruct((d, 384), bf16),
        scratch_shapes=[pltpu.VMEM((384, ROW), bf16)],
        compiler_params=VMEM,
        name="weight_share",
    )(od_a, od_b, joint, kv_b, feats_row)


def on_device(node_feats, w_qkv, w_out, cotangent, block_neighbors, block_counts, global_blocks):
    feats = node_feats[0]
    cot = cotangent[0]
    y = lax.axis_index("y")
    neighbors = lax.dynamic_slice_in_dim(block_neighbors[0], y * QBLK, QBLK, 0)
    counts = lax.dynamic_slice_in_dim(block_counts[0], y * QBLK, QBLK, 0)
    table = jnp.concatenate([jnp.broadcast_to(global_blocks[0][None], (QBLK, NGLOB)), neighbors], axis=1).reshape(-1)
    y_arr = y.reshape(1).astype(jnp.int32)

    kv = project_kv(feats, w_qkv)
    qg = project_qg(feats, cot, w_qkv, w_out)
    kv_row = [gather_row(v) for v in split_heads(swap(kv, "z"))]
    qg_row = [swap(v, "z").reshape(ROW, 128) for v in qg]
    feats_late = hold(feats, qg_row[0])
    feats_row = lax.all_gather(feats_late, "z", axis=0, tiled=True)
    od_a, *kv_a = attend(table, counts, y_arr, kv_row[0], qg_row[0], feats_late)
    to_nodes = lambda v: swap(v.reshape(ZS, NODE_DEV, 128), "z")
    (od_a_late,) = gate([od_a], [qg_row[1]])
    od_nodes_a = to_nodes(od_a_late)
    parts_a = send_row(*kv_a)
    late = attend(table, counts, y_arr, kv_row[1], qg_row[1], od_a_late)
    od_b, *kv_b = gate(late, parts_a[1:] + [od_nodes_a])
    parts_b = send_row(*kv_b)
    joint = sum_join(parts_a, od_b)
    joint_nodes = swap(joint, "z")
    sum_b = sum_parts(parts_b, (joint_nodes,))
    kv_nodes_b = to_nodes(sum_b)
    attn_update = project_out(od_nodes_a, joint_nodes, w_out)
    grad_nodes = node_grads(od_nodes_a, joint_nodes, kv_nodes_b, w_qkv)

    share = weight_share(od_a_late, od_b, joint, sum_b, feats_row)
    d = share.shape[0]
    share = share.reshape(4, 2, d // 8, 384)
    c = lax.axis_index("c")
    mine, theirs = (lax.dynamic_index_in_dim(share, k, 1, keepdims=False) for k in (c, 1 - c))
    theirs = lax.ppermute(theirs, "c", [(0, 1), (1, 0)])
    share = sum_parts([v.reshape(d // 2, 384) for v in (mine, theirs)], (kv_nodes_b,))
    share = share.reshape(16, d // 32, 384)
    share = jnp.sum(swap(share, ("x", "y")).astype(f32), axis=0)
    share = gate([share.reshape(ZS, d // 256, 384)], [attn_update, grad_nodes])[0]
    grad_weights = spread(swap(share, "z"))
    return attn_update[None], grad_nodes[None], grad_weights


def solution(mesh):
    fine = Mesh(np.asarray(mesh.devices).reshape(4, 2, YS, ZS), ("x", "c", "y", "z"))
    dp, seq = ("x", "c"), ("y", "z")
    in_specs = (P(dp, seq, None), P(), P(), P(dp, seq, None), P(dp, None, None), P(dp, None), P(dp, None))
    out_specs = (P(dp, seq, None), P(dp, seq, None), P(dp + seq, None))
    return jax.shard_map(on_device, mesh=fine, in_specs=in_specs, out_specs=out_specs, check_vma=False)
```

```python
import functools
import math

import jax
import jax.numpy as jnp
import numpy as np
from jax import lax
from jax.experimental import pallas as pl
from jax.experimental.pallas import tpu as pltpu
from jax.sharding import Mesh
from jax.sharding import PartitionSpec as P

H = 16
HD = 64
BLOCK = 128
MAXNB = 8
NGLOB = 4
SLOTS = MAXNB + NGLOB
YS = 4
ZS = 8
NODE_DEV = 256
ROW = NODE_DEV * ZS
QBLK = ROW // BLOCK
NODES = ROW * YS
TURNED = (ZS, 2 * HD, NODE_DEV)
PIECES = YS * ZS
SCALE = HD**-0.5
LOG2E = math.log2(math.e)
MASKED = -3.0e38
VMEM = pltpu.CompilerParams(vmem_limit_bytes=60 * 1024 * 1024)

bf16 = jnp.bfloat16
f32 = jnp.float32


def low_half(shape):
    return lax.broadcasted_iota(jnp.int32, shape, 1) < HD


def pair_up(first, second):
    low = low_half(first.shape)
    return (
        jnp.where(low, first, pltpu.roll(second, HD, 1)),
        jnp.where(low, pltpu.roll(first, HD, 1), second),
    )


def pair_rows(first, second):
    return (
        jnp.concatenate([first[:HD], second[:HD]], axis=0),
        jnp.concatenate([first[HD:], second[HD:]], axis=0),
    )


def nt(a, b):
    return lax.dot_general(a, b, (((1,), (1,)), ((), ())), preferred_element_type=f32)


def nn(a, b):
    return lax.dot_general(a, b, (((1,), (0,)), ((), ())), preferred_element_type=f32)


def put_pairs(first, second, a_ref, b_ref):
    for u in (0, 1):
        cols = slice(u * 128, (u + 1) * 128)
        a, b = pair_up(first[:, cols], second[:, cols])
        a_ref[u] = a.astype(bf16)
        b_ref[u] = b.astype(bf16)


def kv_kernel(f_ref, wk_ref, wv_ref, o_ref):
    k = nn(f_ref[...], wk_ref[...])
    v = nn(f_ref[...], wv_ref[...])
    for u in (0, 1):
        cols = slice(u * 128, (u + 1) * 128)
        a, b = pair_rows(k[:, cols].T, v[:, cols].T)
        o_ref[u, :128, :] = a.astype(bf16)
        o_ref[u, 128:, :] = b.astype(bf16)


def split_kernel(x_ref, a_ref, b_ref):
    a_ref[...] = x_ref[:, :128, :]
    b_ref[...] = x_ref[:, 128:, :]


def split_heads(both):
    return pl.pallas_call(
        split_kernel,
        grid=(2,),
        in_specs=[pl.BlockSpec((ZS // 2, 256, NODE_DEV), lambda i: (i, 0, 0))],
        out_specs=[pl.BlockSpec((ZS // 2, 128, NODE_DEV), lambda i: (i, 0, 0))] * 2,
        out_shape=[jax.ShapeDtypeStruct(TURNED, bf16)] * 2,
        compiler_params=VMEM,
        name="split_heads",
    )(both)


def qg_kernel(f_ref, c_ref, wq_ref, wo_ref, a_ref, b_ref):
    put_pairs(nn(f_ref[...], wq_ref[...]), nt(c_ref[...], wo_ref[...]), a_ref, b_ref)


def whole(shape):
    return pl.BlockSpec(shape, lambda i: (0,) * len(shape))


def project_kv(feats, w_qkv):
    d = feats.shape[1]
    return pl.pallas_call(
        kv_kernel,
        grid=(ZS // 2,),
        in_specs=[
            whole((NODE_DEV, d)),
            pl.BlockSpec((d, 256), lambda i: (0, ZS // 2 + i)),
            pl.BlockSpec((d, 256), lambda i: (0, ZS + i)),
        ],
        out_specs=pl.BlockSpec((2, 256, NODE_DEV), lambda i: (i, 0, 0)),
        out_shape=jax.ShapeDtypeStruct((ZS, 256, NODE_DEV), bf16),
        compiler_params=VMEM,
        name="project_kv",
    )(feats, w_qkv, w_qkv)


def project_qg(feats, cot, w_qkv, w_out):
    d = feats.shape[1]
    out = jax.ShapeDtypeStruct((ZS, NODE_DEV, 128), bf16)
    tile = pl.BlockSpec((2, NODE_DEV, 128), lambda i: (i, 0, 0))
    return pl.pallas_call(
        qg_kernel,
        grid=(ZS // 2,),
        in_specs=[
            whole((NODE_DEV, d)),
            whole((NODE_DEV, d)),
            pl.BlockSpec((d, 256), lambda i: (0, i)),
            pl.BlockSpec((256, d), lambda i: (i, 0)),
        ],
        out_specs=[tile, tile],
        out_shape=[out, out],
        compiler_params=VMEM,
        name="project_qg",
    )(feats, cot, w_qkv, w_out)


def attend_kernel(
    tab_ref, cnt_ref, order_ref, y_ref, own_ref, left_ref, right_ref, opp_ref, qg_ref, after_ref,
    od_ref, sum_own_ref, sum_right_ref, sum_left_ref, sum_opp_ref,
    kv_s, acc, sc0, sc1, xs0, xs1,
):
    y = y_ref[0]
    at = lambda step: lax.rem(y + step, YS) * ZS

    for step, ref in ((0, own_ref), (YS - 1, left_ref), (1, right_ref), (2, opp_ref)):
        kv_s[pl.ds(at(step), ZS)] = ref[...]

    @pl.loop(0, PIECES)
    def _(t):
        acc[t] = jnp.zeros((128, NODE_DEV), f32)

    def cols(block):
        return pl.ds(pl.multiple_of(lax.rem(block, 2) * BLOCK, BLOCK), BLOCK)

    def keys(ids, t):
        return jnp.concatenate([kv_s[lax.div(ids[2 * t + u], 2), :, cols(ids[2 * t + u])] for u in (0, 1)], axis=1)

    def score(i, pairs, sc):
        ids = [tab_ref[i * SLOTS + t] for t in range(2 * pairs)]
        rows = pl.ds(pl.multiple_of(i * BLOCK, BLOCK), BLOCK)
        qg = qg_ref[rows, :].astype(f32)
        low = low_half(qg.shape)
        zero = jnp.zeros_like(qg)
        wide32 = jnp.concatenate([jnp.where(low, qg, zero), jnp.where(low, zero, qg)], axis=0)
        wide = wide32.astype(bf16)
        for t in range(pairs):
            sc[:, t * 256 : (t + 1) * 256] = nn(wide, keys(ids, t))
        return i, ids, wide32.T.astype(bf16)

    def soften(i, pairs, sc, xs):
        width = pairs * 256
        count = cnt_ref[i]
        step = 16
        for r in range(BLOCK // step):
            s = sc[r * step : (r + 1) * step, :width]
            dp = sc[BLOCK + r * step : BLOCK + (r + 1) * step, :width]
            kept = [s[:, : (NGLOB + 1) * BLOCK]]
            for t in range(NGLOB + 1, 2 * pairs):
                kept.append(jnp.where(t - NGLOB < count, s[:, t * BLOCK : (t + 1) * BLOCK], MASKED))
            s = jnp.concatenate(kept, axis=1)
            e = jnp.exp2((s - jnp.max(s, axis=1, keepdims=True)) * (SCALE * LOG2E))
            p = e * (1.0 / jnp.sum(e, axis=1, keepdims=True))
            delta = jnp.sum(p * dp, axis=1, keepdims=True)
            ds = p * (dp - delta) * SCALE
            xs[r * step : (r + 1) * step, :width] = ds.astype(bf16)
            xs[BLOCK + r * step : BLOCK + (r + 1) * step, :width] = p.astype(bf16)

    def mix(state, pairs, xs):
        i, ids, wide_t = state
        every = jnp.concatenate([keys(ids, t) for t in range(pairs)], axis=1)
        mixed = nt(every, xs[:, : pairs * 256])
        od = jnp.concatenate([mixed[:HD, :BLOCK], mixed[HD:, BLOCK:]], axis=0)
        od_ref[lax.div(i, 2), :, cols(i)] = od.astype(bf16)
        for t in range(pairs):
            part = nn(wide_t, xs[:, t * 256 : (t + 1) * 256])
            for u in (0, 1):
                block = ids[2 * t + u]
                acc[lax.div(block, 2), :, cols(block)] += part[:, u * BLOCK : (u + 1) * BLOCK]

    def two_blocks(i, k, pairs):
        first = score(i, pairs, sc0)
        second = score(k, pairs, sc1)
        soften(i, pairs, sc0, xs0)
        mix(first, pairs, xs0)
        soften(k, pairs, sc1, xs1)
        mix(second, pairs, xs1)

    @pl.loop(0, QBLK // 2)
    def _(t):
        i, k = order_ref[2 * t], order_ref[2 * t + 1]
        pairs = NGLOB // 2 + (jnp.maximum(cnt_ref[i], cnt_ref[k]) + 1) // 2
        for v in range(NGLOB // 2 + 1, SLOTS // 2 + 1):
            pl.when(pairs == v)(functools.partial(two_blocks, i, k, v))

    for step, out in ((0, sum_own_ref), (1, sum_right_ref), (YS - 1, sum_left_ref), (2, sum_opp_ref)):
        start = at(step)

        @pl.loop(0, ZS)
        def _(t):
            out[t] = acc[start + t].astype(bf16)


def attend(table, counts, order, y, kv_parts, qg, after):
    vmem = pl.BlockSpec(memory_space=pltpu.VMEM)
    smem = pl.BlockSpec(memory_space=pltpu.SMEM)
    row = jax.ShapeDtypeStruct(TURNED, bf16)
    return pl.pallas_call(
        attend_kernel,
        in_specs=[smem] * 4 + [vmem] * 5 + [pl.BlockSpec(memory_space=pl.ANY)],
        out_specs=[vmem] * 5,
        out_shape=[row] * 5,
        scratch_shapes=[
            pltpu.VMEM((PIECES, 128, NODE_DEV), bf16),
            pltpu.VMEM((PIECES, 128, NODE_DEV), f32),
            pltpu.VMEM((256, SLOTS * BLOCK), f32),
            pltpu.VMEM((256, SLOTS * BLOCK), f32),
            pltpu.VMEM((256, SLOTS * BLOCK), bf16),
            pltpu.VMEM((256, SLOTS * BLOCK), bf16),
        ],
        compiler_params=VMEM,
        cost_estimate=pl.CostEstimate(
            flops=26 * 10**9, bytes_accessed=6 << 20, transcendentals=0
        ),
        name="attend",
    )(table, counts, order, y, *kv_parts, qg, after)


def turn(tiles):
    return jnp.concatenate(tiles, axis=0).astype(f32).T.astype(bf16)


def out_kernel(a_ref, b_ref, wo_ref, o_ref, total):
    step = pl.program_id(0)

    @pl.when(step == 0)
    def _():
        total[...] = jnp.zeros_like(total)

    att = [pair_rows(a_ref[u], b_ref[u])[1] for u in (0, 1)]
    total[...] += nn(turn(att), wo_ref[...])

    @pl.when(step == pl.num_programs(0) - 1)
    def _():
        o_ref[...] = total[...].astype(bf16)


SECOND = pl.BlockSpec((2, 128, NODE_DEV), lambda i: (i, 1, 0))


def project_out(od_a, joint, w_out):
    d = w_out.shape[1]
    tile = pl.BlockSpec((2, 128, NODE_DEV), lambda i: (i, 0, 0))
    return pl.pallas_call(
        out_kernel,
        grid=(ZS // 2,),
        in_specs=[tile, SECOND, pl.BlockSpec((256, d), lambda i: (i, 0))],
        out_specs=whole((NODE_DEV, d)),
        out_shape=jax.ShapeDtypeStruct((NODE_DEV, d), bf16),
        scratch_shapes=[pltpu.VMEM((NODE_DEV, d), f32)],
        compiler_params=VMEM,
        name="project_out",
    )(od_a, joint, w_out)


def nodes_kernel(oa_ref, ob_ref, ka_ref, kb_ref, wq_ref, wk_ref, wv_ref, o_ref, total):
    step = pl.program_id(0)

    @pl.when(step == 0)
    def _():
        total[...] = jnp.zeros_like(total)

    dq, dk, dv = [], [], []
    for u in (0, 1):
        dq.append(pair_rows(oa_ref[u], ob_ref[u])[0])
        k, v = pair_rows(ka_ref[u], kb_ref[u])
        dk.append(k)
        dv.append(v)
    add = nt(turn(dq), wq_ref[...])
    add += nt(turn(dk), wk_ref[...])
    add += nt(turn(dv), wv_ref[...])
    total[...] += add

    @pl.when(step == pl.num_programs(0) - 1)
    def _():
        o_ref[...] = total[...].astype(bf16)


def node_grads(od_a, joint, kv_b, w_qkv):
    d = w_qkv.shape[0]
    tile = pl.BlockSpec((2, 128, NODE_DEV), lambda i: (i, 0, 0))
    steps = ZS // 2
    return pl.pallas_call(
        nodes_kernel,
        grid=(steps,),
        in_specs=[tile, SECOND, tile, tile]
        + [pl.BlockSpec((d, 256), functools.partial(lambda i, third: (0, third * steps + i), third=k)) for k in range(3)],
        out_specs=whole((NODE_DEV, d)),
        out_shape=jax.ShapeDtypeStruct((NODE_DEV, d), bf16),
        scratch_shapes=[pltpu.VMEM((NODE_DEV, d), f32)],
        compiler_params=VMEM,
        name="node_grads",
    )(od_a, joint, joint, kv_b, w_qkv, w_qkv, w_qkv)


def spread_kernel(x_ref, o_ref):
    for z in range(ZS):
        for third in range(3):
            cols = third * H * HD + z * 128
            o_ref[:, cols : cols + 128] = x_ref[z, :, third * 128 : (third + 1) * 128]


def spread(share):
    vmem = pl.BlockSpec(memory_space=pltpu.VMEM)
    return pl.pallas_call(
        spread_kernel,
        in_specs=[vmem],
        out_specs=vmem,
        out_shape=jax.ShapeDtypeStruct((share.shape[1], 3 * H * HD), f32),
        compiler_params=VMEM,
        name="spread",
    )(share)


def swap(values, axis):
    return lax.all_to_all(values, axis, split_axis=0, concat_axis=0, tiled=True)


RIGHT = [(i, (i + 1) % YS) for i in range(YS)]
LEFT = [(i, (i - 1) % YS) for i in range(YS)]
OPPOSITE = [(i, (i + 2) % YS) for i in range(YS)]


def gather_row(own):
    return own, lax.ppermute(own, "y", RIGHT), lax.ppermute(own, "y", LEFT), lax.ppermute(own, "y", OPPOSITE)


def sum_kernel(count, *refs):
    parts = (r[...].astype(f32) for r in refs[:count])
    refs[-1][...] = sum(parts).astype(bf16)


def sum_parts(parts, after):
    shape = parts[0].shape
    tile = pl.BlockSpec((shape[0] // 2, *shape[1:]), lambda i: (i,) + (0,) * (len(shape) - 1))
    return pl.pallas_call(
        functools.partial(sum_kernel, len(parts)),
        grid=(2,),
        in_specs=[tile] * len(parts) + [pl.BlockSpec(memory_space=pl.ANY)] * len(after),
        out_specs=tile,
        out_shape=jax.ShapeDtypeStruct(shape, bf16),
        compiler_params=VMEM,
        name="sum_parts",
    )(*parts, *after)


def sum_join_kernel(a_ref, b_ref, c_ref, d_ref, od_ref, o_ref):
    o_ref[:, :128, :] = sum(r[...].astype(f32) for r in (a_ref, b_ref, c_ref, d_ref)).astype(bf16)
    o_ref[:, 128:, :] = od_ref[...]


def sum_join(parts, od):
    tile = pl.BlockSpec((ZS // 2, 128, NODE_DEV), lambda i: (i, 0, 0))
    return pl.pallas_call(
        sum_join_kernel,
        grid=(2,),
        in_specs=[tile] * 5,
        out_specs=pl.BlockSpec((ZS // 2, 256, NODE_DEV), lambda i: (i, 0, 0)),
        out_shape=jax.ShapeDtypeStruct((ZS, 256, NODE_DEV), bf16),
        compiler_params=VMEM,
        name="sum_join",
    )(*parts, od)


def send_row(own, to_right, to_left, opp):
    return [
        own,
        lax.ppermute(to_right, "y", RIGHT),
        lax.ppermute(to_left, "y", LEFT),
        lax.ppermute(opp, "y", OPPOSITE),
    ]


def hold_kernel(x_ref, after_ref, o_ref):
    o_ref[...] = x_ref[...]


def hold(values, after):
    vmem = pl.BlockSpec(memory_space=pltpu.VMEM)
    return pl.pallas_call(
        hold_kernel,
        in_specs=[vmem, pl.BlockSpec(memory_space=pl.ANY)],
        out_specs=vmem,
        out_shape=jax.ShapeDtypeStruct(values.shape, values.dtype),
        compiler_params=VMEM,
        name="hold",
    )(values, after)


def gate_kernel(*refs):
    pass


def gate(values, after):
    anywhere = pl.BlockSpec(memory_space=pl.ANY)
    return pl.pallas_call(
        gate_kernel,
        in_specs=[anywhere] * (len(values) + len(after)),
        out_specs=[anywhere] * len(values),
        out_shape=[jax.ShapeDtypeStruct(v.shape, v.dtype) for v in values],
        input_output_aliases={i: i for i in range(len(values))},
        compiler_params=VMEM,
        name="gate",
    )(*values, *after)


def weight_kernel(oa_ref, ob_ref, ka_ref, kb_ref, f_ref, o_ref, grads):
    @pl.when(pl.program_id(0) == 0)
    def _():
        for t in range(ZS):
            nodes = slice(t * NODE_DEV, (t + 1) * NODE_DEV)
            dq = pair_rows(oa_ref[t], ob_ref[t])[0]
            dk, dv = pair_rows(ka_ref[t, :128, :], kb_ref[t])
            for k, part in enumerate((dq, dk, dv)):
                grads[k * 128 : (k + 1) * 128, nodes] = part

    o_ref[...] = nn(grads[...], f_ref[...]).T.astype(bf16)


def weight_share(od_a, od_b, joint, kv_b, feats_row):
    d = feats_row.shape[1]
    part = whole(TURNED)
    return pl.pallas_call(
        weight_kernel,
        grid=(d // 256,),
        in_specs=[part, part, whole(joint.shape), part, pl.BlockSpec((ROW, 256), lambda i: (0, i))],
        out_specs=pl.BlockSpec((256, 384), lambda i: (i, 0)),
        out_shape=jax.ShapeDtypeStruct((d, 384), bf16),
        scratch_shapes=[pltpu.VMEM((384, ROW), bf16)],
        compiler_params=VMEM,
        name="weight_share",
    )(od_a, od_b, joint, kv_b, feats_row)


def on_device(node_feats, w_qkv, w_out, cotangent, block_neighbors, block_counts, global_blocks):
    feats = node_feats[0]
    cot = cotangent[0]
    y = lax.axis_index("y")
    neighbors = lax.dynamic_slice_in_dim(block_neighbors[0], y * QBLK, QBLK, 0)
    counts = lax.dynamic_slice_in_dim(block_counts[0], y * QBLK, QBLK, 0)
    table = jnp.concatenate([jnp.broadcast_to(global_blocks[0][None], (QBLK, NGLOB)), neighbors], axis=1).reshape(-1)
    place = jnp.arange(QBLK, dtype=jnp.int32)
    key = counts * QBLK + place
    rank = jnp.sum((key[None, :] < key[:, None]).astype(jnp.int32), axis=1)
    order = jnp.sum(jnp.where(rank[None, :] == place[:, None], place[None, :], 0), axis=1)
    y_arr = y.reshape(1).astype(jnp.int32)

    kv = project_kv(feats, w_qkv)
    qg = project_qg(feats, cot, w_qkv, w_out)
    kv_row = [gather_row(v) for v in split_heads(swap(kv, "z"))]
    qg_row = [swap(v, "z").reshape(ROW, 128) for v in qg]
    feats_late = hold(feats, qg_row[0])
    feats_row = lax.all_gather(feats_late, "z", axis=0, tiled=True)
    od_a, *kv_a = attend(table, counts, order, y_arr, kv_row[0], qg_row[0], feats_late)
    to_nodes = lambda v: swap(v, "z")
    (od_a_late,) = gate([od_a], [qg_row[1]])
    od_nodes_a = to_nodes(od_a_late)
    parts_a = send_row(*kv_a)
    late = attend(table, counts, order, y_arr, kv_row[1], qg_row[1], od_a_late)
    od_b, *kv_b = gate(late, parts_a[1:] + [od_nodes_a])
    parts_b = send_row(*kv_b)
    joint = sum_join(parts_a, od_b)
    joint_nodes = swap(joint, "z")
    sum_b = sum_parts(parts_b, (joint_nodes,))
    kv_nodes_b = to_nodes(sum_b)
    attn_update = project_out(od_nodes_a, joint_nodes, w_out)
    grad_nodes = node_grads(od_nodes_a, joint_nodes, kv_nodes_b, w_qkv)

    share = weight_share(od_a_late, od_b, joint, sum_b, feats_row)
    d = share.shape[0]
    share = share.reshape(4, 2, d // 8, 384)
    c = lax.axis_index("c")
    mine, theirs = (lax.dynamic_index_in_dim(share, k, 1, keepdims=False) for k in (c, 1 - c))
    theirs = lax.ppermute(theirs, "c", [(0, 1), (1, 0)])
    share = sum_parts([v.reshape(d // 2, 384) for v in (mine, theirs)], (kv_nodes_b,))
    share = share.reshape(16, d // 32, 384)
    share = jnp.sum(swap(share, ("x", "y")).astype(f32), axis=0)
    share = gate([share.reshape(ZS, d // 256, 384)], [attn_update, grad_nodes])[0]
    grad_weights = spread(swap(share, "z"))
    return attn_update[None], grad_nodes[None], grad_weights


def solution(mesh):
    fine = Mesh(np.asarray(mesh.devices).reshape(4, 2, YS, ZS), ("x", "c", "y", "z"))
    dp, seq = ("x", "c"), ("y", "z")
    in_specs = (P(dp, seq, None), P(), P(), P(dp, seq, None), P(dp, None, None), P(dp, None), P(dp, None))
    out_specs = (P(dp, seq, None), P(dp, seq, None), P(dp + seq, None))
    return jax.shard_map(on_device, mesh=fine, in_specs=in_specs, out_specs=out_specs, check_vma=False)
```

```python
import functools
import math

import jax
import jax.numpy as jnp
import numpy as np
from jax import lax
from jax.experimental import pallas as pl
from jax.experimental.pallas import tpu as pltpu
from jax.sharding import Mesh
from jax.sharding import PartitionSpec as P

H = 16
HD = 64
BLOCK = 128
MAXNB = 8
NGLOB = 4
SLOTS = MAXNB + NGLOB
YS = 4
ZS = 8
NODE_DEV = 256
ROW = NODE_DEV * ZS
QBLK = ROW // BLOCK
NODES = ROW * YS
TURNED = (ZS, 2 * HD, NODE_DEV)
PIECES = YS * ZS
SCALE = HD**-0.5
LOG2E = math.log2(math.e)
MASKED = -3.0e38
VMEM = pltpu.CompilerParams(vmem_limit_bytes=60 * 1024 * 1024)

bf16 = jnp.bfloat16
f32 = jnp.float32


def low_half(shape):
    return lax.broadcasted_iota(jnp.int32, shape, 1) < HD


def pair_up(first, second):
    low = low_half(first.shape)
    return (
        jnp.where(low, first, pltpu.roll(second, HD, 1)),
        jnp.where(low, pltpu.roll(first, HD, 1), second),
    )


def pair_rows(first, second):
    return (
        jnp.concatenate([first[:HD], second[:HD]], axis=0),
        jnp.concatenate([first[HD:], second[HD:]], axis=0),
    )


def nt(a, b):
    return lax.dot_general(a, b, (((1,), (1,)), ((), ())), preferred_element_type=f32)


def nn(a, b):
    return lax.dot_general(a, b, (((1,), (0,)), ((), ())), preferred_element_type=f32)


def put_pairs(first, second, a_ref, b_ref):
    for u in (0, 1):
        cols = slice(u * 128, (u + 1) * 128)
        a, b = pair_up(first[:, cols], second[:, cols])
        a_ref[u] = a.astype(bf16)
        b_ref[u] = b.astype(bf16)


def kv_kernel(f_ref, wk_ref, wv_ref, o_ref):
    k = nn(f_ref[...], wk_ref[...])
    v = nn(f_ref[...], wv_ref[...])
    for u in (0, 1):
        cols = slice(u * 128, (u + 1) * 128)
        a, b = pair_rows(k[:, cols].T, v[:, cols].T)
        o_ref[u, :128, :] = a.astype(bf16)
        o_ref[u, 128:, :] = b.astype(bf16)


def split_kernel(x_ref, a_ref, b_ref):
    a_ref[...] = x_ref[:, :128, :]
    b_ref[...] = x_ref[:, 128:, :]


def split_heads(both):
    return pl.pallas_call(
        split_kernel,
        grid=(2,),
        in_specs=[pl.BlockSpec((ZS // 2, 256, NODE_DEV), lambda i: (i, 0, 0))],
        out_specs=[pl.BlockSpec((ZS // 2, 128, NODE_DEV), lambda i: (i, 0, 0))] * 2,
        out_shape=[jax.ShapeDtypeStruct(TURNED, bf16)] * 2,
        compiler_params=VMEM,
        name="split_heads",
    )(both)


def qg_kernel(f_ref, c_ref, wq_ref, wo_ref, *refs):
    a_ref, b_ref, copy_ref = refs[-3:]

    @pl.when(pl.program_id(0) == 0)
    def _():
        copy_ref[...] = f_ref[...]

    put_pairs(nn(f_ref[...], wq_ref[...]), nt(c_ref[...], wo_ref[...]), a_ref, b_ref)


def whole(shape):
    return pl.BlockSpec(shape, lambda i: (0,) * len(shape))


def project_kv(feats, w_qkv):
    d = feats.shape[1]
    return pl.pallas_call(
        kv_kernel,
        grid=(ZS // 2,),
        in_specs=[
            whole((NODE_DEV, d)),
            pl.BlockSpec((d, 256), lambda i: (0, ZS // 2 + i)),
            pl.BlockSpec((d, 256), lambda i: (0, ZS + i)),
        ],
        out_specs=pl.BlockSpec((2, 256, NODE_DEV), lambda i: (i, 0, 0)),
        out_shape=jax.ShapeDtypeStruct((ZS, 256, NODE_DEV), bf16),
        compiler_params=VMEM,
        name="project_kv",
    )(feats, w_qkv, w_qkv)


def project_qg(feats, cot, w_qkv, w_out, before):
    d = feats.shape[1]
    out = jax.ShapeDtypeStruct((ZS, NODE_DEV, 128), bf16)
    tile = pl.BlockSpec((2, NODE_DEV, 128), lambda i: (i, 0, 0))
    return pl.pallas_call(
        qg_kernel,
        grid=(ZS // 2,),
        in_specs=[
            whole((NODE_DEV, d)),
            whole((NODE_DEV, d)),
            pl.BlockSpec((d, 256), lambda i: (0, i)),
            pl.BlockSpec((256, d), lambda i: (i, 0)),
        ]
        + [pl.BlockSpec(memory_space=pl.ANY)] * len(before),
        out_specs=[tile, tile, whole((NODE_DEV, d))],
        out_shape=[out, out, jax.ShapeDtypeStruct((NODE_DEV, d), bf16)],
        compiler_params=VMEM,
        name="project_qg",
    )(feats, cot, w_qkv, w_out, *before)


def attend_kernel(
    tab_ref, cnt_ref, order_ref, y_ref, own_ref, left_ref, right_ref, opp_ref, qg_ref, after_ref,
    od_ref, sum_own_ref, sum_right_ref, sum_left_ref, sum_opp_ref,
    kv_s, acc, sc0, sc1, xs0, xs1,
):
    y = y_ref[0]
    at = lambda step: lax.rem(y + step, YS) * ZS

    for step, ref in ((0, own_ref), (YS - 1, left_ref), (1, right_ref), (2, opp_ref)):
        kv_s[pl.ds(at(step), ZS)] = ref[...]

    @pl.loop(0, PIECES)
    def _(t):
        acc[t] = jnp.zeros((128, NODE_DEV), f32)

    def cols(block):
        return pl.ds(pl.multiple_of(lax.rem(block, 2) * BLOCK, BLOCK), BLOCK)

    def keys(ids, t):
        return jnp.concatenate([kv_s[lax.div(ids[2 * t + u], 2), :, cols(ids[2 * t + u])] for u in (0, 1)], axis=1)

    def score(i, pairs, sc):
        ids = [tab_ref[i * SLOTS + t] for t in range(2 * pairs)]
        rows = pl.ds(pl.multiple_of(i * BLOCK, BLOCK), BLOCK)
        qg = qg_ref[rows, :].astype(f32)
        low = low_half(qg.shape)
        zero = jnp.zeros_like(qg)
        wide32 = jnp.concatenate([jnp.where(low, qg, zero), jnp.where(low, zero, qg)], axis=0)
        wide = wide32.astype(bf16)
        for t in range(pairs):
            sc[:, t * 256 : (t + 1) * 256] = nn(wide, keys(ids, t))
        return i, ids, wide32.T.astype(bf16)

    def soften(i, pairs, sc, xs):
        width = pairs * 256
        count = cnt_ref[i]
        step = 16
        for r in range(BLOCK // step):
            s = sc[r * step : (r + 1) * step, :width]
            dp = sc[BLOCK + r * step : BLOCK + (r + 1) * step, :width]
            kept = [s[:, : (NGLOB + 1) * BLOCK]]
            for t in range(NGLOB + 1, 2 * pairs):
                kept.append(jnp.where(t - NGLOB < count, s[:, t * BLOCK : (t + 1) * BLOCK], MASKED))
            s = jnp.concatenate(kept, axis=1)
            e = jnp.exp2((s - jnp.max(s, axis=1, keepdims=True)) * (SCALE * LOG2E))
            p = e * (1.0 / jnp.sum(e, axis=1, keepdims=True))
            delta = jnp.sum(p * dp, axis=1, keepdims=True)
            ds = p * (dp - delta) * SCALE
            xs[r * step : (r + 1) * step, :width] = ds.astype(bf16)
            xs[BLOCK + r * step : BLOCK + (r + 1) * step, :width] = p.astype(bf16)

    def mix(state, pairs, xs):
        i, ids, wide_t = state
        every = jnp.concatenate([keys(ids, t) for t in range(pairs)], axis=1)
        mixed = nt(every, xs[:, : pairs * 256])
        od = jnp.concatenate([mixed[:HD, :BLOCK], mixed[HD:, BLOCK:]], axis=0)
        od_ref[lax.div(i, 2), :, cols(i)] = od.astype(bf16)
        for t in range(pairs):
            part = nn(wide_t, xs[:, t * 256 : (t + 1) * 256])
            for u in (0, 1):
                block = ids[2 * t + u]
                acc[lax.div(block, 2), :, cols(block)] += part[:, u * BLOCK : (u + 1) * BLOCK]

    def two_blocks(i, k, pairs):
        first = score(i, pairs, sc0)
        second = score(k, pairs, sc1)
        soften(i, pairs, sc0, xs0)
        mix(first, pairs, xs0)
        soften(k, pairs, sc1, xs1)
        mix(second, pairs, xs1)

    @pl.loop(0, QBLK // 2)
    def _(t):
        i, k = order_ref[2 * t], order_ref[2 * t + 1]
        pairs = NGLOB // 2 + (jnp.maximum(cnt_ref[i], cnt_ref[k]) + 1) // 2
        for v in range(NGLOB // 2 + 1, SLOTS // 2 + 1):
            pl.when(pairs == v)(functools.partial(two_blocks, i, k, v))

    for step, out in ((0, sum_own_ref), (1, sum_right_ref), (YS - 1, sum_left_ref), (2, sum_opp_ref)):
        start = at(step)

        @pl.loop(0, ZS)
        def _(t):
            out[t] = acc[start + t].astype(bf16)


def attend(table, counts, order, y, kv_parts, qg, after):
    vmem = pl.BlockSpec(memory_space=pltpu.VMEM)
    smem = pl.BlockSpec(memory_space=pltpu.SMEM)
    row = jax.ShapeDtypeStruct(TURNED, bf16)
    return pl.pallas_call(
        attend_kernel,
        in_specs=[smem] * 4 + [vmem] * 5 + [pl.BlockSpec(memory_space=pl.ANY)],
        out_specs=[vmem] * 5,
        out_shape=[row] * 5,
        scratch_shapes=[
            pltpu.VMEM((PIECES, 128, NODE_DEV), bf16),
            pltpu.VMEM((PIECES, 128, NODE_DEV), f32),
            pltpu.VMEM((256, SLOTS * BLOCK), f32),
            pltpu.VMEM((256, SLOTS * BLOCK), f32),
            pltpu.VMEM((256, SLOTS * BLOCK), bf16),
            pltpu.VMEM((256, SLOTS * BLOCK), bf16),
        ],
        compiler_params=VMEM,
        cost_estimate=pl.CostEstimate(
            flops=26 * 10**9, bytes_accessed=6 << 20, transcendentals=0
        ),
        name="attend",
    )(table, counts, order, y, *kv_parts, qg, after)


def turn(tiles):
    return jnp.concatenate(tiles, axis=0).astype(f32).T.astype(bf16)


def out_kernel(a_ref, b_ref, wo_ref, o_ref, total):
    step = pl.program_id(0)

    @pl.when(step == 0)
    def _():
        total[...] = jnp.zeros_like(total)

    att = [pair_rows(a_ref[u], b_ref[u])[1] for u in (0, 1)]
    total[...] += nn(turn(att), wo_ref[...])

    @pl.when(step == pl.num_programs(0) - 1)
    def _():
        o_ref[...] = total[...].astype(bf16)


SECOND = pl.BlockSpec((2, 128, NODE_DEV), lambda i: (i, 1, 0))


def project_out(od_a, joint, w_out):
    d = w_out.shape[1]
    tile = pl.BlockSpec((2, 128, NODE_DEV), lambda i: (i, 0, 0))
    return pl.pallas_call(
        out_kernel,
        grid=(ZS // 2,),
        in_specs=[tile, SECOND, pl.BlockSpec((256, d), lambda i: (i, 0))],
        out_specs=whole((NODE_DEV, d)),
        out_shape=jax.ShapeDtypeStruct((NODE_DEV, d), bf16),
        scratch_shapes=[pltpu.VMEM((NODE_DEV, d), f32)],
        compiler_params=VMEM,
        name="project_out",
    )(od_a, joint, w_out)


def nodes_kernel(oa_ref, ob_ref, ka_ref, kb_ref, wq_ref, wk_ref, wv_ref, o_ref, total):
    step = pl.program_id(0)

    @pl.when(step == 0)
    def _():
        total[...] = jnp.zeros_like(total)

    dq, dk, dv = [], [], []
    for u in (0, 1):
        dq.append(pair_rows(oa_ref[u], ob_ref[u])[0])
        k, v = pair_rows(ka_ref[u], kb_ref[u])
        dk.append(k)
        dv.append(v)
    add = nt(turn(dq), wq_ref[...])
    add += nt(turn(dk), wk_ref[...])
    add += nt(turn(dv), wv_ref[...])
    total[...] += add

    @pl.when(step == pl.num_programs(0) - 1)
    def _():
        o_ref[...] = total[...].astype(bf16)


def node_grads(od_a, joint, kv_b, w_qkv):
    d = w_qkv.shape[0]
    tile = pl.BlockSpec((2, 128, NODE_DEV), lambda i: (i, 0, 0))
    steps = ZS // 2
    return pl.pallas_call(
        nodes_kernel,
        grid=(steps,),
        in_specs=[tile, SECOND, tile, tile]
        + [pl.BlockSpec((d, 256), functools.partial(lambda i, third: (0, third * steps + i), third=k)) for k in range(3)],
        out_specs=whole((NODE_DEV, d)),
        out_shape=jax.ShapeDtypeStruct((NODE_DEV, d), bf16),
        scratch_shapes=[pltpu.VMEM((NODE_DEV, d), f32)],
        compiler_params=VMEM,
        name="node_grads",
    )(od_a, joint, joint, kv_b, w_qkv, w_qkv, w_qkv)


def spread_kernel(x_ref, *refs):
    o_ref = refs[-1]
    parts = x_ref[...].astype(f32).reshape(x_ref.shape[0] // ZS, ZS, *x_ref.shape[1:])
    total = jnp.sum(parts, axis=0)
    for z in range(ZS):
        for third in range(3):
            cols = third * H * HD + z * 128
            o_ref[:, cols : cols + 128] = total[z, :, third * 128 : (third + 1) * 128]


def spread(share, after):
    vmem = pl.BlockSpec(memory_space=pltpu.VMEM)
    return pl.pallas_call(
        spread_kernel,
        in_specs=[vmem] + [pl.BlockSpec(memory_space=pl.ANY)] * len(after),
        out_specs=vmem,
        out_shape=jax.ShapeDtypeStruct((share.shape[1], 3 * H * HD), f32),
        compiler_params=VMEM,
        name="spread",
    )(share, *after)


def swap(values, axis):
    return lax.all_to_all(values, axis, split_axis=0, concat_axis=0, tiled=True)


RIGHT = [(i, (i + 1) % YS) for i in range(YS)]
LEFT = [(i, (i - 1) % YS) for i in range(YS)]
OPPOSITE = [(i, (i + 2) % YS) for i in range(YS)]


def gather_row(own):
    return own, lax.ppermute(own, "y", RIGHT), lax.ppermute(own, "y", LEFT), lax.ppermute(own, "y", OPPOSITE)


def sum_kernel(count, *refs):
    parts = (r[...].astype(f32) for r in refs[:count])
    refs[-1][...] = sum(parts).astype(bf16)


def sum_parts(parts, after):
    shape = parts[0].shape
    tile = pl.BlockSpec((shape[0] // 2, *shape[1:]), lambda i: (i,) + (0,) * (len(shape) - 1))
    return pl.pallas_call(
        functools.partial(sum_kernel, len(parts)),
        grid=(2,),
        in_specs=[tile] * len(parts) + [pl.BlockSpec(memory_space=pl.ANY)] * len(after),
        out_specs=tile,
        out_shape=jax.ShapeDtypeStruct(shape, bf16),
        compiler_params=VMEM,
        name="sum_parts",
    )(*parts, *after)


def sum_join_kernel(a_ref, b_ref, c_ref, d_ref, od_ref, o_ref):
    o_ref[:, :128, :] = sum(r[...].astype(f32) for r in (a_ref, b_ref, c_ref, d_ref)).astype(bf16)
    o_ref[:, 128:, :] = od_ref[...]


def sum_join(parts, od):
    tile = pl.BlockSpec((ZS // 2, 128, NODE_DEV), lambda i: (i, 0, 0))
    return pl.pallas_call(
        sum_join_kernel,
        grid=(2,),
        in_specs=[tile] * 5,
        out_specs=pl.BlockSpec((ZS // 2, 256, NODE_DEV), lambda i: (i, 0, 0)),
        out_shape=jax.ShapeDtypeStruct((ZS, 256, NODE_DEV), bf16),
        compiler_params=VMEM,
        name="sum_join",
    )(*parts, od)


def send_row(own, to_right, to_left, opp):
    return [
        own,
        lax.ppermute(to_right, "y", RIGHT),
        lax.ppermute(to_left, "y", LEFT),
        lax.ppermute(opp, "y", OPPOSITE),
    ]


def gate_kernel(*refs):
    pass


def gate(values, after):
    anywhere = pl.BlockSpec(memory_space=pl.ANY)
    return pl.pallas_call(
        gate_kernel,
        in_specs=[anywhere] * (len(values) + len(after)),
        out_specs=[anywhere] * len(values),
        out_shape=[jax.ShapeDtypeStruct(v.shape, v.dtype) for v in values],
        input_output_aliases={i: i for i in range(len(values))},
        compiler_params=VMEM,
        name="gate",
    )(*values, *after)


def weight_kernel(oa_ref, ob_ref, ka_ref, kb_ref, f_ref, o_ref, grads):
    @pl.when(pl.program_id(0) == 0)
    def _():
        for t in range(ZS):
            nodes = slice(t * NODE_DEV, (t + 1) * NODE_DEV)
            dq = pair_rows(oa_ref[t], ob_ref[t])[0]
            dk, dv = pair_rows(ka_ref[t, :128, :], kb_ref[t])
            for k, part in enumerate((dq, dk, dv)):
                grads[k * 128 : (k + 1) * 128, nodes] = part

    o_ref[...] = nn(grads[...], f_ref[...]).T.astype(bf16)


def weight_share(od_a, od_b, joint, kv_b, feats_row):
    d = feats_row.shape[1]
    part = whole(TURNED)
    return pl.pallas_call(
        weight_kernel,
        grid=(d // 256,),
        in_specs=[part, part, whole(joint.shape), part, pl.BlockSpec((ROW, 256), lambda i: (0, i))],
        out_specs=pl.BlockSpec((256, 384), lambda i: (i, 0)),
        out_shape=jax.ShapeDtypeStruct((d, 384), bf16),
        scratch_shapes=[pltpu.VMEM((384, ROW), bf16)],
        compiler_params=VMEM,
        name="weight_share",
    )(od_a, od_b, joint, kv_b, feats_row)


def on_device(node_feats, w_qkv, w_out, cotangent, block_neighbors, block_counts, global_blocks):
    feats = node_feats[0]
    cot = cotangent[0]
    y = lax.axis_index("y")
    neighbors = lax.dynamic_slice_in_dim(block_neighbors[0], y * QBLK, QBLK, 0)
    counts = lax.dynamic_slice_in_dim(block_counts[0], y * QBLK, QBLK, 0)
    table = jnp.concatenate([jnp.broadcast_to(global_blocks[0][None], (QBLK, NGLOB)), neighbors], axis=1).reshape(-1)
    place = jnp.arange(QBLK, dtype=jnp.int32)
    key = counts * QBLK + place
    rank = jnp.sum((key[None, :] < key[:, None]).astype(jnp.int32), axis=1)
    order = jnp.sum(jnp.where(rank[None, :] == place[:, None], place[None, :], 0), axis=1)
    y_arr = y.reshape(1).astype(jnp.int32)

    kv = project_kv(feats, w_qkv)
    *qg, feats_copy = project_qg(feats, cot, w_qkv, w_out, (table, counts, order))
    kv_row = [gather_row(v) for v in split_heads(swap(kv, "z"))]
    qg_row = [swap(v, "z").reshape(ROW, 128) for v in qg]
    (feats_late,) = gate([feats_copy], [qg_row[0]])
    feats_row = lax.all_gather(feats_late, "z", axis=0, tiled=True)
    od_a, *kv_a = attend(table, counts, order, y_arr, kv_row[0], qg_row[0], feats_late)
    to_nodes = lambda v: swap(v, "z")
    (od_a_late,) = gate([od_a], [qg_row[1]])
    od_nodes_a = to_nodes(od_a_late)
    parts_a = send_row(*kv_a)
    late = attend(table, counts, order, y_arr, kv_row[1], qg_row[1], od_a_late)
    od_b, *kv_b = gate(late, parts_a[1:] + [od_nodes_a])
    parts_b = send_row(*kv_b)
    joint = sum_join(parts_a, od_b)
    joint_nodes = swap(joint, "z")
    sum_b = sum_parts(parts_b, (joint_nodes,))
    kv_nodes_b = to_nodes(sum_b)
    attn_update = project_out(od_nodes_a, joint_nodes, w_out)
    grad_nodes = node_grads(od_nodes_a, joint_nodes, kv_nodes_b, w_qkv)

    share = weight_share(od_a_late, od_b, joint, sum_b, feats_row)
    d = share.shape[0]
    share = share.reshape(4, 2, d // 8, 384)
    c = lax.axis_index("c")
    mine, theirs = (lax.dynamic_index_in_dim(share, k, 1, keepdims=False) for k in (c, 1 - c))
    theirs = lax.ppermute(theirs, "c", [(0, 1), (1, 0)])
    share = sum_parts([v.reshape(d // 2, 384) for v in (mine, theirs)], (kv_nodes_b,))
    share = swap(share.reshape(16 * ZS, d // 256, 384), ("x", "y", "z"))
    grad_weights = spread(share, (attn_update, grad_nodes))
    return attn_update[None], grad_nodes[None], grad_weights


def solution(mesh):
    fine = Mesh(np.asarray(mesh.devices).reshape(4, 2, YS, ZS), ("x", "c", "y", "z"))
    dp, seq = ("x", "c"), ("y", "z")
    in_specs = (P(dp, seq, None), P(), P(), P(dp, seq, None), P(dp, None, None), P(dp, None), P(dp, None))
    out_specs = (P(dp, seq, None), P(dp, seq, None), P(dp + seq, None))
    return jax.shard_map(on_device, mesh=fine, in_specs=in_specs, out_specs=out_specs, check_vma=False)
```

```python
import functools
import math

import jax
import jax.numpy as jnp
import numpy as np
from jax import lax
from jax.experimental import pallas as pl
from jax.experimental.pallas import tpu as pltpu
from jax.sharding import Mesh
from jax.sharding import PartitionSpec as P

H = 16
HD = 64
BLOCK = 128
MAXNB = 8
NGLOB = 4
SLOTS = MAXNB + NGLOB
YS = 4
ZS = 8
NODE_DEV = 256
ROW = NODE_DEV * ZS
QBLK = ROW // BLOCK
NODES = ROW * YS
TURNED = (ZS, 2 * HD, NODE_DEV)
PIECES = YS * ZS
SCALE = HD**-0.5
LOG2E = math.log2(math.e)
MASKED = -3.0e38
VMEM = pltpu.CompilerParams(vmem_limit_bytes=60 * 1024 * 1024)

bf16 = jnp.bfloat16
f32 = jnp.float32


def low_half(shape):
    return lax.broadcasted_iota(jnp.int32, shape, 1) < HD


def pair_up(first, second):
    low = low_half(first.shape)
    return (
        jnp.where(low, first, pltpu.roll(second, HD, 1)),
        jnp.where(low, pltpu.roll(first, HD, 1), second),
    )


def pair_rows(first, second):
    return (
        jnp.concatenate([first[:HD], second[:HD]], axis=0),
        jnp.concatenate([first[HD:], second[HD:]], axis=0),
    )


def nt(a, b):
    return lax.dot_general(a, b, (((1,), (1,)), ((), ())), preferred_element_type=f32)


def nn(a, b):
    return lax.dot_general(a, b, (((1,), (0,)), ((), ())), preferred_element_type=f32)


def put_pairs(first, second, a_ref, b_ref):
    for u in (0, 1):
        cols = slice(u * 128, (u + 1) * 128)
        a, b = pair_rows(first[:, cols].T, second[:, cols].T)
        a_ref[u] = a.astype(bf16)
        b_ref[u] = b.astype(bf16)


def kv_kernel(f_ref, wk_ref, wv_ref, a_ref, b_ref):
    put_pairs(nn(f_ref[...], wk_ref[...]), nn(f_ref[...], wv_ref[...]), a_ref, b_ref)


def first_kernel(x_ref, o_ref):
    o_ref[...] = x_ref[...]


def first_half(both):
    return pl.pallas_call(
        first_kernel,
        grid=(2,),
        in_specs=[pl.BlockSpec((ZS // 2, 128, NODE_DEV), lambda i: (i, 0, 0))],
        out_specs=pl.BlockSpec((ZS // 2, 128, NODE_DEV), lambda i: (i, 0, 0)),
        out_shape=jax.ShapeDtypeStruct(TURNED, bf16),
        compiler_params=VMEM,
        name="first_half",
    )(both)


def qg_kernel(f_ref, c_ref, wq_ref, wo_ref, kv_ref, *refs):
    joint_ref, b_ref, copy_ref = refs[-3:]

    @pl.when(pl.program_id(0) == 0)
    def _():
        copy_ref[...] = f_ref[...]

    joint_ref[:, :128, :] = kv_ref[...]
    put_pairs(nn(f_ref[...], wq_ref[...]), nt(c_ref[...], wo_ref[...]), joint_ref.at[:, 128:], b_ref)


def whole(shape):
    return pl.BlockSpec(shape, lambda i: (0,) * len(shape))


def project_kv(feats, w_qkv):
    d = feats.shape[1]
    return pl.pallas_call(
        kv_kernel,
        grid=(ZS // 2,),
        in_specs=[
            whole((NODE_DEV, d)),
            pl.BlockSpec((d, 256), lambda i: (0, ZS // 2 + i)),
            pl.BlockSpec((d, 256), lambda i: (0, ZS + i)),
        ],
        out_specs=[pl.BlockSpec((2, 128, NODE_DEV), lambda i: (i, 0, 0))] * 2,
        out_shape=[jax.ShapeDtypeStruct(TURNED, bf16)] * 2,
        compiler_params=VMEM,
        name="project_kv",
    )(feats, w_qkv, w_qkv)


def project_qg(feats, cot, w_qkv, w_out, kv, before):
    d = feats.shape[1]
    tile = pl.BlockSpec((2, 128, NODE_DEV), lambda i: (i, 0, 0))
    return pl.pallas_call(
        qg_kernel,
        grid=(ZS // 2,),
        in_specs=[
            whole((NODE_DEV, d)),
            whole((NODE_DEV, d)),
            pl.BlockSpec((d, 256), lambda i: (0, i)),
            pl.BlockSpec((256, d), lambda i: (i, 0)),
            tile,
        ]
        + [pl.BlockSpec(memory_space=pl.ANY)] * len(before),
        out_specs=[pl.BlockSpec((2, 256, NODE_DEV), lambda i: (i, 0, 0)), tile, whole((NODE_DEV, d))],
        out_shape=[
            jax.ShapeDtypeStruct((ZS, 256, NODE_DEV), bf16),
            jax.ShapeDtypeStruct(TURNED, bf16),
            jax.ShapeDtypeStruct((NODE_DEV, d), bf16),
        ],
        compiler_params=VMEM,
        name="project_qg",
    )(feats, cot, w_qkv, w_out, kv, *before)


def attend_kernel(
    skip, tab_ref, cnt_ref, order_ref, y_ref, own_ref, left_ref, right_ref, opp_ref, qg_ref, after_ref,
    od_ref, sum_own_ref, sum_right_ref, sum_left_ref, sum_opp_ref,
    kv_s, acc, sc0, sc1, xs0, xs1,
):
    y = y_ref[0]
    at = lambda step: lax.rem(y + step, YS) * ZS

    for step, ref in ((0, own_ref), (YS - 1, left_ref), (1, right_ref), (2, opp_ref)):
        kv_s[pl.ds(at(step), ZS)] = ref[...]

    @pl.loop(0, PIECES)
    def _(t):
        acc[t] = jnp.zeros((128, NODE_DEV), f32)

    def cols(block):
        return pl.ds(pl.multiple_of(lax.rem(block, 2) * BLOCK, BLOCK), BLOCK)

    def keys(ids, t):
        return jnp.concatenate([kv_s[lax.div(ids[2 * t + u], 2), :, cols(ids[2 * t + u])] for u in (0, 1)], axis=1)

    def score(i, pairs, sc):
        ids = [tab_ref[i * SLOTS + t] for t in range(2 * pairs)]
        qg = qg_ref[lax.div(i, 2), skip : skip + 128, cols(i)].astype(f32)
        top = lax.broadcasted_iota(jnp.int32, qg.shape, 0) < HD
        zero = jnp.zeros_like(qg)
        wide_t = jnp.concatenate([jnp.where(top, qg, zero), jnp.where(top, zero, qg)], axis=1)
        wide = wide_t.T.astype(bf16)
        for t in range(pairs):
            sc[:, t * 256 : (t + 1) * 256] = nn(wide, keys(ids, t))
        return i, ids, wide_t.astype(bf16)

    def soften(i, pairs, sc, xs):
        width = pairs * 256
        count = cnt_ref[i]
        step = 16
        for r in range(BLOCK // step):
            s = sc[r * step : (r + 1) * step, :width]
            dp = sc[BLOCK + r * step : BLOCK + (r + 1) * step, :width]
            kept = [s[:, : (NGLOB + 1) * BLOCK]]
            for t in range(NGLOB + 1, 2 * pairs):
                kept.append(jnp.where(t - NGLOB < count, s[:, t * BLOCK : (t + 1) * BLOCK], MASKED))
            s = jnp.concatenate(kept, axis=1)
            e = jnp.exp2((s - jnp.max(s, axis=1, keepdims=True)) * (SCALE * LOG2E))
            p = e * (1.0 / jnp.sum(e, axis=1, keepdims=True))
            delta = jnp.sum(p * dp, axis=1, keepdims=True)
            ds = p * (dp - delta) * SCALE
            xs[r * step : (r + 1) * step, :width] = ds.astype(bf16)
            xs[BLOCK + r * step : BLOCK + (r + 1) * step, :width] = p.astype(bf16)

    def mix(state, pairs, xs):
        i, ids, wide_t = state
        every = jnp.concatenate([keys(ids, t) for t in range(pairs)], axis=1)
        mixed = nt(every, xs[:, : pairs * 256])
        od = jnp.concatenate([mixed[:HD, :BLOCK], mixed[HD:, BLOCK:]], axis=0)
        od_ref[lax.div(i, 2), :, cols(i)] = od.astype(bf16)
        for t in range(pairs):
            part = nn(wide_t, xs[:, t * 256 : (t + 1) * 256])
            for u in (0, 1):
                block = ids[2 * t + u]
                acc[lax.div(block, 2), :, cols(block)] += part[:, u * BLOCK : (u + 1) * BLOCK]

    def two_blocks(i, k, pairs):
        first = score(i, pairs, sc0)
        second = score(k, pairs, sc1)
        soften(i, pairs, sc0, xs0)
        mix(first, pairs, xs0)
        soften(k, pairs, sc1, xs1)
        mix(second, pairs, xs1)

    @pl.loop(0, QBLK // 2)
    def _(t):
        i, k = order_ref[2 * t], order_ref[2 * t + 1]
        pairs = NGLOB // 2 + (jnp.maximum(cnt_ref[i], cnt_ref[k]) + 1) // 2
        for v in range(NGLOB // 2 + 1, SLOTS // 2 + 1):
            pl.when(pairs == v)(functools.partial(two_blocks, i, k, v))

    for step, out in ((0, sum_own_ref), (1, sum_right_ref), (YS - 1, sum_left_ref), (2, sum_opp_ref)):
        start = at(step)

        @pl.loop(0, ZS)
        def _(t):
            out[t] = acc[start + t].astype(bf16)


def attend(table, counts, order, y, kv_parts, qg, after):
    vmem = pl.BlockSpec(memory_space=pltpu.VMEM)
    smem = pl.BlockSpec(memory_space=pltpu.SMEM)
    row = jax.ShapeDtypeStruct(TURNED, bf16)
    return pl.pallas_call(
        functools.partial(attend_kernel, qg.shape[1] - 128),
        in_specs=[smem] * 4 + [vmem] * 5 + [pl.BlockSpec(memory_space=pl.ANY)],
        out_specs=[vmem] * 5,
        out_shape=[row] * 5,
        scratch_shapes=[
            pltpu.VMEM((PIECES, 128, NODE_DEV), bf16),
            pltpu.VMEM((PIECES, 128, NODE_DEV), f32),
            pltpu.VMEM((256, SLOTS * BLOCK), f32),
            pltpu.VMEM((256, SLOTS * BLOCK), f32),
            pltpu.VMEM((256, SLOTS * BLOCK), bf16),
            pltpu.VMEM((256, SLOTS * BLOCK), bf16),
        ],
        compiler_params=VMEM,
        cost_estimate=pl.CostEstimate(
            flops=26 * 10**9, bytes_accessed=6 << 20, transcendentals=0
        ),
        name="attend",
    )(table, counts, order, y, *kv_parts, qg, after)


def turn(tiles):
    return jnp.concatenate(tiles, axis=0).astype(f32).T.astype(bf16)


def out_kernel(a_ref, b_ref, wo_ref, o_ref, total):
    step = pl.program_id(0)

    @pl.when(step == 0)
    def _():
        total[...] = jnp.zeros_like(total)

    att = [pair_rows(a_ref[u], b_ref[u])[1] for u in (0, 1)]
    total[...] += nn(turn(att), wo_ref[...])

    @pl.when(step == pl.num_programs(0) - 1)
    def _():
        o_ref[...] = total[...].astype(bf16)


SECOND = pl.BlockSpec((2, 128, NODE_DEV), lambda i: (i, 1, 0))


def project_out(od_a, joint, w_out):
    d = w_out.shape[1]
    tile = pl.BlockSpec((2, 128, NODE_DEV), lambda i: (i, 0, 0))
    return pl.pallas_call(
        out_kernel,
        grid=(ZS // 2,),
        in_specs=[tile, SECOND, pl.BlockSpec((256, d), lambda i: (i, 0))],
        out_specs=whole((NODE_DEV, d)),
        out_shape=jax.ShapeDtypeStruct((NODE_DEV, d), bf16),
        scratch_shapes=[pltpu.VMEM((NODE_DEV, d), f32)],
        compiler_params=VMEM,
        name="project_out",
    )(od_a, joint, w_out)


def nodes_kernel(oa_ref, ob_ref, ka_ref, kb_ref, wq_ref, wk_ref, wv_ref, o_ref, total):
    step = pl.program_id(0)

    @pl.when(step == 0)
    def _():
        total[...] = jnp.zeros_like(total)

    dq, dk, dv = [], [], []
    for u in (0, 1):
        dq.append(pair_rows(oa_ref[u], ob_ref[u])[0])
        k, v = pair_rows(ka_ref[u], kb_ref[u])
        dk.append(k)
        dv.append(v)
    add = nt(turn(dq), wq_ref[...])
    add += nt(turn(dk), wk_ref[...])
    add += nt(turn(dv), wv_ref[...])
    total[...] += add

    @pl.when(step == pl.num_programs(0) - 1)
    def _():
        o_ref[...] = total[...].astype(bf16)


def node_grads(od_a, joint, kv_b, w_qkv):
    d = w_qkv.shape[0]
    tile = pl.BlockSpec((2, 128, NODE_DEV), lambda i: (i, 0, 0))
    steps = ZS // 2
    return pl.pallas_call(
        nodes_kernel,
        grid=(steps,),
        in_specs=[tile, SECOND, tile, tile]
        + [pl.BlockSpec((d, 256), functools.partial(lambda i, third: (0, third * steps + i), third=k)) for k in range(3)],
        out_specs=whole((NODE_DEV, d)),
        out_shape=jax.ShapeDtypeStruct((NODE_DEV, d), bf16),
        scratch_shapes=[pltpu.VMEM((NODE_DEV, d), f32)],
        compiler_params=VMEM,
        name="node_grads",
    )(od_a, joint, joint, kv_b, w_qkv, w_qkv, w_qkv)


def spread_kernel(x_ref, *refs):
    o_ref = refs[-1]
    parts = x_ref[...].astype(f32).reshape(x_ref.shape[0] // ZS, ZS, *x_ref.shape[1:])
    total = jnp.sum(parts, axis=0)
    for z in range(ZS):
        for third in range(3):
            cols = third * H * HD + z * 128
            o_ref[:, cols : cols + 128] = total[z, :, third * 128 : (third + 1) * 128]


def spread(share, after):
    vmem = pl.BlockSpec(memory_space=pltpu.VMEM)
    return pl.pallas_call(
        spread_kernel,
        in_specs=[vmem] + [pl.BlockSpec(memory_space=pl.ANY)] * len(after),
        out_specs=vmem,
        out_shape=jax.ShapeDtypeStruct((share.shape[1], 3 * H * HD), f32),
        compiler_params=VMEM,
        name="spread",
    )(share, *after)


def swap(values, axis):
    return lax.all_to_all(values, axis, split_axis=0, concat_axis=0, tiled=True)


RIGHT = [(i, (i + 1) % YS) for i in range(YS)]
LEFT = [(i, (i - 1) % YS) for i in range(YS)]
OPPOSITE = [(i, (i + 2) % YS) for i in range(YS)]


def gather_row(own):
    return own, lax.ppermute(own, "y", RIGHT), lax.ppermute(own, "y", LEFT), lax.ppermute(own, "y", OPPOSITE)


def sum_kernel(count, *refs):
    parts = (r[...].astype(f32) for r in refs[:count])
    refs[-1][...] = sum(parts).astype(bf16)


def sum_parts(parts, after):
    shape = parts[0].shape
    tile = pl.BlockSpec((shape[0] // 2, *shape[1:]), lambda i: (i,) + (0,) * (len(shape) - 1))
    return pl.pallas_call(
        functools.partial(sum_kernel, len(parts)),
        grid=(2,),
        in_specs=[tile] * len(parts) + [pl.BlockSpec(memory_space=pl.ANY)] * len(after),
        out_specs=tile,
        out_shape=jax.ShapeDtypeStruct(shape, bf16),
        compiler_params=VMEM,
        name="sum_parts",
    )(*parts, *after)


def sum_join_kernel(a_ref, b_ref, c_ref, d_ref, od_ref, o_ref):
    o_ref[:, :128, :] = sum(r[...].astype(f32) for r in (a_ref, b_ref, c_ref, d_ref)).astype(bf16)
    o_ref[:, 128:, :] = od_ref[...]


def sum_join(parts, od):
    tile = pl.BlockSpec((ZS // 2, 128, NODE_DEV), lambda i: (i, 0, 0))
    return pl.pallas_call(
        sum_join_kernel,
        grid=(2,),
        in_specs=[tile] * 5,
        out_specs=pl.BlockSpec((ZS // 2, 256, NODE_DEV), lambda i: (i, 0, 0)),
        out_shape=jax.ShapeDtypeStruct((ZS, 256, NODE_DEV), bf16),
        compiler_params=VMEM,
        name="sum_join",
    )(*parts, od)


def send_row(own, to_right, to_left, opp):
    return [
        own,
        lax.ppermute(to_right, "y", RIGHT),
        lax.ppermute(to_left, "y", LEFT),
        lax.ppermute(opp, "y", OPPOSITE),
    ]


def gate_kernel(*refs):
    pass


def gate(values, after):
    anywhere = pl.BlockSpec(memory_space=pl.ANY)
    return pl.pallas_call(
        gate_kernel,
        in_specs=[anywhere] * (len(values) + len(after)),
        out_specs=[anywhere] * len(values),
        out_shape=[jax.ShapeDtypeStruct(v.shape, v.dtype) for v in values],
        input_output_aliases={i: i for i in range(len(values))},
        compiler_params=VMEM,
        name="gate",
    )(*values, *after)


def weight_kernel(c_ref, oa_ref, ob_ref, ka_ref, kb_ref, f_ref, mine_ref, theirs_ref, grads):
    @pl.when(pl.program_id(0) == 0)
    def _():
        for t in range(ZS):
            nodes = slice(t * NODE_DEV, (t + 1) * NODE_DEV)
            dq = pair_rows(oa_ref[t], ob_ref[t])[0]
            dk, dv = pair_rows(ka_ref[t, :128, :], kb_ref[t])
            for k, part in enumerate((dq, dk, dv)):
                grads[k * 128 : (k + 1) * 128, nodes] = part

    both = nn(grads[...], f_ref[...]).T.astype(bf16)
    first = c_ref[0] == 0
    mine_ref[...] = jnp.where(first, both[:128], both[128:])
    theirs_ref[...] = jnp.where(first, both[128:], both[:128])


def weight_share(c, od_a, od_b, joint, kv_b, feats_row):
    d = feats_row.shape[1]
    part = whole(TURNED)
    return pl.pallas_call(
        weight_kernel,
        grid=(d // 256,),
        in_specs=[pl.BlockSpec(memory_space=pltpu.SMEM), part, part, whole(joint.shape), part, pl.BlockSpec((ROW, 256), lambda i: (0, i))],
        out_specs=[pl.BlockSpec((128, 384), lambda i: (i, 0))] * 2,
        out_shape=[jax.ShapeDtypeStruct((d // 2, 384), bf16)] * 2,
        scratch_shapes=[pltpu.VMEM((384, ROW), bf16)],
        compiler_params=VMEM,
        name="weight_share",
    )(c, od_a, od_b, joint, kv_b, feats_row)


def on_device(node_feats, w_qkv, w_out, cotangent, block_neighbors, block_counts, global_blocks):
    feats = node_feats[0]
    cot = cotangent[0]
    y = lax.axis_index("y")
    neighbors = lax.dynamic_slice_in_dim(block_neighbors[0], y * QBLK, QBLK, 0)
    counts = lax.dynamic_slice_in_dim(block_counts[0], y * QBLK, QBLK, 0)
    table = jnp.concatenate([jnp.broadcast_to(global_blocks[0][None], (QBLK, NGLOB)), neighbors], axis=1).reshape(-1)
    place = jnp.arange(QBLK, dtype=jnp.int32)
    key = counts * QBLK + place
    rank = jnp.sum((key[None, :] < key[:, None]).astype(jnp.int32), axis=1)
    order = jnp.sum(jnp.where(rank[None, :] == place[:, None], place[None, :], 0), axis=1)
    y_arr = y.reshape(1).astype(jnp.int32)

    kv_a, kv_b = project_kv(feats, w_qkv)
    joint, qg_b, feats_copy = project_qg(feats, cot, w_qkv, w_out, kv_b, (table, counts, order))
    row_a = gather_row(swap(kv_a, "z"))
    joint_row = swap(joint, "z")
    row_b = gather_row(first_half(joint_row))
    (feats_late, qg_b) = gate([feats_copy, qg_b], [joint_row])
    qg_row_b = swap(qg_b, "z")
    feats_row = lax.all_gather(feats_late, "z", axis=0, tiled=True)
    od_a, *kv_a = attend(table, counts, order, y_arr, row_a, joint_row, feats_late)
    to_nodes = lambda v: swap(v, "z")
    (od_a_late,) = gate([od_a], [qg_row_b])
    od_nodes_a = to_nodes(od_a_late)
    parts_a = send_row(*kv_a)
    late = attend(table, counts, order, y_arr, row_b, qg_row_b, od_a_late)
    od_b, *kv_b = gate(late, parts_a[1:] + [od_nodes_a])
    parts_b = send_row(*kv_b)
    joint = sum_join(parts_a, od_b)
    joint_nodes = swap(joint, "z")
    sum_b = sum_parts(parts_b, (joint_nodes,))
    kv_nodes_b = to_nodes(sum_b)
    attn_update = project_out(od_nodes_a, joint_nodes, w_out)
    grad_nodes = node_grads(od_nodes_a, joint_nodes, kv_nodes_b, w_qkv)

    d = feats.shape[1]
    c_arr = lax.axis_index("c").reshape(1).astype(jnp.int32)
    mine, theirs = weight_share(c_arr, od_a_late, od_b, joint, sum_b, feats_row)
    theirs = lax.ppermute(theirs, "c", [(0, 1), (1, 0)])
    share = sum_parts([mine, theirs], ()).reshape(16 * ZS, d // 256, 384)
    (share,) = gate([share], [kv_nodes_b])
    share = swap(share, ("x", "y", "z"))
    grad_weights = spread(share, (attn_update, grad_nodes))
    return attn_update[None], grad_nodes[None], grad_weights


def solution(mesh):
    fine = Mesh(np.asarray(mesh.devices).reshape(4, 2, YS, ZS), ("x", "c", "y", "z"))
    dp, seq = ("x", "c"), ("y", "z")
    in_specs = (P(dp, seq, None), P(), P(), P(dp, seq, None), P(dp, None, None), P(dp, None), P(dp, None))
    out_specs = (P(dp, seq, None), P(dp, seq, None), P(dp + seq, None))
    return jax.shard_map(on_device, mesh=fine, in_specs=in_specs, out_specs=out_specs, check_vma=False)
```

```python
import functools
import math

import jax
import jax.numpy as jnp
import numpy as np
from jax import lax
from jax.experimental import pallas as pl
from jax.experimental.pallas import tpu as pltpu
from jax.sharding import Mesh
from jax.sharding import PartitionSpec as P

H = 16
HD = 64
BLOCK = 128
MAXNB = 8
NGLOB = 4
SLOTS = MAXNB + NGLOB
YS = 4
ZS = 8
NODE_DEV = 256
ROW = NODE_DEV * ZS
QBLK = ROW // BLOCK
NODES = ROW * YS
TURNED = (ZS, 2 * HD, NODE_DEV)
PIECES = YS * ZS
SCALE = HD**-0.5
LOG2E = math.log2(math.e)
MASKED = -3.0e38
VMEM = pltpu.CompilerParams(vmem_limit_bytes=60 * 1024 * 1024)

bf16 = jnp.bfloat16
f32 = jnp.float32


def low_half(shape):
    return lax.broadcasted_iota(jnp.int32, shape, 1) < HD


def pair_up(first, second):
    low = low_half(first.shape)
    return (
        jnp.where(low, first, pltpu.roll(second, HD, 1)),
        jnp.where(low, pltpu.roll(first, HD, 1), second),
    )


def pair_rows(first, second):
    return (
        jnp.concatenate([first[:HD], second[:HD]], axis=0),
        jnp.concatenate([first[HD:], second[HD:]], axis=0),
    )


def nt(a, b):
    return lax.dot_general(a, b, (((1,), (1,)), ((), ())), preferred_element_type=f32)


def nn(a, b):
    return lax.dot_general(a, b, (((1,), (0,)), ((), ())), preferred_element_type=f32)


def put_pairs(first, second, a_ref, b_ref):
    for u in (0, 1):
        cols = slice(u * 128, (u + 1) * 128)
        a, b = pair_rows(first[:, cols].T, second[:, cols].T)
        a_ref[u] = a.astype(bf16)
        b_ref[u] = b.astype(bf16)


def kv_kernel(f_ref, wk_ref, wv_ref, a_ref, b_ref):
    put_pairs(nn(f_ref[...], wk_ref[...]), nn(f_ref[...], wv_ref[...]), a_ref, b_ref)


def first_kernel(x_ref, o_ref):
    o_ref[...] = x_ref[...]


def first_half(both):
    return pl.pallas_call(
        first_kernel,
        grid=(2,),
        in_specs=[pl.BlockSpec((ZS // 2, 128, NODE_DEV), lambda i: (i, 0, 0))],
        out_specs=pl.BlockSpec((ZS // 2, 128, NODE_DEV), lambda i: (i, 0, 0)),
        out_shape=jax.ShapeDtypeStruct(TURNED, bf16),
        compiler_params=VMEM,
        name="first_half",
    )(both)


def qg_kernel(f_ref, c_ref, wq_ref, wo_ref, kv_ref, *refs):
    joint_ref, b_ref, copy_ref = refs[-3:]

    @pl.when(pl.program_id(0) == 0)
    def _():
        copy_ref[...] = f_ref[...]

    joint_ref[:, :128, :] = kv_ref[...]
    put_pairs(nn(f_ref[...], wq_ref[...]), nt(c_ref[...], wo_ref[...]), joint_ref.at[:, 128:], b_ref)


def whole(shape):
    return pl.BlockSpec(shape, lambda i: (0,) * len(shape))


def project_kv(feats, w_qkv):
    d = feats.shape[1]
    return pl.pallas_call(
        kv_kernel,
        grid=(ZS // 2,),
        in_specs=[
            whole((NODE_DEV, d)),
            pl.BlockSpec((d, 256), lambda i: (0, ZS // 2 + i)),
            pl.BlockSpec((d, 256), lambda i: (0, ZS + i)),
        ],
        out_specs=[pl.BlockSpec((2, 128, NODE_DEV), lambda i: (i, 0, 0))] * 2,
        out_shape=[jax.ShapeDtypeStruct(TURNED, bf16)] * 2,
        compiler_params=VMEM,
        name="project_kv",
    )(feats, w_qkv, w_qkv)


def project_qg(feats, cot, w_qkv, w_out, kv, before):
    d = feats.shape[1]
    tile = pl.BlockSpec((2, 128, NODE_DEV), lambda i: (i, 0, 0))
    return pl.pallas_call(
        qg_kernel,
        grid=(ZS // 2,),
        in_specs=[
            whole((NODE_DEV, d)),
            whole((NODE_DEV, d)),
            pl.BlockSpec((d, 256), lambda i: (0, i)),
            pl.BlockSpec((256, d), lambda i: (i, 0)),
            tile,
        ]
        + [pl.BlockSpec(memory_space=pl.ANY)] * len(before),
        out_specs=[pl.BlockSpec((2, 256, NODE_DEV), lambda i: (i, 0, 0)), tile, whole((NODE_DEV, d))],
        out_shape=[
            jax.ShapeDtypeStruct((ZS, 256, NODE_DEV), bf16),
            jax.ShapeDtypeStruct(TURNED, bf16),
            jax.ShapeDtypeStruct((NODE_DEV, d), bf16),
        ],
        compiler_params=VMEM,
        name="project_qg",
    )(feats, cot, w_qkv, w_out, kv, *before)


def attend_kernel(
    skip, tab_ref, cnt_ref, order_ref, y_ref, own_ref, left_ref, right_ref, opp_ref, qg_ref, after_ref,
    od_ref, sum_own_ref, sum_right_ref, sum_left_ref, sum_opp_ref,
    kv_s, acc, sc0, sc1, xs0, xs1,
):
    y = y_ref[0]
    at = lambda step: lax.rem(y + step, YS) * ZS

    for step, ref in ((0, own_ref), (YS - 1, left_ref), (1, right_ref), (2, opp_ref)):
        kv_s[pl.ds(at(step), ZS)] = ref[...]

    @pl.loop(0, PIECES)
    def _(t):
        acc[t] = jnp.zeros((128, NODE_DEV), f32)

    def cols(block):
        return pl.ds(pl.multiple_of(lax.rem(block, 2) * BLOCK, BLOCK), BLOCK)

    def keys(ids, t):
        return jnp.concatenate([kv_s[lax.div(ids[2 * t + u], 2), :, cols(ids[2 * t + u])] for u in (0, 1)], axis=1)

    def score(i, pairs, sc):
        ids = [tab_ref[i * SLOTS + t] for t in range(2 * pairs)]
        qg = qg_ref[lax.div(i, 2), skip : skip + 128, cols(i)].astype(f32)
        top = lax.broadcasted_iota(jnp.int32, qg.shape, 0) < HD
        zero = jnp.zeros_like(qg)
        wide_t = jnp.concatenate([jnp.where(top, qg, zero), jnp.where(top, zero, qg)], axis=1)
        wide = wide_t.T.astype(bf16)
        for t in range(pairs):
            sc[:, t * 256 : (t + 1) * 256] = nn(wide, keys(ids, t))
        return i, ids, wide_t.astype(bf16)

    def soften(i, pairs, sc, xs):
        width = pairs * 256
        count = cnt_ref[i]
        step = 16
        for r in range(BLOCK // step):
            s = sc[r * step : (r + 1) * step, :width]
            dp = sc[BLOCK + r * step : BLOCK + (r + 1) * step, :width]
            kept = [s[:, : (NGLOB + 1) * BLOCK]]
            for t in range(NGLOB + 1, 2 * pairs):
                kept.append(jnp.where(t - NGLOB < count, s[:, t * BLOCK : (t + 1) * BLOCK], MASKED))
            s = jnp.concatenate(kept, axis=1)
            e = jnp.exp2((s - jnp.max(s, axis=1, keepdims=True)) * (SCALE * LOG2E))
            p = e * (1.0 / jnp.sum(e, axis=1, keepdims=True))
            delta = jnp.sum(p * dp, axis=1, keepdims=True)
            ds = p * (dp - delta) * SCALE
            xs[r * step : (r + 1) * step, :width] = ds.astype(bf16)
            xs[BLOCK + r * step : BLOCK + (r + 1) * step, :width] = p.astype(bf16)

    def mix(state, pairs, xs):
        i, ids, wide_t = state
        every = jnp.concatenate([keys(ids, t) for t in range(pairs)], axis=1)
        mixed = nt(every, xs[:, : pairs * 256])
        od = jnp.concatenate([mixed[:HD, :BLOCK], mixed[HD:, BLOCK:]], axis=0)
        od_ref[lax.div(i, 2), :, cols(i)] = od.astype(bf16)
        for t in range(pairs):
            part = nn(wide_t, xs[:, t * 256 : (t + 1) * 256])
            for u in (0, 1):
                block = ids[2 * t + u]
                acc[lax.div(block, 2), :, cols(block)] += part[:, u * BLOCK : (u + 1) * BLOCK]

    def two_blocks(i, k, pairs):
        first = score(i, pairs, sc0)
        second = score(k, pairs, sc1)
        soften(i, pairs, sc0, xs0)
        mix(first, pairs, xs0)
        soften(k, pairs, sc1, xs1)
        mix(second, pairs, xs1)

    @pl.loop(0, QBLK // 2)
    def _(t):
        i, k = order_ref[2 * t], order_ref[2 * t + 1]
        pairs = NGLOB // 2 + (jnp.maximum(cnt_ref[i], cnt_ref[k]) + 1) // 2
        for v in range(NGLOB // 2 + 1, SLOTS // 2 + 1):
            pl.when(pairs == v)(functools.partial(two_blocks, i, k, v))

    for step, out in ((0, sum_own_ref), (1, sum_right_ref), (YS - 1, sum_left_ref), (2, sum_opp_ref)):
        start = at(step)

        @pl.loop(0, ZS)
        def _(t):
            out[t] = acc[start + t].astype(bf16)


def attend(table, counts, order, y, kv_parts, qg, after):
    vmem = pl.BlockSpec(memory_space=pltpu.VMEM)
    smem = pl.BlockSpec(memory_space=pltpu.SMEM)
    row = jax.ShapeDtypeStruct(TURNED, bf16)
    return pl.pallas_call(
        functools.partial(attend_kernel, qg.shape[1] - 128),
        in_specs=[smem] * 4 + [vmem] * 5 + [pl.BlockSpec(memory_space=pl.ANY)],
        out_specs=[vmem] * 5,
        out_shape=[row] * 5,
        scratch_shapes=[
            pltpu.VMEM((PIECES, 128, NODE_DEV), bf16),
            pltpu.VMEM((PIECES, 128, NODE_DEV), f32),
            pltpu.VMEM((256, SLOTS * BLOCK), f32),
            pltpu.VMEM((256, SLOTS * BLOCK), f32),
            pltpu.VMEM((256, SLOTS * BLOCK), bf16),
            pltpu.VMEM((256, SLOTS * BLOCK), bf16),
        ],
        compiler_params=VMEM,
        cost_estimate=pl.CostEstimate(
            flops=26 * 10**9, bytes_accessed=6 << 20, transcendentals=0
        ),
        name="attend",
    )(table, counts, order, y, *kv_parts, qg, after)


def turn(tiles):
    return jnp.concatenate(tiles, axis=0).astype(f32).T.astype(bf16)


def out_kernel(a_ref, b_ref, wo_ref, o_ref, total):
    step = pl.program_id(0)

    @pl.when(step == 0)
    def _():
        total[...] = jnp.zeros_like(total)

    att = [pair_rows(a_ref[u], b_ref[u])[1] for u in (0, 1)]
    total[...] += nn(turn(att), wo_ref[...])

    @pl.when(step == pl.num_programs(0) - 1)
    def _():
        o_ref[...] = total[...].astype(bf16)


SECOND = pl.BlockSpec((2, 128, NODE_DEV), lambda i: (i, 1, 0))


def project_out(od_a, joint, w_out):
    d = w_out.shape[1]
    tile = pl.BlockSpec((2, 128, NODE_DEV), lambda i: (i, 0, 0))
    return pl.pallas_call(
        out_kernel,
        grid=(ZS // 2,),
        in_specs=[tile, SECOND, pl.BlockSpec((256, d), lambda i: (i, 0))],
        out_specs=whole((NODE_DEV, d)),
        out_shape=jax.ShapeDtypeStruct((NODE_DEV, d), bf16),
        scratch_shapes=[pltpu.VMEM((NODE_DEV, d), f32)],
        compiler_params=VMEM,
        name="project_out",
    )(od_a, joint, w_out)


def nodes_kernel(oa_ref, ob_ref, ka_ref, kb_ref, wq_ref, wk_ref, wv_ref, o_ref, total):
    step = pl.program_id(0)

    @pl.when(step == 0)
    def _():
        total[...] = jnp.zeros_like(total)

    dq, dk, dv = [], [], []
    for u in (0, 1):
        dq.append(pair_rows(oa_ref[u], ob_ref[u])[0])
        k, v = pair_rows(ka_ref[u], kb_ref[u])
        dk.append(k)
        dv.append(v)
    add = nt(turn(dq), wq_ref[...])
    add += nt(turn(dk), wk_ref[...])
    add += nt(turn(dv), wv_ref[...])
    total[...] += add

    @pl.when(step == pl.num_programs(0) - 1)
    def _():
        o_ref[...] = total[...].astype(bf16)


def node_grads(od_a, joint, kv_b, w_qkv):
    d = w_qkv.shape[0]
    tile = pl.BlockSpec((2, 128, NODE_DEV), lambda i: (i, 0, 0))
    steps = ZS // 2
    return pl.pallas_call(
        nodes_kernel,
        grid=(steps,),
        in_specs=[tile, SECOND, tile, tile]
        + [pl.BlockSpec((d, 256), functools.partial(lambda i, third: (0, third * steps + i), third=k)) for k in range(3)],
        out_specs=whole((NODE_DEV, d)),
        out_shape=jax.ShapeDtypeStruct((NODE_DEV, d), bf16),
        scratch_shapes=[pltpu.VMEM((NODE_DEV, d), f32)],
        compiler_params=VMEM,
        name="node_grads",
    )(od_a, joint, joint, kv_b, w_qkv, w_qkv, w_qkv)


def rows_kernel(x_ref, *refs):
    o_ref = refs[-1]
    total = jnp.sum(x_ref[...].astype(f32), axis=0)
    step = total.shape[0] // ZS
    for z in range(ZS):
        o_ref[z] = total[z * step : (z + 1) * step]


def sum_rows(parts, after):
    vmem = pl.BlockSpec(memory_space=pltpu.VMEM)
    return pl.pallas_call(
        rows_kernel,
        in_specs=[vmem] + [pl.BlockSpec(memory_space=pl.ANY)] * len(after),
        out_specs=vmem,
        out_shape=jax.ShapeDtypeStruct((ZS, parts.shape[1] // ZS, parts.shape[2]), f32),
        compiler_params=VMEM,
        name="sum_rows",
    )(parts, *after)


def spread_kernel(x_ref, *refs):
    o_ref = refs[-1]
    parts = x_ref[...].astype(f32).reshape(x_ref.shape[0] // ZS, ZS, *x_ref.shape[1:])
    total = jnp.sum(parts, axis=0)
    for z in range(ZS):
        for third in range(3):
            cols = third * H * HD + z * 128
            o_ref[:, cols : cols + 128] = total[z, :, third * 128 : (third + 1) * 128]


def spread(share, after):
    vmem = pl.BlockSpec(memory_space=pltpu.VMEM)
    return pl.pallas_call(
        spread_kernel,
        in_specs=[vmem] + [pl.BlockSpec(memory_space=pl.ANY)] * len(after),
        out_specs=vmem,
        out_shape=jax.ShapeDtypeStruct((share.shape[1], 3 * H * HD), f32),
        compiler_params=VMEM,
        name="spread",
    )(share, *after)


def swap(values, axis):
    return lax.all_to_all(values, axis, split_axis=0, concat_axis=0, tiled=True)


RIGHT = [(i, (i + 1) % YS) for i in range(YS)]
LEFT = [(i, (i - 1) % YS) for i in range(YS)]
OPPOSITE = [(i, (i + 2) % YS) for i in range(YS)]


def gather_row(own):
    return own, lax.ppermute(own, "y", RIGHT), lax.ppermute(own, "y", LEFT), lax.ppermute(own, "y", OPPOSITE)


def sum_kernel(count, *refs):
    parts = (r[...].astype(f32) for r in refs[:count])
    refs[-1][...] = sum(parts).astype(bf16)


def sum_parts(parts, after):
    shape = parts[0].shape
    tile = pl.BlockSpec((shape[0] // 2, *shape[1:]), lambda i: (i,) + (0,) * (len(shape) - 1))
    return pl.pallas_call(
        functools.partial(sum_kernel, len(parts)),
        grid=(2,),
        in_specs=[tile] * len(parts) + [pl.BlockSpec(memory_space=pl.ANY)] * len(after),
        out_specs=tile,
        out_shape=jax.ShapeDtypeStruct(shape, bf16),
        compiler_params=VMEM,
        name="sum_parts",
    )(*parts, *after)


def sum_join_kernel(a_ref, b_ref, c_ref, d_ref, od_ref, o_ref):
    o_ref[:, :128, :] = sum(r[...].astype(f32) for r in (a_ref, b_ref, c_ref, d_ref)).astype(bf16)
    o_ref[:, 128:, :] = od_ref[...]


def sum_join(parts, od):
    tile = pl.BlockSpec((ZS // 2, 128, NODE_DEV), lambda i: (i, 0, 0))
    return pl.pallas_call(
        sum_join_kernel,
        grid=(2,),
        in_specs=[tile] * 5,
        out_specs=pl.BlockSpec((ZS // 2, 256, NODE_DEV), lambda i: (i, 0, 0)),
        out_shape=jax.ShapeDtypeStruct((ZS, 256, NODE_DEV), bf16),
        compiler_params=VMEM,
        name="sum_join",
    )(*parts, od)


def send_row(own, to_right, to_left, opp):
    return [
        own,
        lax.ppermute(to_right, "y", RIGHT),
        lax.ppermute(to_left, "y", LEFT),
        lax.ppermute(opp, "y", OPPOSITE),
    ]


def gate_kernel(*refs):
    pass


def gate(values, after):
    anywhere = pl.BlockSpec(memory_space=pl.ANY)
    return pl.pallas_call(
        gate_kernel,
        in_specs=[anywhere] * (len(values) + len(after)),
        out_specs=[anywhere] * len(values),
        out_shape=[jax.ShapeDtypeStruct(v.shape, v.dtype) for v in values],
        input_output_aliases={i: i for i in range(len(values))},
        compiler_params=VMEM,
        name="gate",
    )(*values, *after)


def weight_kernel(c_ref, oa_ref, ob_ref, ka_ref, kb_ref, f_ref, mine_ref, theirs_ref, grads):
    @pl.when(pl.program_id(0) == 0)
    def _():
        for t in range(ZS):
            nodes = slice(t * NODE_DEV, (t + 1) * NODE_DEV)
            dq = pair_rows(oa_ref[t], ob_ref[t])[0]
            dk, dv = pair_rows(ka_ref[t, :128, :], kb_ref[t])
            for k, part in enumerate((dq, dk, dv)):
                grads[k * 128 : (k + 1) * 128, nodes] = part

    both = nn(grads[...], f_ref[...]).T.astype(bf16)
    first = c_ref[0] == 0
    mine_ref[...] = jnp.where(first, both[:128], both[128:])
    theirs_ref[...] = jnp.where(first, both[128:], both[:128])


def weight_share(c, od_a, od_b, joint, kv_b, feats_row):
    d = feats_row.shape[1]
    part = whole(TURNED)
    return pl.pallas_call(
        weight_kernel,
        grid=(d // 256,),
        in_specs=[pl.BlockSpec(memory_space=pltpu.SMEM), part, part, whole(joint.shape), part, pl.BlockSpec((ROW, 256), lambda i: (0, i))],
        out_specs=[pl.BlockSpec((128, 384), lambda i: (i, 0))] * 2,
        out_shape=[jax.ShapeDtypeStruct((d // 2, 384), bf16)] * 2,
        scratch_shapes=[pltpu.VMEM((384, ROW), bf16)],
        compiler_params=VMEM,
        name="weight_share",
    )(c, od_a, od_b, joint, kv_b, feats_row)


def on_device(node_feats, w_qkv, w_out, cotangent, block_neighbors, block_counts, global_blocks):
    feats = node_feats[0]
    cot = cotangent[0]
    y = lax.axis_index("y")
    neighbors = lax.dynamic_slice_in_dim(block_neighbors[0], y * QBLK, QBLK, 0)
    counts = lax.dynamic_slice_in_dim(block_counts[0], y * QBLK, QBLK, 0)
    table = jnp.concatenate([jnp.broadcast_to(global_blocks[0][None], (QBLK, NGLOB)), neighbors], axis=1).reshape(-1)
    place = jnp.arange(QBLK, dtype=jnp.int32)
    key = counts * QBLK + place
    rank = jnp.sum((key[None, :] < key[:, None]).astype(jnp.int32), axis=1)
    order = jnp.sum(jnp.where(rank[None, :] == place[:, None], place[None, :], 0), axis=1)
    y_arr = y.reshape(1).astype(jnp.int32)

    kv_a, kv_b = project_kv(feats, w_qkv)
    joint, qg_b, feats_copy = project_qg(feats, cot, w_qkv, w_out, kv_b, (table, counts, order))
    row_a = gather_row(swap(kv_a, "z"))
    joint_row = swap(joint, "z")
    row_b = gather_row(first_half(joint_row))
    (feats_late, qg_b) = gate([feats_copy, qg_b], [joint_row])
    qg_row_b = swap(qg_b, "z")
    feats_row = lax.all_gather(feats_late, "z", axis=0, tiled=True)
    od_a, *kv_a = attend(table, counts, order, y_arr, row_a, joint_row, feats_late)
    to_nodes = lambda v: swap(v, "z")
    (od_a_late,) = gate([od_a], [qg_row_b])
    od_nodes_a = to_nodes(od_a_late)
    parts_a = send_row(*kv_a)
    late = attend(table, counts, order, y_arr, row_b, qg_row_b, od_a_late)
    od_b, *kv_b = gate(late, parts_a[1:] + [od_nodes_a])
    parts_b = send_row(*kv_b)
    joint = sum_join(parts_a, od_b)
    joint_nodes = swap(joint, "z")
    sum_b = sum_parts(parts_b, (joint_nodes,))
    kv_nodes_b = to_nodes(sum_b)
    attn_update = project_out(od_nodes_a, joint_nodes, w_out)
    grad_nodes = node_grads(od_nodes_a, joint_nodes, kv_nodes_b, w_qkv)

    d = feats.shape[1]
    c_arr = lax.axis_index("c").reshape(1).astype(jnp.int32)
    mine, theirs = weight_share(c_arr, od_a_late, od_b, joint, sum_b, feats_row)
    theirs = lax.ppermute(theirs, "c", [(0, 1), (1, 0)])
    share = sum_parts([mine, theirs], ()).reshape(16, d // 32, 384)
    (share,) = gate([share], [kv_nodes_b])
    share = sum_rows(swap(share, ("x", "y")), (grad_nodes,))
    grad_weights = spread(swap(share, "z"), (attn_update,))
    return attn_update[None], grad_nodes[None], grad_weights


def solution(mesh):
    fine = Mesh(np.asarray(mesh.devices).reshape(4, 2, YS, ZS), ("x", "c", "y", "z"))
    dp, seq = ("x", "c"), ("y", "z")
    in_specs = (P(dp, seq, None), P(), P(), P(dp, seq, None), P(dp, None, None), P(dp, None), P(dp, None))
    out_specs = (P(dp, seq, None), P(dp, seq, None), P(dp + seq, None))
    return jax.shard_map(on_device, mesh=fine, in_specs=in_specs, out_specs=out_specs, check_vma=False)
```

```python
import functools
import math

import jax
import jax.numpy as jnp
import numpy as np
from jax import lax
from jax.experimental import pallas as pl
from jax.experimental.pallas import tpu as pltpu
from jax.sharding import Mesh
from jax.sharding import PartitionSpec as P

H = 16
HD = 64
BLOCK = 128
MAXNB = 8
NGLOB = 4
SLOTS = MAXNB + NGLOB
YS = 4
ZS = 8
NODE_DEV = 256
ROW = NODE_DEV * ZS
QBLK = ROW // BLOCK
NODES = ROW * YS
TURNED = (ZS, 2 * HD, NODE_DEV)
PIECES = YS * ZS
SCALE = HD**-0.5
LOG2E = math.log2(math.e)
MASKED = -3.0e38
VMEM = pltpu.CompilerParams(vmem_limit_bytes=60 * 1024 * 1024)

bf16 = jnp.bfloat16
f32 = jnp.float32


def low_half(shape):
    return lax.broadcasted_iota(jnp.int32, shape, 1) < HD


def pair_up(first, second):
    low = low_half(first.shape)
    return (
        jnp.where(low, first, pltpu.roll(second, HD, 1)),
        jnp.where(low, pltpu.roll(first, HD, 1), second),
    )


def pair_rows(first, second):
    return (
        jnp.concatenate([first[:HD], second[:HD]], axis=0),
        jnp.concatenate([first[HD:], second[HD:]], axis=0),
    )


def nt(a, b):
    return lax.dot_general(a, b, (((1,), (1,)), ((), ())), preferred_element_type=f32)


def nn(a, b):
    return lax.dot_general(a, b, (((1,), (0,)), ((), ())), preferred_element_type=f32)


def put_pairs(first, second, a_ref, b_ref):
    for u in (0, 1):
        cols = slice(u * 128, (u + 1) * 128)
        a, b = pair_rows(first[:, cols].T, second[:, cols].T)
        a_ref[u] = a.astype(bf16)
        b_ref[u] = b.astype(bf16)


def kv_kernel(f_ref, wk_ref, wv_ref, a_ref, b_ref):
    put_pairs(nn(f_ref[...], wk_ref[...]), nn(f_ref[...], wv_ref[...]), a_ref, b_ref)


def first_kernel(x_ref, o_ref):
    o_ref[...] = x_ref[...]


def first_half(both):
    return pl.pallas_call(
        first_kernel,
        grid=(4,),
        in_specs=[pl.BlockSpec((ZS // 4, 128, NODE_DEV), lambda i: (i, 0, 0))],
        out_specs=pl.BlockSpec((ZS // 4, 128, NODE_DEV), lambda i: (i, 0, 0)),
        out_shape=jax.ShapeDtypeStruct(TURNED, bf16),
        compiler_params=VMEM,
        name="first_half",
    )(both)


def qg_kernel(f_ref, c_ref, wq_ref, wo_ref, kv_ref, *refs):
    joint_ref, b_ref, copy_ref = refs[-3:]

    @pl.when(pl.program_id(0) == 0)
    def _():
        copy_ref[...] = f_ref[...]

    joint_ref[:, :128, :] = kv_ref[...]
    put_pairs(nn(f_ref[...], wq_ref[...]), nt(c_ref[...], wo_ref[...]), joint_ref.at[:, 128:], b_ref)


def whole(shape):
    return pl.BlockSpec(shape, lambda i: (0,) * len(shape))


def project_kv(feats, w_qkv):
    d = feats.shape[1]
    return pl.pallas_call(
        kv_kernel,
        grid=(ZS // 2,),
        in_specs=[
            whole((NODE_DEV, d)),
            pl.BlockSpec((d, 256), lambda i: (0, ZS // 2 + i)),
            pl.BlockSpec((d, 256), lambda i: (0, ZS + i)),
        ],
        out_specs=[pl.BlockSpec((2, 128, NODE_DEV), lambda i: (i, 0, 0))] * 2,
        out_shape=[jax.ShapeDtypeStruct(TURNED, bf16)] * 2,
        compiler_params=VMEM,
        name="project_kv",
    )(feats, w_qkv, w_qkv)


def project_qg(feats, cot, w_qkv, w_out, kv, before):
    d = feats.shape[1]
    tile = pl.BlockSpec((2, 128, NODE_DEV), lambda i: (i, 0, 0))
    return pl.pallas_call(
        qg_kernel,
        grid=(ZS // 2,),
        in_specs=[
            whole((NODE_DEV, d)),
            whole((NODE_DEV, d)),
            pl.BlockSpec((d, 256), lambda i: (0, i)),
            pl.BlockSpec((256, d), lambda i: (i, 0)),
            tile,
        ]
        + [pl.BlockSpec(memory_space=pl.ANY)] * len(before),
        out_specs=[pl.BlockSpec((2, 256, NODE_DEV), lambda i: (i, 0, 0)), tile, whole((NODE_DEV, d))],
        out_shape=[
            jax.ShapeDtypeStruct((ZS, 256, NODE_DEV), bf16),
            jax.ShapeDtypeStruct(TURNED, bf16),
            jax.ShapeDtypeStruct((NODE_DEV, d), bf16),
        ],
        compiler_params=VMEM,
        name="project_qg",
    )(feats, cot, w_qkv, w_out, kv, *before)


def attend_kernel(
    skip, tab_ref, cnt_ref, order_ref, y_ref, own_ref, left_ref, right_ref, opp_ref, qg_ref, after_ref,
    od_ref, sum_own_ref, sum_right_ref, sum_left_ref, sum_opp_ref,
    kv_s, acc, sc0, sc1, xs0, xs1,
):
    y = y_ref[0]
    at = lambda step: lax.rem(y + step, YS) * ZS

    for step, ref in ((0, own_ref), (YS - 1, left_ref), (1, right_ref), (2, opp_ref)):
        kv_s[pl.ds(at(step), ZS)] = ref[...]

    @pl.loop(0, PIECES)
    def _(t):
        acc[t] = jnp.zeros((128, NODE_DEV), f32)

    def cols(block):
        return pl.ds(pl.multiple_of(lax.rem(block, 2) * BLOCK, BLOCK), BLOCK)

    def keys(ids, t):
        return jnp.concatenate([kv_s[lax.div(ids[2 * t + u], 2), :, cols(ids[2 * t + u])] for u in (0, 1)], axis=1)

    def score(i, pairs, sc):
        ids = [tab_ref[i * SLOTS + t] for t in range(2 * pairs)]
        qg = qg_ref[lax.div(i, 2), skip : skip + 128, cols(i)].astype(f32)
        top = lax.broadcasted_iota(jnp.int32, qg.shape, 0) < HD
        zero = jnp.zeros_like(qg)
        wide_t = jnp.concatenate([jnp.where(top, qg, zero), jnp.where(top, zero, qg)], axis=1)
        wide = wide_t.T.astype(bf16)
        for t in range(pairs):
            sc[:, t * 256 : (t + 1) * 256] = nn(wide, keys(ids, t))
        return i, ids, wide_t.astype(bf16)

    def soften(i, pairs, sc, xs):
        width = pairs * 256
        count = cnt_ref[i]
        step = 16
        for r in range(BLOCK // step):
            s = sc[r * step : (r + 1) * step, :width]
            dp = sc[BLOCK + r * step : BLOCK + (r + 1) * step, :width]
            kept = [s[:, : (NGLOB + 1) * BLOCK]]
            for t in range(NGLOB + 1, 2 * pairs):
                kept.append(jnp.where(t - NGLOB < count, s[:, t * BLOCK : (t + 1) * BLOCK], MASKED))
            s = jnp.concatenate(kept, axis=1)
            e = jnp.exp2((s - jnp.max(s, axis=1, keepdims=True)) * (SCALE * LOG2E))
            p = e * (1.0 / jnp.sum(e, axis=1, keepdims=True))
            delta = jnp.sum(p * dp, axis=1, keepdims=True)
            ds = p * (dp - delta) * SCALE
            xs[r * step : (r + 1) * step, :width] = ds.astype(bf16)
            xs[BLOCK + r * step : BLOCK + (r + 1) * step, :width] = p.astype(bf16)

    def mix(state, pairs, xs):
        i, ids, wide_t = state
        every = jnp.concatenate([keys(ids, t) for t in range(pairs)], axis=1)
        mixed = nt(every, xs[:, : pairs * 256])
        od = jnp.concatenate([mixed[:HD, :BLOCK], mixed[HD:, BLOCK:]], axis=0)
        od_ref[lax.div(i, 2), :, cols(i)] = od.astype(bf16)
        for t in range(pairs):
            part = nn(wide_t, xs[:, t * 256 : (t + 1) * 256])
            for u in (0, 1):
                block = ids[2 * t + u]
                acc[lax.div(block, 2), :, cols(block)] += part[:, u * BLOCK : (u + 1) * BLOCK]

    def two_blocks(i, k, pairs):
        first = score(i, pairs, sc0)
        second = score(k, pairs, sc1)
        soften(i, pairs, sc0, xs0)
        mix(first, pairs, xs0)
        soften(k, pairs, sc1, xs1)
        mix(second, pairs, xs1)

    @pl.loop(0, QBLK // 2)
    def _(t):
        i, k = order_ref[2 * t], order_ref[2 * t + 1]
        pairs = NGLOB // 2 + (jnp.maximum(cnt_ref[i], cnt_ref[k]) + 1) // 2
        for v in range(NGLOB // 2 + 1, SLOTS // 2 + 1):
            pl.when(pairs == v)(functools.partial(two_blocks, i, k, v))

    for step, out in ((0, sum_own_ref), (1, sum_right_ref), (YS - 1, sum_left_ref), (2, sum_opp_ref)):
        start = at(step)

        @pl.loop(0, ZS)
        def _(t):
            out[t] = acc[start + t].astype(bf16)


def attend(table, counts, order, y, kv_parts, qg, after):
    vmem = pl.BlockSpec(memory_space=pltpu.VMEM)
    smem = pl.BlockSpec(memory_space=pltpu.SMEM)
    row = jax.ShapeDtypeStruct(TURNED, bf16)
    return pl.pallas_call(
        functools.partial(attend_kernel, qg.shape[1] - 128),
        in_specs=[smem] * 4 + [vmem] * 5 + [pl.BlockSpec(memory_space=pl.ANY)],
        out_specs=[vmem] * 5,
        out_shape=[row] * 5,
        scratch_shapes=[
            pltpu.VMEM((PIECES, 128, NODE_DEV), bf16),
            pltpu.VMEM((PIECES, 128, NODE_DEV), f32),
            pltpu.VMEM((256, SLOTS * BLOCK), f32),
            pltpu.VMEM((256, SLOTS * BLOCK), f32),
            pltpu.VMEM((256, SLOTS * BLOCK), bf16),
            pltpu.VMEM((256, SLOTS * BLOCK), bf16),
        ],
        compiler_params=VMEM,
        cost_estimate=pl.CostEstimate(
            flops=26 * 10**9, bytes_accessed=6 << 20, transcendentals=0
        ),
        name="attend",
    )(table, counts, order, y, *kv_parts, qg, after)


def turn(tiles):
    return jnp.concatenate(tiles, axis=0).astype(f32).T.astype(bf16)


def out_kernel(a_ref, b_ref, wo_ref, o_ref, total):
    step = pl.program_id(0)

    @pl.when(step == 0)
    def _():
        total[...] = jnp.zeros_like(total)

    att = [pair_rows(a_ref[u], b_ref[u])[1] for u in (0, 1)]
    total[...] += nn(turn(att), wo_ref[...])

    @pl.when(step == pl.num_programs(0) - 1)
    def _():
        o_ref[...] = total[...].astype(bf16)


SECOND = pl.BlockSpec((2, 128, NODE_DEV), lambda i: (i, 1, 0))


def project_out(od_a, joint, w_out):
    d = w_out.shape[1]
    tile = pl.BlockSpec((2, 128, NODE_DEV), lambda i: (i, 0, 0))
    return pl.pallas_call(
        out_kernel,
        grid=(ZS // 2,),
        in_specs=[tile, SECOND, pl.BlockSpec((256, d), lambda i: (i, 0))],
        out_specs=whole((NODE_DEV, d)),
        out_shape=jax.ShapeDtypeStruct((NODE_DEV, d), bf16),
        scratch_shapes=[pltpu.VMEM((NODE_DEV, d), f32)],
        compiler_params=VMEM,
        name="project_out",
    )(od_a, joint, w_out)


def nodes_kernel(oa_ref, ob_ref, ka_ref, kb_ref, wq_ref, wk_ref, wv_ref, o_ref, total):
    step = pl.program_id(0)

    @pl.when(step == 0)
    def _():
        total[...] = jnp.zeros_like(total)

    dq, dk, dv = [], [], []
    for u in (0, 1):
        dq.append(pair_rows(oa_ref[u], ob_ref[u])[0])
        k, v = pair_rows(ka_ref[u], kb_ref[u])
        dk.append(k)
        dv.append(v)
    add = nt(turn(dq), wq_ref[...])
    add += nt(turn(dk), wk_ref[...])
    add += nt(turn(dv), wv_ref[...])
    total[...] += add

    @pl.when(step == pl.num_programs(0) - 1)
    def _():
        o_ref[...] = total[...].astype(bf16)


def node_grads(od_a, joint, kv_b, w_qkv):
    d = w_qkv.shape[0]
    tile = pl.BlockSpec((2, 128, NODE_DEV), lambda i: (i, 0, 0))
    steps = ZS // 2
    return pl.pallas_call(
        nodes_kernel,
        grid=(steps,),
        in_specs=[tile, SECOND, tile, tile]
        + [pl.BlockSpec((d, 256), functools.partial(lambda i, third: (0, third * steps + i), third=k)) for k in range(3)],
        out_specs=whole((NODE_DEV, d)),
        out_shape=jax.ShapeDtypeStruct((NODE_DEV, d), bf16),
        scratch_shapes=[pltpu.VMEM((NODE_DEV, d), f32)],
        compiler_params=VMEM,
        name="node_grads",
    )(od_a, joint, joint, kv_b, w_qkv, w_qkv, w_qkv)


def rows_kernel(x_ref, *refs):
    o_ref = refs[-1]
    total = jnp.sum(x_ref[...].astype(f32), axis=0)
    step = total.shape[0] // ZS
    for z in range(ZS):
        o_ref[z] = total[z * step : (z + 1) * step]


def sum_rows(parts, after):
    vmem = pl.BlockSpec(memory_space=pltpu.VMEM)
    return pl.pallas_call(
        rows_kernel,
        in_specs=[vmem] + [pl.BlockSpec(memory_space=pl.ANY)] * len(after),
        out_specs=vmem,
        out_shape=jax.ShapeDtypeStruct((ZS, parts.shape[1] // ZS, parts.shape[2]), f32),
        compiler_params=VMEM,
        name="sum_rows",
    )(parts, *after)


def spread_kernel(x_ref, *refs):
    o_ref = refs[-1]
    parts = x_ref[...].astype(f32).reshape(x_ref.shape[0] // ZS, ZS, *x_ref.shape[1:])
    total = jnp.sum(parts, axis=0)
    for z in range(ZS):
        for third in range(3):
            cols = third * H * HD + z * 128
            o_ref[:, cols : cols + 128] = total[z, :, third * 128 : (third + 1) * 128]


def spread(share, after):
    vmem = pl.BlockSpec(memory_space=pltpu.VMEM)
    return pl.pallas_call(
        spread_kernel,
        in_specs=[vmem] + [pl.BlockSpec(memory_space=pl.ANY)] * len(after),
        out_specs=vmem,
        out_shape=jax.ShapeDtypeStruct((share.shape[1], 3 * H * HD), f32),
        compiler_params=VMEM,
        name="spread",
    )(share, *after)


def swap(values, axis):
    return lax.all_to_all(values, axis, split_axis=0, concat_axis=0, tiled=True)


RIGHT = [(i, (i + 1) % YS) for i in range(YS)]
LEFT = [(i, (i - 1) % YS) for i in range(YS)]
OPPOSITE = [(i, (i + 2) % YS) for i in range(YS)]


def gather_row(own):
    return own, lax.ppermute(own, "y", RIGHT), lax.ppermute(own, "y", LEFT), lax.ppermute(own, "y", OPPOSITE)


def sum_kernel(count, *refs):
    parts = (r[...].astype(f32) for r in refs[:count])
    refs[-1][...] = sum(parts).astype(bf16)


def sum_parts(parts, after):
    shape = parts[0].shape
    tile = pl.BlockSpec((shape[0] // 4, *shape[1:]), lambda i: (i,) + (0,) * (len(shape) - 1))
    return pl.pallas_call(
        functools.partial(sum_kernel, len(parts)),
        grid=(4,),
        in_specs=[tile] * len(parts) + [pl.BlockSpec(memory_space=pl.ANY)] * len(after),
        out_specs=tile,
        out_shape=jax.ShapeDtypeStruct(shape, bf16),
        compiler_params=VMEM,
        name="sum_parts",
    )(*parts, *after)


def sum_join_kernel(a_ref, b_ref, c_ref, d_ref, od_ref, o_ref):
    o_ref[:, :128, :] = sum(r[...].astype(f32) for r in (a_ref, b_ref, c_ref, d_ref)).astype(bf16)
    o_ref[:, 128:, :] = od_ref[...]


def sum_join(parts, od):
    tile = pl.BlockSpec((ZS // 4, 128, NODE_DEV), lambda i: (i, 0, 0))
    return pl.pallas_call(
        sum_join_kernel,
        grid=(4,),
        in_specs=[tile] * 5,
        out_specs=pl.BlockSpec((ZS // 4, 256, NODE_DEV), lambda i: (i, 0, 0)),
        out_shape=jax.ShapeDtypeStruct((ZS, 256, NODE_DEV), bf16),
        compiler_params=VMEM,
        name="sum_join",
    )(*parts, od)


def send_row(own, to_right, to_left, opp):
    return [
        own,
        lax.ppermute(to_right, "y", RIGHT),
        lax.ppermute(to_left, "y", LEFT),
        lax.ppermute(opp, "y", OPPOSITE),
    ]


def gate_kernel(*refs):
    pass


def gate(values, after):
    anywhere = pl.BlockSpec(memory_space=pl.ANY)
    return pl.pallas_call(
        gate_kernel,
        in_specs=[anywhere] * (len(values) + len(after)),
        out_specs=[anywhere] * len(values),
        out_shape=[jax.ShapeDtypeStruct(v.shape, v.dtype) for v in values],
        input_output_aliases={i: i for i in range(len(values))},
        compiler_params=VMEM,
        name="gate",
    )(*values, *after)


def weight_kernel(c_ref, oa_ref, ob_ref, ka_ref, kb_ref, f_ref, mine_ref, theirs_ref, grads):
    @pl.when(pl.program_id(0) == 0)
    def _():
        for t in range(ZS):
            nodes = slice(t * NODE_DEV, (t + 1) * NODE_DEV)
            dq = pair_rows(oa_ref[t], ob_ref[t])[0]
            dk, dv = pair_rows(ka_ref[t, :128, :], kb_ref[t])
            for k, part in enumerate((dq, dk, dv)):
                grads[k * 128 : (k + 1) * 128, nodes] = part

    both = nn(grads[...], f_ref[...]).T.astype(bf16)
    first = c_ref[0] == 0
    mine_ref[...] = jnp.where(first, both[:128], both[128:])
    theirs_ref[...] = jnp.where(first, both[128:], both[:128])


def weight_share(c, od_a, od_b, joint, kv_b, feats_row):
    d = feats_row.shape[1]
    part = whole(TURNED)
    return pl.pallas_call(
        weight_kernel,
        grid=(d // 256,),
        in_specs=[pl.BlockSpec(memory_space=pltpu.SMEM), part, part, whole(joint.shape), part, pl.BlockSpec((ROW, 256), lambda i: (0, i))],
        out_specs=[pl.BlockSpec((128, 384), lambda i: (i, 0))] * 2,
        out_shape=[jax.ShapeDtypeStruct((d // 2, 384), bf16)] * 2,
        scratch_shapes=[pltpu.VMEM((384, ROW), bf16)],
        compiler_params=VMEM,
        name="weight_share",
    )(c, od_a, od_b, joint, kv_b, feats_row)


def on_device(node_feats, w_qkv, w_out, cotangent, block_neighbors, block_counts, global_blocks):
    feats = node_feats[0]
    cot = cotangent[0]
    y = lax.axis_index("y")
    neighbors = lax.dynamic_slice_in_dim(block_neighbors[0], y * QBLK, QBLK, 0)
    counts = lax.dynamic_slice_in_dim(block_counts[0], y * QBLK, QBLK, 0)
    table = jnp.concatenate([jnp.broadcast_to(global_blocks[0][None], (QBLK, NGLOB)), neighbors], axis=1).reshape(-1)
    place = jnp.arange(QBLK, dtype=jnp.int32)
    key = counts * QBLK + place
    rank = jnp.sum((key[None, :] < key[:, None]).astype(jnp.int32), axis=1)
    order = jnp.sum(jnp.where(rank[None, :] == place[:, None], place[None, :], 0), axis=1)
    y_arr = y.reshape(1).astype(jnp.int32)

    kv_a, kv_b = project_kv(feats, w_qkv)
    joint, qg_b, feats_copy = project_qg(feats, cot, w_qkv, w_out, kv_b, (table, counts, order))
    row_a = gather_row(swap(kv_a, "z"))
    joint_row = swap(joint, "z")
    row_b = gather_row(first_half(joint_row))
    (feats_late, qg_b) = gate([feats_copy, qg_b], [joint_row])
    qg_row_b = swap(qg_b, "z")
    feats_row = lax.all_gather(feats_late, "z", axis=0, tiled=True)
    od_a, *kv_a = attend(table, counts, order, y_arr, row_a, joint_row, feats_late)
    to_nodes = lambda v: swap(v, "z")
    (od_a_late,) = gate([od_a], [qg_row_b])
    od_nodes_a = to_nodes(od_a_late)
    parts_a = send_row(*kv_a)
    late = attend(table, counts, order, y_arr, row_b, qg_row_b, od_a_late)
    od_b, *kv_b = gate(late, parts_a[1:] + [od_nodes_a])
    parts_b = send_row(*kv_b)
    joint = sum_join(parts_a, od_b)
    joint_nodes = swap(joint, "z")
    sum_b = sum_parts(parts_b, (joint_nodes,))
    kv_nodes_b = to_nodes(sum_b)
    attn_update = project_out(od_nodes_a, joint_nodes, w_out)
    grad_nodes = node_grads(od_nodes_a, joint_nodes, kv_nodes_b, w_qkv)

    d = feats.shape[1]
    c_arr = lax.axis_index("c").reshape(1).astype(jnp.int32)
    mine, theirs = weight_share(c_arr, od_a_late, od_b, joint, sum_b, feats_row)
    theirs = lax.ppermute(theirs, "c", [(0, 1), (1, 0)])
    share = sum_parts([mine, theirs], ()).reshape(16, d // 32, 384)
    (share,) = gate([share], [kv_nodes_b])
    share = sum_rows(swap(share, ("x", "y")), (grad_nodes,))
    grad_weights = spread(swap(share, "z"), (attn_update,))
    return attn_update[None], grad_nodes[None], grad_weights


def solution(mesh):
    fine = Mesh(np.asarray(mesh.devices).reshape(4, 2, YS, ZS), ("x", "c", "y", "z"))
    dp, seq = ("x", "c"), ("y", "z")
    in_specs = (P(dp, seq, None), P(), P(), P(dp, seq, None), P(dp, None, None), P(dp, None), P(dp, None))
    out_specs = (P(dp, seq, None), P(dp, seq, None), P(dp + seq, None))
    return jax.shard_map(on_device, mesh=fine, in_specs=in_specs, out_specs=out_specs, check_vma=False)
```

```python
import functools
import math

import jax
import jax.numpy as jnp
import numpy as np
from jax import lax
from jax.experimental import pallas as pl
from jax.experimental.pallas import tpu as pltpu
from jax.sharding import Mesh
from jax.sharding import PartitionSpec as P

H = 16
HD = 64
BLOCK = 128
MAXNB = 8
NGLOB = 4
SLOTS = MAXNB + NGLOB
YS = 4
ZS = 8
NODE_DEV = 256
ROW = NODE_DEV * ZS
QBLK = ROW // BLOCK
NODES = ROW * YS
TURNED = (ZS, 2 * HD, NODE_DEV)
PIECES = YS * ZS
SCALE = HD**-0.5
LOG2E = math.log2(math.e)
MASKED = -3.0e38
VMEM = pltpu.CompilerParams(vmem_limit_bytes=60 * 1024 * 1024)

bf16 = jnp.bfloat16
f32 = jnp.float32


def low_half(shape):
    return lax.broadcasted_iota(jnp.int32, shape, 1) < HD


def pair_up(first, second):
    low = low_half(first.shape)
    return (
        jnp.where(low, first, pltpu.roll(second, HD, 1)),
        jnp.where(low, pltpu.roll(first, HD, 1), second),
    )


def pair_rows(first, second):
    return (
        jnp.concatenate([first[:HD], second[:HD]], axis=0),
        jnp.concatenate([first[HD:], second[HD:]], axis=0),
    )


def nt(a, b):
    return lax.dot_general(a, b, (((1,), (1,)), ((), ())), preferred_element_type=f32)


def nn(a, b):
    return lax.dot_general(a, b, (((1,), (0,)), ((), ())), preferred_element_type=f32)


def put_pairs(first, second, a_ref, b_ref):
    for u in (0, 1):
        cols = slice(u * 128, (u + 1) * 128)
        a, b = pair_rows(first[:, cols].T, second[:, cols].T)
        a_ref[u] = a.astype(bf16)
        b_ref[u] = b.astype(bf16)


def kv_kernel(f_ref, wk_ref, wv_ref, a_ref, b_ref):
    put_pairs(nn(f_ref[...], wk_ref[...]), nn(f_ref[...], wv_ref[...]), a_ref, b_ref)


def first_kernel(x_ref, o_ref):
    o_ref[...] = x_ref[...]


def first_half(both):
    return pl.pallas_call(
        first_kernel,
        grid=(2,),
        in_specs=[pl.BlockSpec((ZS // 2, 128, NODE_DEV), lambda i: (i, 0, 0))],
        out_specs=pl.BlockSpec((ZS // 2, 128, NODE_DEV), lambda i: (i, 0, 0)),
        out_shape=jax.ShapeDtypeStruct(TURNED, bf16),
        compiler_params=VMEM,
        name="first_half",
    )(both)


def qg_kernel(f_ref, c_ref, wq_ref, wo_ref, kv_ref, *refs):
    joint_ref, b_ref, copy_ref = refs[-3:]

    @pl.when(pl.program_id(0) == 0)
    def _():
        copy_ref[...] = f_ref[...]

    joint_ref[:, :128, :] = kv_ref[...]
    put_pairs(nn(f_ref[...], wq_ref[...]), nt(c_ref[...], wo_ref[...]), joint_ref.at[:, 128:], b_ref)


def whole(shape):
    return pl.BlockSpec(shape, lambda i: (0,) * len(shape))


def project_kv(feats, w_qkv):
    d = feats.shape[1]
    return pl.pallas_call(
        kv_kernel,
        grid=(ZS // 2,),
        in_specs=[
            whole((NODE_DEV, d)),
            pl.BlockSpec((d, 256), lambda i: (0, ZS // 2 + i)),
            pl.BlockSpec((d, 256), lambda i: (0, ZS + i)),
        ],
        out_specs=[pl.BlockSpec((2, 128, NODE_DEV), lambda i: (i, 0, 0))] * 2,
        out_shape=[jax.ShapeDtypeStruct(TURNED, bf16)] * 2,
        compiler_params=VMEM,
        name="project_kv",
    )(feats, w_qkv, w_qkv)


def project_qg(feats, cot, w_qkv, w_out, kv, before):
    d = feats.shape[1]
    tile = pl.BlockSpec((2, 128, NODE_DEV), lambda i: (i, 0, 0))
    return pl.pallas_call(
        qg_kernel,
        grid=(ZS // 2,),
        in_specs=[
            whole((NODE_DEV, d)),
            whole((NODE_DEV, d)),
            pl.BlockSpec((d, 256), lambda i: (0, i)),
            pl.BlockSpec((256, d), lambda i: (i, 0)),
            tile,
        ]
        + [pl.BlockSpec(memory_space=pl.ANY)] * len(before),
        out_specs=[pl.BlockSpec((2, 256, NODE_DEV), lambda i: (i, 0, 0)), tile, whole((NODE_DEV, d))],
        out_shape=[
            jax.ShapeDtypeStruct((ZS, 256, NODE_DEV), bf16),
            jax.ShapeDtypeStruct(TURNED, bf16),
            jax.ShapeDtypeStruct((NODE_DEV, d), bf16),
        ],
        compiler_params=VMEM,
        name="project_qg",
    )(feats, cot, w_qkv, w_out, kv, *before)


def attend_kernel(
    skip, tab_ref, cnt_ref, order_ref, y_ref, own_ref, left_ref, right_ref, opp_ref, qg_ref, after_ref,
    od_ref, sum_own_ref, sum_right_ref, sum_left_ref, sum_opp_ref,
    kv_s, acc, sc0, sc1, xs0, xs1,
):
    y = y_ref[0]
    at = lambda step: lax.rem(y + step, YS) * ZS

    for step, ref in ((0, own_ref), (YS - 1, left_ref), (1, right_ref), (2, opp_ref)):
        kv_s[pl.ds(at(step), ZS)] = ref[...]

    @pl.loop(0, PIECES)
    def _(t):
        acc[t] = jnp.zeros((128, NODE_DEV), f32)

    def cols(block):
        return pl.ds(pl.multiple_of(lax.rem(block, 2) * BLOCK, BLOCK), BLOCK)

    def keys(ids, t):
        return jnp.concatenate([kv_s[lax.div(ids[2 * t + u], 2), :, cols(ids[2 * t + u])] for u in (0, 1)], axis=1)

    def score(i, pairs, sc):
        ids = [tab_ref[i * SLOTS + t] for t in range(2 * pairs)]
        qg = qg_ref[lax.div(i, 2), skip : skip + 128, cols(i)].astype(f32)
        top = lax.broadcasted_iota(jnp.int32, qg.shape, 0) < HD
        zero = jnp.zeros_like(qg)
        wide_t = jnp.concatenate([jnp.where(top, qg, zero), jnp.where(top, zero, qg)], axis=1)
        wide = wide_t.T.astype(bf16)
        for t in range(pairs):
            sc[:, t * 256 : (t + 1) * 256] = nn(wide, keys(ids, t))
        return i, ids, wide_t.astype(bf16)

    def soften(i, pairs, sc, xs):
        width = pairs * 256
        count = cnt_ref[i]
        step = 16
        for r in range(BLOCK // step):
            s = sc[r * step : (r + 1) * step, :width]
            dp = sc[BLOCK + r * step : BLOCK + (r + 1) * step, :width]
            kept = [s[:, : (NGLOB + 1) * BLOCK]]
            for t in range(NGLOB + 1, 2 * pairs):
                kept.append(jnp.where(t - NGLOB < count, s[:, t * BLOCK : (t + 1) * BLOCK], MASKED))
            s = jnp.concatenate(kept, axis=1)
            e = jnp.exp2((s - jnp.max(s, axis=1, keepdims=True)) * (SCALE * LOG2E))
            p = e * (1.0 / jnp.sum(e, axis=1, keepdims=True))
            delta = jnp.sum(p * dp, axis=1, keepdims=True)
            ds = p * (dp - delta) * SCALE
            xs[r * step : (r + 1) * step, :width] = ds.astype(bf16)
            xs[BLOCK + r * step : BLOCK + (r + 1) * step, :width] = p.astype(bf16)

    def mix(state, pairs, xs):
        i, ids, wide_t = state
        every = jnp.concatenate([keys(ids, t) for t in range(pairs)], axis=1)
        mixed = nt(every, xs[:, : pairs * 256])
        od = jnp.concatenate([mixed[:HD, :BLOCK], mixed[HD:, BLOCK:]], axis=0)
        od_ref[lax.div(i, 2), :, cols(i)] = od.astype(bf16)
        for t in range(pairs):
            part = nn(wide_t, xs[:, t * 256 : (t + 1) * 256])
            for u in (0, 1):
                block = ids[2 * t + u]
                acc[lax.div(block, 2), :, cols(block)] += part[:, u * BLOCK : (u + 1) * BLOCK]

    def two_blocks(i, k, pairs):
        first = score(i, pairs, sc0)
        second = score(k, pairs, sc1)
        soften(i, pairs, sc0, xs0)
        mix(first, pairs, xs0)
        soften(k, pairs, sc1, xs1)
        mix(second, pairs, xs1)

    @pl.loop(0, QBLK // 2)
    def _(t):
        i, k = order_ref[2 * t], order_ref[2 * t + 1]
        pairs = NGLOB // 2 + (jnp.maximum(cnt_ref[i], cnt_ref[k]) + 1) // 2
        for v in range(NGLOB // 2 + 1, SLOTS // 2 + 1):
            pl.when(pairs == v)(functools.partial(two_blocks, i, k, v))

    for step, out in ((0, sum_own_ref), (1, sum_right_ref), (YS - 1, sum_left_ref), (2, sum_opp_ref)):
        start = at(step)

        @pl.loop(0, ZS)
        def _(t):
            out[t] = acc[start + t].astype(bf16)


def attend(table, counts, order, y, kv_parts, qg, after):
    vmem = pl.BlockSpec(memory_space=pltpu.VMEM)
    smem = pl.BlockSpec(memory_space=pltpu.SMEM)
    row = jax.ShapeDtypeStruct(TURNED, bf16)
    return pl.pallas_call(
        functools.partial(attend_kernel, qg.shape[1] - 128),
        in_specs=[smem] * 4 + [vmem] * 5 + [pl.BlockSpec(memory_space=pl.ANY)],
        out_specs=[vmem] * 5,
        out_shape=[row] * 5,
        scratch_shapes=[
            pltpu.VMEM((PIECES, 128, NODE_DEV), bf16),
            pltpu.VMEM((PIECES, 128, NODE_DEV), f32),
            pltpu.VMEM((256, SLOTS * BLOCK), f32),
            pltpu.VMEM((256, SLOTS * BLOCK), f32),
            pltpu.VMEM((256, SLOTS * BLOCK), bf16),
            pltpu.VMEM((256, SLOTS * BLOCK), bf16),
        ],
        compiler_params=VMEM,
        cost_estimate=pl.CostEstimate(
            flops=26 * 10**9, bytes_accessed=6 << 20, transcendentals=0
        ),
        name="attend",
    )(table, counts, order, y, *kv_parts, qg, after)


def turn(tiles):
    return jnp.concatenate(tiles, axis=0).astype(f32).T.astype(bf16)


def out_kernel(a_ref, b_ref, wo_ref, o_ref, total):
    step = pl.program_id(0)

    @pl.when(step == 0)
    def _():
        total[...] = jnp.zeros_like(total)

    att = [pair_rows(a_ref[u], b_ref[u])[1] for u in (0, 1)]
    total[...] += nn(turn(att), wo_ref[...])

    @pl.when(step == pl.num_programs(0) - 1)
    def _():
        o_ref[...] = total[...].astype(bf16)


SECOND = pl.BlockSpec((2, 128, NODE_DEV), lambda i: (i, 1, 0))


def project_out(od_a, joint, w_out):
    d = w_out.shape[1]
    tile = pl.BlockSpec((2, 128, NODE_DEV), lambda i: (i, 0, 0))
    return pl.pallas_call(
        out_kernel,
        grid=(ZS // 2,),
        in_specs=[tile, SECOND, pl.BlockSpec((256, d), lambda i: (i, 0))],
        out_specs=whole((NODE_DEV, d)),
        out_shape=jax.ShapeDtypeStruct((NODE_DEV, d), bf16),
        scratch_shapes=[pltpu.VMEM((NODE_DEV, d), f32)],
        compiler_params=VMEM,
        name="project_out",
    )(od_a, joint, w_out)


def nodes_kernel(oa_ref, ob_ref, ka_ref, kb_ref, wq_ref, wk_ref, wv_ref, o_ref, total):
    step = pl.program_id(0)

    @pl.when(step == 0)
    def _():
        total[...] = jnp.zeros_like(total)

    dq, dk, dv = [], [], []
    for u in (0, 1):
        dq.append(pair_rows(oa_ref[u], ob_ref[u])[0])
        k, v = pair_rows(ka_ref[u], kb_ref[u])
        dk.append(k)
        dv.append(v)
    add = nt(turn(dq), wq_ref[...])
    add += nt(turn(dk), wk_ref[...])
    add += nt(turn(dv), wv_ref[...])
    total[...] += add

    @pl.when(step == pl.num_programs(0) - 1)
    def _():
        o_ref[...] = total[...].astype(bf16)


def node_grads(od_a, joint, kv_b, w_qkv):
    d = w_qkv.shape[0]
    tile = pl.BlockSpec((2, 128, NODE_DEV), lambda i: (i, 0, 0))
    steps = ZS // 2
    return pl.pallas_call(
        nodes_kernel,
        grid=(steps,),
        in_specs=[tile, SECOND, tile, tile]
        + [pl.BlockSpec((d, 256), functools.partial(lambda i, third: (0, third * steps + i), third=k)) for k in range(3)],
        out_specs=whole((NODE_DEV, d)),
        out_shape=jax.ShapeDtypeStruct((NODE_DEV, d), bf16),
        scratch_shapes=[pltpu.VMEM((NODE_DEV, d), f32)],
        compiler_params=VMEM,
        name="node_grads",
    )(od_a, joint, joint, kv_b, w_qkv, w_qkv, w_qkv)


def rows_kernel(x_ref, *refs):
    o_ref = refs[-1]
    total = jnp.sum(x_ref[...].astype(f32), axis=0)
    step = total.shape[0] // ZS
    for z in range(ZS):
        o_ref[z] = total[z * step : (z + 1) * step]


def sum_rows(parts, after):
    vmem = pl.BlockSpec(memory_space=pltpu.VMEM)
    return pl.pallas_call(
        rows_kernel,
        in_specs=[vmem] + [pl.BlockSpec(memory_space=pl.ANY)] * len(after),
        out_specs=vmem,
        out_shape=jax.ShapeDtypeStruct((ZS, parts.shape[1] // ZS, parts.shape[2]), f32),
        compiler_params=VMEM,
        name="sum_rows",
    )(parts, *after)


def spread_kernel(x_ref, *refs):
    o_ref = refs[-1]
    parts = x_ref[...].astype(f32).reshape(x_ref.shape[0] // ZS, ZS, *x_ref.shape[1:])
    total = jnp.sum(parts, axis=0)
    for z in range(ZS):
        for third in range(3):
            cols = third * H * HD + z * 128
            o_ref[:, cols : cols + 128] = total[z, :, third * 128 : (third + 1) * 128]


def spread(share, after):
    vmem = pl.BlockSpec(memory_space=pltpu.VMEM)
    return pl.pallas_call(
        spread_kernel,
        in_specs=[vmem] + [pl.BlockSpec(memory_space=pl.ANY)] * len(after),
        out_specs=vmem,
        out_shape=jax.ShapeDtypeStruct((share.shape[1], 3 * H * HD), f32),
        compiler_params=VMEM,
        name="spread",
    )(share, *after)


def swap(values, axis):
    return lax.all_to_all(values, axis, split_axis=0, concat_axis=0, tiled=True)


RIGHT = [(i, (i + 1) % YS) for i in range(YS)]
LEFT = [(i, (i - 1) % YS) for i in range(YS)]
OPPOSITE = [(i, (i + 2) % YS) for i in range(YS)]


def gather_row(own):
    return own, lax.ppermute(own, "y", RIGHT), lax.ppermute(own, "y", LEFT), lax.ppermute(own, "y", OPPOSITE)


def sum_kernel(count, *refs):
    parts = (r[...].astype(f32) for r in refs[:count])
    refs[-1][...] = sum(parts).astype(bf16)


def sum_parts(parts, after):
    shape = parts[0].shape
    tile = pl.BlockSpec((shape[0] // 2, *shape[1:]), lambda i: (i,) + (0,) * (len(shape) - 1))
    return pl.pallas_call(
        functools.partial(sum_kernel, len(parts)),
        grid=(2,),
        in_specs=[tile] * len(parts) + [pl.BlockSpec(memory_space=pl.ANY)] * len(after),
        out_specs=tile,
        out_shape=jax.ShapeDtypeStruct(shape, bf16),
        compiler_params=VMEM,
        name="sum_parts",
    )(*parts, *after)


def sum_join_kernel(a_ref, b_ref, c_ref, d_ref, od_ref, o_ref):
    o_ref[:, :128, :] = sum(r[...].astype(f32) for r in (a_ref, b_ref, c_ref, d_ref)).astype(bf16)
    o_ref[:, 128:, :] = od_ref[...]


def sum_join(parts, od):
    tile = pl.BlockSpec((ZS // 2, 128, NODE_DEV), lambda i: (i, 0, 0))
    return pl.pallas_call(
        sum_join_kernel,
        grid=(2,),
        in_specs=[tile] * 5,
        out_specs=pl.BlockSpec((ZS // 2, 256, NODE_DEV), lambda i: (i, 0, 0)),
        out_shape=jax.ShapeDtypeStruct((ZS, 256, NODE_DEV), bf16),
        compiler_params=VMEM,
        name="sum_join",
    )(*parts, od)


def send_row(own, to_right, to_left, opp):
    return [
        own,
        lax.ppermute(to_right, "y", RIGHT),
        lax.ppermute(to_left, "y", LEFT),
        lax.ppermute(opp, "y", OPPOSITE),
    ]


def gate_kernel(*refs):
    pass


def gate(values, after):
    anywhere = pl.BlockSpec(memory_space=pl.ANY)
    return pl.pallas_call(
        gate_kernel,
        in_specs=[anywhere] * (len(values) + len(after)),
        out_specs=[anywhere] * len(values),
        out_shape=[jax.ShapeDtypeStruct(v.shape, v.dtype) for v in values],
        input_output_aliases={i: i for i in range(len(values))},
        compiler_params=VMEM,
        name="gate",
    )(*values, *after)


def weight_kernel(c_ref, oa_ref, ob_ref, ka_ref, kb_ref, f_ref, mine_ref, theirs_ref, grads):
    @pl.when(pl.program_id(0) == 0)
    def _():
        for t in range(ZS):
            nodes = slice(t * NODE_DEV, (t + 1) * NODE_DEV)
            dq = pair_rows(oa_ref[t], ob_ref[t])[0]
            dk, dv = pair_rows(ka_ref[t, :128, :], kb_ref[t])
            for k, part in enumerate((dq, dk, dv)):
                grads[k * 128 : (k + 1) * 128, nodes] = part

    both = nn(grads[...], f_ref[...]).T.astype(bf16)
    first = c_ref[0] == 0
    mine_ref[...] = jnp.where(first, both[:128], both[128:])
    theirs_ref[...] = jnp.where(first, both[128:], both[:128])


def weight_share(c, od_a, od_b, joint, kv_b, feats_row):
    d = feats_row.shape[1]
    part = whole(TURNED)
    return pl.pallas_call(
        weight_kernel,
        grid=(d // 256,),
        in_specs=[pl.BlockSpec(memory_space=pltpu.SMEM), part, part, whole(joint.shape), part, pl.BlockSpec((ROW, 256), lambda i: (0, i))],
        out_specs=[pl.BlockSpec((128, 384), lambda i: (i, 0))] * 2,
        out_shape=[jax.ShapeDtypeStruct((d // 2, 384), bf16)] * 2,
        scratch_shapes=[pltpu.VMEM((384, ROW), bf16)],
        compiler_params=VMEM,
        name="weight_share",
    )(c, od_a, od_b, joint, kv_b, feats_row)


def on_device(node_feats, w_qkv, w_out, cotangent, block_neighbors, block_counts, global_blocks):
    feats = node_feats[0]
    cot = cotangent[0]
    y = lax.axis_index("y")
    neighbors = lax.dynamic_slice_in_dim(block_neighbors[0], y * QBLK, QBLK, 0)
    counts = lax.dynamic_slice_in_dim(block_counts[0], y * QBLK, QBLK, 0)
    table = jnp.concatenate([jnp.broadcast_to(global_blocks[0][None], (QBLK, NGLOB)), neighbors], axis=1).reshape(-1)
    place = jnp.arange(QBLK, dtype=jnp.int32)
    key = counts * QBLK + place
    rank = jnp.sum((key[None, :] < key[:, None]).astype(jnp.int32), axis=1)
    order = jnp.sum(jnp.where(rank[None, :] == place[:, None], place[None, :], 0), axis=1)
    y_arr = y.reshape(1).astype(jnp.int32)

    kv_a, kv_b = project_kv(feats, w_qkv)
    joint, qg_b, feats_copy = project_qg(feats, cot, w_qkv, w_out, kv_b, (table, counts, order))
    row_a = gather_row(swap(kv_a, "z"))
    joint_row = swap(joint, "z")
    row_b = gather_row(first_half(joint_row))
    (feats_late, qg_b) = gate([feats_copy, qg_b], [joint_row])
    qg_row_b = swap(qg_b, "z")
    feats_row = lax.all_gather(feats_late, "z", axis=0, tiled=True)
    od_a, *kv_a = attend(table, counts, order, y_arr, row_a, joint_row, feats_late)
    to_nodes = lambda v: swap(v, "z")
    (od_a_late,) = gate([od_a], [qg_row_b])
    od_nodes_a = to_nodes(od_a_late)
    parts_a = send_row(*kv_a)
    late = attend(table, counts, order, y_arr, row_b, qg_row_b, od_a_late)
    od_b, *kv_b = gate(late, parts_a[1:])
    parts_b = send_row(*kv_b)
    (joint,) = gate([sum_join(parts_a, od_b)], [od_nodes_a])
    joint_nodes = swap(joint, "z")
    sum_b = sum_parts(parts_b, (joint_nodes,))
    kv_nodes_b = to_nodes(sum_b)
    attn_update = project_out(od_nodes_a, joint_nodes, w_out)
    grad_nodes = node_grads(od_nodes_a, joint_nodes, kv_nodes_b, w_qkv)

    d = feats.shape[1]
    c_arr = lax.axis_index("c").reshape(1).astype(jnp.int32)
    mine, theirs = weight_share(c_arr, od_a_late, od_b, joint, sum_b, feats_row)
    theirs = lax.ppermute(theirs, "c", [(0, 1), (1, 0)])
    share = sum_parts([mine, theirs], ()).reshape(16, d // 32, 384)
    (share,) = gate([share], [kv_nodes_b])
    share = sum_rows(swap(share, ("x", "y")), (grad_nodes,))
    grad_weights = spread(swap(share, "z"), (attn_update,))
    return attn_update[None], grad_nodes[None], grad_weights


def solution(mesh):
    fine = Mesh(np.asarray(mesh.devices).reshape(4, 2, YS, ZS), ("x", "c", "y", "z"))
    dp, seq = ("x", "c"), ("y", "z")
    in_specs = (P(dp, seq, None), P(), P(), P(dp, seq, None), P(dp, None, None), P(dp, None), P(dp, None))
    out_specs = (P(dp, seq, None), P(dp, seq, None), P(dp + seq, None))
    return jax.shard_map(on_device, mesh=fine, in_specs=in_specs, out_specs=out_specs, check_vma=False)
```
